256 devices in a mesh: section: 4 (over y), tile: 16 (over z_hi, x, core), col: 4 (over z_lo).
Axes of the slice: x: 4, y: 4, z: 8 (z_hi: 2, z_lo: 4; z = z_hi * 4 + z_lo), core: 2. Of those that a mesh axis runs over, the one named last changes fastest.
Arguments:
- initial_states: float32 [8, 128, 32, 512], P(None, None, 'tile', 'col'), may hold values from -6 to 6
- targets: bfloat16 [4, 8, 128, 32, 512], P('section', None, None, 'tile', 'col'), may hold values from -6 to 6
- w_in: bfloat16 [4096, 128], replicated, may hold values from -0.5 to 0.5
- w_out: bfloat16 [128, 4096], replicated, may hold values from -0.09375 to 0.09375
- diffusivity: float32 [128], replicated, may hold values from 0.03 to 0.22
- stiffness: float32 [128], replicated, may hold values from 0.5 to 4000
- land_mask: int32 [32, 512], P('tile', 'col'), may hold values 0 or 1
- wet_levels: int32 [32, 512], P('tile', 'col'), may hold values from 1 to 16
- plan: int32 [8], replicated, may hold values from 0 to 7, each once
Outputs:
- trajectory: float32 [4, 8, 128, 32, 512], P('section', None, None, 'tile', 'col')
- grad_w_in: float32 [4096, 128], replicated
- grad_w_out: float32 [128, 4096], replicated
The draws below stay inside these ranges and needn't reach their ends.
Inputs may be any that keep to these rules, and one draw needn't show every extreme that they name: `plan`: each of the 8 samples appears once.
All inputs are finite; a program needn't handle non-finite values. No bound on the sum of `land_mask` on one device may be relied on, other than what follows from the above.
Results may differ from the reference program's by a relative error of at most 0.0026.
Values may be sent and summed in bfloat16 or wider, within the bound.
No kernel may reach another device: no remote copies, remote signals or barrier semaphores. Data moves between devices by JAX's collectives and lax.ppermute only.
A program may use at most 64 MiB of HBM per device.

```python
import math
import jax
import jax.numpy as jnp
from jax import lax

V = 8
L = 16
H = 4096
F = 128
SECTIONS = 4
MB = 8
NX = 32
NY = 512


def with_ends(drawn, key, smallest, largest):
    index_at = [jax.random.randint(jax.random.fold_in(key, axis), (), 0, length) for axis, length in enumerate(drawn.shape)]
    longest = drawn.shape.index(max(drawn.shape))
    next_to = index_at[:longest] + [(index_at[longest] + 1) % drawn.shape[longest]] + index_at[longest + 1:]
    return drawn.at[tuple(index_at)].set(smallest).at[tuple(next_to)].set(largest)


def level_of(rng, dims, shards, smallest, largest):
    def one(dim, parts):
        steps = jax.random.uniform(jax.random.fold_in(jax.random.fold_in(rng, 6), dim), (parts,), jnp.float32, smallest / len(shards), largest / len(shards))
        return jnp.repeat(jnp.exp(steps), dims[dim] // parts).reshape((-1,) + (1,) * (len(dims) - dim - 1))

    gain = one(*shards[0])
    for cut in shards[1:]:
        gain = gain * one(*cut)
    return gain


def noise(own_key, shape, width, bound, cuts=(), kind=jnp.bfloat16):
    values = width * jax.random.normal(own_key, shape, jnp.float32)
    if cuts:
        values = values * level_of(own_key, shape, cuts, -0.22, 0.18)
    return jnp.clip(values, -bound, bound).astype(kind)


def setup_inputs(seed: int = 0) -> dict:
    arg_keys = jax.random.split(jax.random.key(seed), 10)
    return {
        "initial_states": noise(arg_keys[0], (MB, F, NX, NY), 1.0, 6.0, ((2, 16), (3, 4)), jnp.float32),
        "targets": noise(arg_keys[1], (SECTIONS, MB, F, NX, NY), 1.0, 6.0, ((0, 4), (3, 16), (4, 4))),
        "w_in": noise(arg_keys[2], (H, F), F ** -0.5, 0.5),
        "w_out": noise(arg_keys[3], (F, H), H ** -0.5, 0.09375),
        "diffusivity": jnp.clip(jax.random.uniform(arg_keys[4], (F,), jnp.float32, 0.03, 0.22), 0.03, 0.22),
        "stiffness": jnp.clip(jnp.exp(jax.random.uniform(arg_keys[5], (F,), jnp.float32, math.log(0.5), math.log(4000.0))), 0.5, 4000.0),
        "land_mask": with_ends((jax.random.randint(arg_keys[6], (NX, NY), 0, 5) < 4).astype(jnp.int32), jax.random.fold_in(arg_keys[6], 1), 0, 1),
        "wet_levels": with_ends(jax.random.randint(arg_keys[7], (NX, NY), 1, L + 1), jax.random.fold_in(arg_keys[7], 1), 1, L).astype(jnp.int32),
        "plan": jax.random.permutation(arg_keys[8], MB).astype(jnp.int32),
    }


def mode_table(level_count):
    order_index = jnp.arange(level_count).astype(jnp.float32)
    angles = jnp.pi * (order_index[None, :] + 0.5) * order_index[:, None] / level_count
    weights = jnp.where(order_index[:, None] == 0.0, math.sqrt(1.0 / level_count), math.sqrt(2.0 / level_count))
    return jnp.cos(angles) * weights

def implicit_solve(right_side, coupling):
    cell_count = right_side.shape[1]
    ones_grid = jnp.ones((right_side.shape[0], cell_count), right_side.dtype)
    off_diag = -coupling[:, None] * ones_grid
    lower_diag = off_diag.at[:, 0].set(0.0)
    upper_diag = off_diag.at[:, cell_count - 1].set(0.0)
    middle = (1.0 + 2.0 * coupling[:, None]) * ones_grid
    return lax.linalg.tridiagonal_solve(lower_diag, middle, upper_diag, right_side)

def contract_rows(left_operand, right_operand):
    return lax.dot_general(left_operand.astype(jnp.float32), right_operand.astype(jnp.float32), (((1,), (1,)), ((), ())), preferred_element_type=jnp.float32)

def contract_lead(left_operand, right_operand):
    return lax.dot_general(left_operand.astype(jnp.float32), right_operand.astype(jnp.float32), (((0,), (0,)), ((), ())), preferred_element_type=jnp.float32)

def reference(initial_states, targets, w_in, w_out, diffusivity, stiffness, land_mask, wet_levels, plan):
    mode_matrix = mode_table(L)
    level_index = jnp.arange(L).astype(jnp.int32)
    wet_cells = ((land_mask[None] == 1) & (level_index[:, None, None] < wet_levels[None])).astype(jnp.float32)
    wet_rows = jnp.tile(wet_cells, (V, 1, 1)).reshape(F, NX * NY)
    grad_scale = 1.0 / math.sqrt(MB * SECTIONS * NX * NY)

    def advance(running, sample):
        grad_in, grad_out = running
        column_state = initial_states[sample]
        outputs = []
        for section_index in range(SECTIONS):
            padded = jnp.pad(column_state, ((0, 0), (1, 1), (1, 1)))
            laplace = padded[:, 2:, 1:-1] + padded[:, :-2, 1:-1] + padded[:, 1:-1, 2:] + padded[:, 1:-1, :-2] - 4.0 * column_state
            smoothed = (column_state + diffusivity[:, None, None] * laplace).reshape(V, L, NX, NY) * wet_cells[None]
            modal_fields = jnp.einsum('ml,vlxy->vmxy', mode_matrix, smoothed, precision=lax.Precision.HIGHEST)
            relaxed = implicit_solve(modal_fields.reshape(F, NX, NY), stiffness).reshape(V, L, NX, NY)
            levels_back = jnp.einsum('ml,vmxy->vlxy', mode_matrix, relaxed, precision=lax.Precision.HIGHEST)
            after_dynamics = (levels_back * wet_cells[None]).reshape(F, NX * NY)
            inputs = after_dynamics.astype(jnp.bfloat16)
            hidden = jnp.tanh(jnp.dot(w_in.astype(jnp.float32), inputs.astype(jnp.float32), preferred_element_type=jnp.float32))
            hidden_bf = hidden.astype(jnp.bfloat16)
            tendency = jnp.dot(w_out.astype(jnp.float32), hidden_bf.astype(jnp.float32), preferred_element_type=jnp.float32)
            result = wet_rows * (after_dynamics + tendency)
            target = targets[section_index, sample].reshape(F, NX * NY).astype(jnp.float32)
            misfit = (wet_rows * (tendency - target) * grad_scale).astype(jnp.bfloat16)
            grad_out = grad_out + contract_rows(misfit, hidden_bf)
            back_hidden = (contract_lead(w_out, misfit) * (1.0 - hidden * hidden)).astype(jnp.bfloat16)
            grad_in = grad_in + contract_rows(back_hidden, inputs)
            column_state = result.reshape(F, NX, NY)
            outputs.append(column_state)
        return ((grad_in, grad_out), jnp.stack(outputs))
    start = (jnp.zeros((H, F), jnp.float32), jnp.zeros((F, H), jnp.float32))
    (grad_in, grad_out), stacked = lax.scan(advance, start, plan)
    trajectory = jnp.transpose(stacked, (1, 0, 2, 3, 4))
    return (trajectory, grad_in, grad_out)
```

```python
import math

import jax
import jax.numpy as jnp
import numpy as np
from jax import lax
from jax.experimental import pallas as pl
from jax.experimental.pallas import tpu as pltpu
from jax.sharding import Mesh, PartitionSpec as P

V = 8
L = 16
H = 4096
F = 128
STEPS = 4
MB = 8
NX = 32
NY = 512
CHUNK = 16
HALO = STEPS
SLAB = CHUNK + 2 * HALO
MSG = 48
CODE = 32000.0
UNIT = 32768.0 / CODE
OWN = NX * CHUNK
COLS = STEPS * OWN
HB1 = 512
HB2 = 256
HALF = H // 2
GRAD_SCALE = 1.0 / math.sqrt(MB * STEPS * NX * NY)
TILE = ("zh", "cx", "core")
COL = ("c1", "c0")
SPREAD = ("sec", "cx", "c0")
PARTS = 32
ROWS = H // 2 // PARTS


def mode_block():
    order = np.arange(L)
    angles = np.pi * (order[None, :] + 0.5) * order[:, None] / L
    weights = np.where(order[:, None] == 0, math.sqrt(1.0 / L), math.sqrt(2.0 / L))
    return np.kron(np.eye(V), np.cos(angles) * weights).astype(np.float32)


def params(semantics=None, mib=60):
    return pltpu.CompilerParams(dimension_semantics=semantics, vmem_limit_bytes=mib * 2**20)


def exponent(largest):
    return jnp.ceil(jnp.log(jnp.maximum(largest, 1e-30)) * (1.0 / math.log(2.0)) + 0.01)


def encode(value, power):
    scaled = value * (jnp.exp2(15.0 - power) * (1.0 / UNIT))
    return jnp.round(jnp.clip(scaled, -32767.0, 32767.0))


def to_int16(value):
    return value.astype(jnp.int32).astype(jnp.int16)


def to_float(code):
    return code.astype(jnp.int32).astype(jnp.float32)


def decode(value, power):
    return value * (jnp.exp2(power - 15.0) * UNIT)


def init_kernel(meta_ref, plan_ref, state_ref, land_ref, levels_ref, msg_ref):
    power = exponent(jnp.max(jnp.abs(state_ref[0]), keepdims=True))
    code = [encode(state_ref[0, pl.ds(x, F, stride=2), :], power).T for x in range(2)]
    depth = jnp.where(land_ref[...] == 1, levels_ref[...], 0).astype(jnp.float32)
    extra = jnp.concatenate(
        [depth, jnp.broadcast_to(power, (1, 128)), jnp.zeros((5, 128), jnp.float32)], axis=0
    )
    for j in range(8):
        y = CHUNK * j
        first = [c[y : y + HALO] for c in code]
        middle = [c[y + HALO : y + CHUNK - HALO] for c in code]
        last = [c[y + CHUNK - HALO : y + CHUNK] for c in code]
        msg_ref[j] = to_int16(jnp.concatenate(first + [extra] + middle + last + [extra], axis=0))


def init_slabs(meta, plan, states, land_mask, wet_levels):
    whole = lambda i, meta, plan: (0, 0)
    return pl.pallas_call(
        init_kernel,
        grid_spec=pltpu.PrefetchScalarGridSpec(
            num_scalar_prefetch=2,
            grid=(2,),
            in_specs=[
                pl.BlockSpec((1, 2 * F, 128), lambda i, meta, plan: (plan[2 * meta[0] + i], 0, 0)),
                pl.BlockSpec((2, 128), whole),
                pl.BlockSpec((2, 128), whole),
            ],
            out_specs=pl.BlockSpec((8, MSG, F), lambda i, meta, plan: (i, 0, 0)),
        ),
        out_shape=jax.ShapeDtypeStruct((16, MSG, F), jnp.int16),
        compiler_params=params(("arbitrary",)),
        name="init_slabs",
    )(meta, plan, states, land_mask, wet_levels)


def levels():
    return (lax.broadcasted_iota(jnp.int32, (1, F), 1) % L).astype(jnp.float32)


def rollout_kernel(
    meta_ref, msg_ref, left_ref, right_ref, w_in_t, w_out_t, mode_ref, mode_t, diff_ref, stiff_ref,
    traj_ref, inputs_ref, tend_ref, own_wet_ref,
    state, wet, modal, acc, x_scr, gain, pull, depth, depth_t,
):
    for t in range(16):
        for n, (ref, base) in enumerate(
            ((msg_ref, 0), (msg_ref, 16), (msg_ref, 32), (right_ref, 0), (left_ref, 0))
        ):
            piece = to_float(ref[t, base : base + 16])
            if n != 1:
                scale = decode(1.0, piece[10:11])
            rows = 8 if n == 1 else HALO
            at = (0, HALO, CHUNK - HALO, CHUNK, CHUNK + HALO)[n]
            for x in range(2):
                state[2 * t + x, at : at + rows] = piece[x * rows : (x + 1) * rows] * scale
            if n in (0, 3, 4):
                depth[n // 2 if n else 0, 2 * t : 2 * t + 2] = piece[8:10]
    for n in range(3):
        depth_t[n] = depth[n].T
    mine = meta_ref[1]
    y_own = pl.multiple_of(mine * CHUNK, CHUNK)
    y_right = pl.multiple_of(lax.rem(mine + 1, 8) * CHUNK, CHUNK)
    y_left = pl.multiple_of(lax.rem(mine + 7, 8) * CHUNK + 8, 8)
    here = jnp.concatenate(
        [
            depth_t[0, pl.ds(y_own, CHUNK)],
            depth_t[1, pl.ds(y_right, 8)][:HALO],
            depth_t[2, pl.ds(y_left, 8)][8 - HALO :],
        ],
        axis=0,
    )
    level = levels()
    for x in range(NX):
        wet[x] = jnp.where(level < here[:, x : x + 1], 1.0, 0.0)
    own_wet_ref[...] = wet[:, :CHUNK]

    a = stiff_ref[...]
    u = 1.0 + a
    for i in range(NX):
        r = 1.0 / (a + u)
        gain[pl.ds(i, 1), :] = r
        pull[pl.ds(i, 1), :] = a * r
        u = 1.0 + a * (u * r)
    diff = diff_ref[...].reshape(1, 1, F)
    edge = jnp.zeros((1, SLAB, F), jnp.float32)
    for step in range(STEPS):
        now = state[...]
        around = (
            jnp.concatenate([edge, now[:-1]], axis=0)
            + jnp.concatenate([now[1:], edge], axis=0)
            + pltpu.roll(now, 1, 1)
            + pltpu.roll(now, SLAB - 1, 1)
            - 4.0 * now
        )
        smoothed = wet[...] * (now + diff * around)
        modal[...] = jnp.dot(
            smoothed.reshape(NX * SLAB, F),
            mode_t[...],
            precision=lax.Precision.HIGHEST,
            preferred_element_type=jnp.float32,
        ).reshape(NX, SLAB, F)
        part = modal[0] * gain[pl.ds(0, 1), :]
        modal[0] = part
        for i in range(1, NX):
            part = modal[i] * gain[pl.ds(i, 1), :] + pull[pl.ds(i, 1), :] * part
            modal[i] = part
        for i in range(NX - 2, -1, -1):
            part = modal[i] + pull[pl.ds(i, 1), :] * part
            modal[i] = part
        after = wet[...] * jnp.dot(
            modal[...].reshape(NX * SLAB, F),
            mode_ref[...],
            precision=lax.Precision.HIGHEST,
            preferred_element_type=jnp.float32,
        ).reshape(NX, SLAB, F)
        rows = SLAB if step < STEPS - 1 else CHUNK
        after = after[:, :rows]
        state[:, :rows] = after
        x_scr[0 : NX * rows] = after.reshape(NX * rows, F).astype(jnp.bfloat16)
        inputs_ref[step] = after[:, :CHUNK].astype(jnp.bfloat16)
        acc[0 : NX * rows] = jnp.zeros((NX * rows, F), jnp.float32)

        def block(b, carry, rows=rows):
            at = pl.multiple_of(b * HB1, HB1)
            hidden = jnp.tanh(
                jnp.dot(
                    x_scr[0 : NX * rows],
                    w_in_t[:, pl.ds(at, HB1)],
                    preferred_element_type=jnp.float32,
                )
            ).astype(jnp.bfloat16)
            acc[0 : NX * rows] += jnp.dot(
                hidden, w_out_t[pl.ds(at, HB1), :], preferred_element_type=jnp.float32
            )
            return carry

        lax.fori_loop(0, H // HB1, block, 0, unroll=2)
        tendency = acc[0 : NX * rows].reshape(NX, rows, F)
        result = wet[:, :rows] * (state[:, :rows] + tendency)
        state[:, :rows] = result
        traj_ref[step] = result[:, :CHUNK].astype(jnp.bfloat16)
        tend_ref[step] = tendency[:, :CHUNK]


def rollout(meta, msg, left, right, w_in_t, w_out_t, diffusivity, stiffness):
    block = mode_block()
    vmem = pl.BlockSpec(memory_space=pltpu.VMEM)
    return pl.pallas_call(
        rollout_kernel,
        out_shape=[
            jax.ShapeDtypeStruct((STEPS, NX, CHUNK, F), jnp.bfloat16),
            jax.ShapeDtypeStruct((STEPS, NX, CHUNK, F), jnp.bfloat16),
            jax.ShapeDtypeStruct((STEPS, NX, CHUNK, F), jnp.float32),
            jax.ShapeDtypeStruct((NX, CHUNK, F), jnp.float32),
        ],
        in_specs=[pl.BlockSpec(memory_space=pltpu.SMEM)] + [vmem] * 9,
        out_specs=[vmem] * 4,
        scratch_shapes=[
            pltpu.VMEM((NX, SLAB, F), jnp.float32),
            pltpu.VMEM((NX, SLAB, F), jnp.float32),
            pltpu.VMEM((NX, SLAB, F), jnp.float32),
            pltpu.VMEM((NX * SLAB, F), jnp.float32),
            pltpu.VMEM((NX * SLAB, F), jnp.bfloat16),
            pltpu.VMEM((NX, F), jnp.float32),
            pltpu.VMEM((NX, F), jnp.float32),
            pltpu.VMEM((3, NX, 128), jnp.float32),
            pltpu.VMEM((3, 128, NX), jnp.float32),
        ],
        compiler_params=params(),
        cost_estimate=pl.CostEstimate(
            flops=4 * 2816 * F * H, bytes_accessed=6 * 2**20, transcendentals=2816 * H
        ),
        name="rollout",
    )(
        meta,
        msg,
        left,
        right,
        w_in_t,
        w_out_t,
        jnp.asarray(block),
        jnp.asarray(np.ascontiguousarray(block.T)),
        diffusivity.reshape(1, F),
        stiffness.reshape(1, F),
    )


def prepare_kernel(plan_ref, target_ref, w_in_ref, w_out_ref, out_ref, w_in_t, w_out_t, wide):
    wide[...] = target_ref[0].astype(jnp.float32)
    for x in range(2):
        t = wide[pl.ds(x, F, stride=2), :].T
        out_ref[0, :, x] = t.reshape(8, CHUNK, F).astype(jnp.bfloat16)
    w_in_t[...] = w_in_ref[...].T
    w_out_t[...] = w_out_ref[...].T


def prepare(targets, w_in, w_out, plan):
    part = H // MB
    down = lambda i, plan: (i, 0)
    along = lambda i, plan: (0, i)
    return pl.pallas_call(
        prepare_kernel,
        grid_spec=pltpu.PrefetchScalarGridSpec(
            num_scalar_prefetch=1,
            grid=(MB,),
            in_specs=[
                pl.BlockSpec((1, 2 * F, 128), lambda i, plan: (plan[i], 0, 0)),
                pl.BlockSpec((part, F), down),
                pl.BlockSpec((F, part), along),
            ],
            out_specs=[
                pl.BlockSpec((1, 8, 2, CHUNK, F), lambda i, plan: (i, 0, 0, 0, 0)),
                pl.BlockSpec((F, part), along),
                pl.BlockSpec((part, F), down),
            ],
            scratch_shapes=[pltpu.VMEM((2 * F, 128), jnp.float32)],
        ),
        out_shape=[
            jax.ShapeDtypeStruct((MB, 8, 2, CHUNK, F), jnp.bfloat16),
            jax.ShapeDtypeStruct((F, H), jnp.bfloat16),
            jax.ShapeDtypeStruct((H, F), jnp.bfloat16),
        ],
        compiler_params=params(),
        cost_estimate=pl.CostEstimate(flops=0, bytes_accessed=6 * 2**20, transcendentals=0),
        name="prepare",
    )(plan, targets, w_in, w_out)


def spread_kernel(in_ref, out_ref):
    for x in range(2):
        block = in_ref[0, :, x].astype(jnp.float32).reshape(128, F)
        out_ref[0, pl.ds(x, F, stride=2), :] = block.T


def spread_trajectory(arrived):
    return pl.pallas_call(
        spread_kernel,
        grid=(MB,),
        in_specs=[pl.BlockSpec((1, 8, 2, CHUNK, F), lambda i: (i, 0, 0, 0, 0))],
        out_specs=pl.BlockSpec((1, 2 * F, 128), lambda i: (i, 0, 0)),
        out_shape=jax.ShapeDtypeStruct((MB, 2 * F, 128), jnp.float32),
        compiler_params=params(),
        name="spread_trajectory",
    )(arrived)


def grad_block(x_ref, x_t, misfit, misfit_t, w_in_ref, w_out_ref):
    width = w_in_ref.shape[1]
    grad_in = jnp.zeros((F, width), jnp.float32)
    grad_out = jnp.zeros((F, width), jnp.float32)
    for part in range(STEPS):
        at = slice(part * OWN, (part + 1) * OWN)
        hidden = jnp.tanh(jnp.dot(x_ref[at], w_in_ref[...], preferred_element_type=jnp.float32))
        grad_out += jnp.dot(
            misfit_t[:, at], hidden.astype(jnp.bfloat16), preferred_element_type=jnp.float32
        )
        back = jnp.dot(misfit[at], w_out_ref[...], preferred_element_type=jnp.float32)
        back = (back * (1.0 - hidden * hidden)).astype(jnp.bfloat16)
        grad_in += jnp.dot(x_t[:, at], back, preferred_element_type=jnp.float32)
    shape = (width // ROWS, ROWS, F)
    return grad_in.T.reshape(shape), grad_out.T.reshape(shape)


def first_kernel(
    half_ref, x_ref, tend_ref, target_ref, wet_ref, w_in_ref, w_out_ref, out_ref, x_t, misfit, misfit_t
):
    @pl.when(pl.program_id(0) == 0)
    def _():
        for step in range(STEPS):
            at = slice(step * OWN, (step + 1) * OWN)
            gap = wet_ref[...] * (tend_ref[at] - target_ref[at].astype(jnp.float32))
            gap = (gap * GRAD_SCALE).astype(jnp.bfloat16)
            misfit[at] = gap
            misfit_t[:, at] = gap.T
            x_t[:, at] = x_ref[at].T

    grad_in, grad_out = grad_block(x_ref, x_t, misfit, misfit_t, w_in_ref, w_out_ref)
    out_ref[:, 0] = grad_in
    out_ref[:, 1] = grad_out


def second_kernel(half_ref, x_ref, x_t, misfit, misfit_t, w_in_ref, w_out_ref, add_ref, out_ref):
    grad_in, grad_out = grad_block(x_ref, x_t, misfit, misfit_t, w_in_ref, w_out_ref)
    out_ref[:, 0] = (grad_in + add_ref[:, 0]).astype(jnp.bfloat16)
    out_ref[:, 1] = (grad_out + add_ref[:, 1]).astype(jnp.bfloat16)


def half_grads(half, columns, w_in_t, w_out, add=None):
    first = add is None
    width = 512 if first else 256
    blocks = HALF // width
    whole = lambda i, half: (0, 0)
    weight = lambda i, half: (0, half[0] * blocks + i)
    rows = pl.BlockSpec((width // ROWS, 2, ROWS, F), lambda i, half: (i, 0, 0, 0))
    in_specs = [pl.BlockSpec(c.shape, whole) for c in columns] + [pl.BlockSpec((F, width), weight)] * 2
    out_specs = [rows]
    out_shape = [jax.ShapeDtypeStruct((PARTS, 2, ROWS, F), jnp.float32 if first else jnp.bfloat16)]
    if first:
        for shape in ((F, COLS), (COLS, F), (F, COLS)):
            out_specs.append(pl.BlockSpec(shape, whole))
            out_shape.append(jax.ShapeDtypeStruct(shape, jnp.bfloat16))
    return pl.pallas_call(
        first_kernel if first else second_kernel,
        grid_spec=pltpu.PrefetchScalarGridSpec(
            num_scalar_prefetch=1,
            grid=(blocks,),
            in_specs=in_specs if first else in_specs + [rows],
            out_specs=out_specs,
        ),
        out_shape=out_shape,
        compiler_params=params(("arbitrary",)),
        cost_estimate=pl.CostEstimate(
            flops=8 * COLS * F * HALF, bytes_accessed=5 * 2**20, transcendentals=COLS * HALF
        ),
        name="first_grads" if first else "second_grads",
    )(half, *columns, w_in_t, w_out, *(() if first else (add,)))


def plane_kernel(in_ref, out_ref):
    total = in_ref[0].astype(jnp.float32)
    for n in range(1, PARTS):
        total += in_ref[n].astype(jnp.float32)
    total = total.astype(jnp.bfloat16)
    for n in range(4):
        out_ref[n] = total


def plane_copies(parts):
    vmem = pl.BlockSpec(memory_space=pltpu.VMEM)
    return pl.pallas_call(
        plane_kernel,
        out_shape=jax.ShapeDtypeStruct((4, 2, ROWS, F), jnp.bfloat16),
        in_specs=[vmem],
        out_specs=vmem,
        compiler_params=params(mib=32),
        name="plane_copies",
    )(parts)


def column_kernel(in_ref, out_ref):
    powers = []
    for g in range(2):
        total = in_ref[0, g].astype(jnp.float32)
        for n in range(1, 4):
            total += in_ref[n, g].astype(jnp.float32)
        power = exponent(jnp.max(jnp.abs(total), axis=0, keepdims=True))
        powers.append(power)
        code = to_int16(encode(total, power))
        for n in range(PARTS):
            out_ref[n, g * ROWS : (g + 1) * ROWS] = code
    tail = to_int16(jnp.concatenate(powers + [jnp.zeros((14, F), jnp.float32)], axis=0))
    for n in range(PARTS):
        out_ref[n, 2 * ROWS : 2 * ROWS + 16] = tail


def column_copies(planes):
    vmem = pl.BlockSpec(memory_space=pltpu.VMEM)
    return pl.pallas_call(
        column_kernel,
        out_shape=jax.ShapeDtypeStruct((PARTS, 2 * ROWS + 16, F), jnp.int16),
        in_specs=[vmem],
        out_specs=vmem,
        compiler_params=params(mib=32),
        name="column_copies",
    )(planes)


def finish_kernel(half_ref, code_ref, *refs):
    grad_in_ref, grad_out_ref = refs[-2:]
    for n in range(0, code_ref.shape[0], 2):
        at = slice(n * ROWS, (n + 2) * ROWS)
        both = []
        for m in (n, n + 1):
            code = to_float(code_ref[m])
            grad_in_ref[m * ROWS : (m + 1) * ROWS] = decode(
                code[0:ROWS], code[2 * ROWS : 2 * ROWS + 1]
            )
            both.append(decode(code[ROWS : 2 * ROWS], code[2 * ROWS + 1 : 2 * ROWS + 2]))
        grad_out_ref[:, at] = jnp.concatenate(both, axis=0).T


def finish_half(half, code, before=()):
    return pl.pallas_call(
        finish_kernel,
        grid_spec=pltpu.PrefetchScalarGridSpec(
            num_scalar_prefetch=1,
            grid=(2,),
            in_specs=[pl.BlockSpec((PARTS // 2, 2 * ROWS + 16, F), lambda i, half: (i, 0, 0))]
            + [pl.BlockSpec(memory_space=pl.ANY)] * len(before),
            out_specs=[
                pl.BlockSpec((1024, F), lambda i, half: (half[0] * 2 + i, 0)),
                pl.BlockSpec((F, 1024), lambda i, half: (0, half[0] * 2 + i)),
            ],
        ),
        out_shape=[
            jax.ShapeDtypeStruct((H, F), jnp.float32),
            jax.ShapeDtypeStruct((F, H), jnp.float32),
        ],
        input_output_aliases={2: 0, 3: 1} if before else {},
        compiler_params=params(("arbitrary",), 32),
        name="finish_half",
    )(half, code, *before)


def swap(value, axes):
    return lax.all_to_all(value, axes, split_axis=0, concat_axis=0, tiled=True)


def local(initial_states, targets, w_in, w_out, diffusivity, stiffness, land_mask, wet_levels, plan):
    core = lax.axis_index("core").astype(jnp.int32).reshape(1)
    meta = jnp.stack([lax.axis_index("sec"), lax.axis_index(TILE) % 8]).astype(jnp.int32)

    states = initial_states.reshape(MB, 2 * F, 128)
    msg = swap(init_slabs(meta, plan, states, land_mask, wet_levels), TILE)
    place = lambda half, chunk, col: (half * 8 + chunk) * 4 + col
    forward = [
        (place(h, j, c), place(h, (j + 1) % 8, c + (j + 1) // 8))
        for h in range(2)
        for j in range(8)
        for c in range(4)
        if c + (j + 1) // 8 < 4
    ]
    left = lax.ppermute(msg[:, 32:48], TILE + COL, forward)
    right = lax.ppermute(msg[:, 0:16], TILE + COL, [(b, a) for a, b in forward])

    target, w_in_t, w_out_t = prepare(targets.reshape(MB, 2 * F, 128), w_in, w_out, plan)
    target = swap(target.reshape(64, 2, CHUNK, F), ("sec",) + TILE).reshape(COLS, F)

    traj, inputs, tend, wet = rollout(meta, msg, left, right, w_in_t, w_out_t, diffusivity, stiffness)
    arrived = swap(traj.reshape(64, 2, CHUNK, F), ("sec",) + TILE)

    inputs = inputs.reshape(COLS, F)
    columns = (inputs, tend.reshape(COLS, F), target, wet.reshape(OWN, F))
    other, *columns = half_grads(1 - core, columns, w_in_t, w_out)
    swapped = lax.ppermute(other, "core", [(0, 1), (1, 0)])
    (pair,) = half_grads(core, (inputs, *columns), w_in_t, w_out, swapped)
    pair, arrived = lax.optimization_barrier((pair, arrived))

    planes = swap(plane_copies(swap(pair, SPREAD)), ("zh", "c1"))
    code = swap(column_copies(planes), SPREAD)
    across = lax.ppermute(code, "core", [(0, 1), (1, 0)])
    grad_in, grad_out = finish_half(1 - core, across, finish_half(core, code))
    trajectory = spread_trajectory(arrived.reshape(MB, 8, 2, CHUNK, F))
    return (trajectory.reshape(1, MB, F, 2, 128), grad_in, grad_out)


def solution(mesh):
    fine = Mesh(mesh.devices.reshape(4, 2, 4, 2, 2, 2), ("sec", "zh", "cx", "core", "c1", "c0"))
    in_specs = (
        P(None, None, TILE, COL),
        P("sec", None, None, TILE, COL),
        P(),
        P(),
        P(),
        P(),
        P(TILE, COL),
        P(TILE, COL),
        P(),
    )
    out_specs = (P("sec", None, None, TILE, COL), P(), P())
    return jax.shard_map(local, mesh=fine, in_specs=in_specs, out_specs=out_specs, check_vma=False)
```

```python
import math

import jax
import jax.numpy as jnp
import numpy as np
from jax import lax
from jax.experimental import pallas as pl
from jax.experimental.pallas import tpu as pltpu
from jax.sharding import Mesh, PartitionSpec as P

V = 8
L = 16
H = 4096
F = 128
STEPS = 4
MB = 8
NX = 32
NY = 512
CHUNK = 16
HALO = STEPS
SLAB = CHUNK + 2 * HALO
MSG = 48
CODE = 32000.0
UNIT = 32768.0 / CODE
OWN = NX * CHUNK
COLS = STEPS * OWN
HB1 = 2048
HB2 = 1024
WIDE = 512
STRIP = 32
HALF = H // 2
GRAD_SCALE = 1.0 / math.sqrt(MB * STEPS * NX * NY)
TILE = ("zh", "cx", "core")
COL = ("c1", "c0")
SPREAD = ("sec", "cx", "c0")
PARTS = 32
ROWS = H // 2 // PARTS


def mode_block():
    order = np.arange(L)
    angles = np.pi * (order[None, :] + 0.5) * order[:, None] / L
    weights = np.where(order[:, None] == 0, math.sqrt(1.0 / L), math.sqrt(2.0 / L))
    return np.kron(np.eye(V), np.cos(angles) * weights)


def split_table(matrix):
    high = matrix.astype(jnp.bfloat16)
    low = (matrix - high.astype(np.float64)).astype(jnp.bfloat16)
    return np.concatenate([high, high, low], axis=0)


def params(semantics=None, mib=60):
    return pltpu.CompilerParams(dimension_semantics=semantics, vmem_limit_bytes=mib * 2**20)


def exponent(largest):
    return jnp.ceil(jnp.log(jnp.maximum(largest, 1e-30)) * (1.0 / math.log(2.0)) + 0.01)


def encode(value, power):
    scaled = value * (jnp.exp2(15.0 - power) * (1.0 / UNIT))
    return jnp.round(jnp.clip(scaled, -32767.0, 32767.0))


def to_int16(value):
    return value.astype(jnp.int32).astype(jnp.int16)


def to_float(code):
    return code.astype(jnp.int32).astype(jnp.float32)


def decode(value, power):
    return value * (jnp.exp2(power - 15.0) * UNIT)


def init_kernel(meta_ref, plan_ref, state_ref, land_ref, levels_ref, msg_ref):
    power = exponent(jnp.max(jnp.abs(state_ref[0]), keepdims=True))
    code = [encode(state_ref[0, pl.ds(x, F, stride=2), :], power).T for x in range(2)]
    depth = jnp.where(land_ref[...] == 1, levels_ref[...], 0).astype(jnp.float32)
    extra = jnp.concatenate(
        [depth, jnp.broadcast_to(power, (1, 128)), jnp.zeros((5, 128), jnp.float32)], axis=0
    )
    for j in range(8):
        y = CHUNK * j
        first = [c[y : y + HALO] for c in code]
        middle = [c[y + HALO : y + CHUNK - HALO] for c in code]
        last = [c[y + CHUNK - HALO : y + CHUNK] for c in code]
        msg_ref[j] = to_int16(jnp.concatenate(first + [extra] + middle + last + [extra], axis=0))


def init_slabs(meta, plan, states, land_mask, wet_levels):
    whole = lambda i, meta, plan: (0, 0)
    return pl.pallas_call(
        init_kernel,
        grid_spec=pltpu.PrefetchScalarGridSpec(
            num_scalar_prefetch=2,
            grid=(2,),
            in_specs=[
                pl.BlockSpec((1, 2 * F, 128), lambda i, meta, plan: (plan[2 * meta[0] + i], 0, 0)),
                pl.BlockSpec((2, 128), whole),
                pl.BlockSpec((2, 128), whole),
            ],
            out_specs=pl.BlockSpec((8, MSG, F), lambda i, meta, plan: (i, 0, 0)),
        ),
        out_shape=jax.ShapeDtypeStruct((16, MSG, F), jnp.int16),
        compiler_params=params(("arbitrary",)),
        name="init_slabs",
    )(meta, plan, states, land_mask, wet_levels)


def levels():
    return (lax.broadcasted_iota(jnp.int32, (1, F), 1) % L).astype(jnp.float32)


def split_dot(value, table):
    high = value.astype(jnp.bfloat16)
    low = (value - high.astype(jnp.float32)).astype(jnp.bfloat16)
    both = jnp.concatenate([high, low], axis=1)
    return jnp.dot(both, table[0 : 2 * F], preferred_element_type=jnp.float32) + jnp.dot(
        high, table[2 * F :], preferred_element_type=jnp.float32
    )


def rollout_kernel(
    meta_ref, msg_ref, left_ref, right_ref, w_in_t, w_out_t, mode_ref, mode_t, diff_ref, stiff_ref,
    traj_ref, inputs_ref, tend_ref, own_wet_ref,
    state, wet, modal, acc, x_scr, gain, pull, depth, depth_t, before, hidden,
):
    for t in range(16):
        for n, (ref, base) in enumerate(
            ((msg_ref, 0), (msg_ref, 16), (msg_ref, 32), (right_ref, 0), (left_ref, 0))
        ):
            piece = to_float(ref[t, base : base + 16])
            if n != 1:
                scale = decode(1.0, piece[10:11])
            rows = 8 if n == 1 else HALO
            at = (0, HALO, CHUNK - HALO, CHUNK, CHUNK + HALO)[n]
            for x in range(2):
                state[2 * t + x, at : at + rows] = piece[x * rows : (x + 1) * rows] * scale
            if n in (0, 3, 4):
                depth[n // 2 if n else 0, 2 * t : 2 * t + 2] = piece[8:10]
    for n in range(3):
        depth_t[n] = depth[n].T
    mine = meta_ref[1]
    y_own = pl.multiple_of(mine * CHUNK, CHUNK)
    y_right = pl.multiple_of(lax.rem(mine + 1, 8) * CHUNK, CHUNK)
    y_left = pl.multiple_of(lax.rem(mine + 7, 8) * CHUNK + 8, 8)
    here = jnp.concatenate(
        [
            depth_t[0, pl.ds(y_own, CHUNK)],
            depth_t[1, pl.ds(y_right, 8)][:HALO],
            depth_t[2, pl.ds(y_left, 8)][8 - HALO :],
        ],
        axis=0,
    )
    level = levels()
    for x in range(NX):
        wet[x] = jnp.where(level < here[:, x : x + 1], 1.0, 0.0)
    own_wet_ref[...] = wet[:, :CHUNK]

    a = stiff_ref[...]
    u = 1.0 + a
    for i in range(NX):
        r = 1.0 / (a + u)
        gain[pl.ds(i, 1), :] = r
        pull[pl.ds(i, 1), :] = a * r
        u = 1.0 + a * (u * r)
    diff = diff_ref[...].reshape(1, 1, F)
    edge = jnp.zeros((1, SLAB, F), jnp.float32)
    for step in range(STEPS):
        now = state[...]
        around = (
            jnp.concatenate([edge, now[:-1]], axis=0)
            + jnp.concatenate([now[1:], edge], axis=0)
            + pltpu.roll(now, 1, 1)
            + pltpu.roll(now, SLAB - 1, 1)
            - 4.0 * now
        )
        smoothed = wet[...] * (now + diff * around)
        modal[...] = split_dot(smoothed.reshape(NX * SLAB, F), mode_t).reshape(NX, SLAB, F)
        part = modal[0] * gain[pl.ds(0, 1), :]
        modal[0] = part
        for i in range(1, NX):
            part = modal[i] * gain[pl.ds(i, 1), :] + pull[pl.ds(i, 1), :] * part
            modal[i] = part
        for i in range(NX - 2, -1, -1):
            part = modal[i] + pull[pl.ds(i, 1), :] * part
            modal[i] = part
        after = split_dot(modal[...].reshape(NX * SLAB, F), mode_ref).reshape(NX, SLAB, F)
        after = wet[...] * after
        rows = SLAB if step < STEPS - 1 else CHUNK
        after = after[:, :rows]
        state[:, :rows] = after
        x_scr[0 : NX * rows] = after.reshape(NX * rows, F).astype(jnp.bfloat16)
        inputs_ref[step] = after[:, :CHUNK].astype(jnp.bfloat16)
        acc[0 : NX * rows] = jnp.zeros((NX * rows, F), jnp.float32)

        def block(b, carry, n=NX * rows):
            def front(i):
                at = pl.multiple_of(b * HB1 + i * WIDE, WIDE)
                before[i % 2, 0:n] = jnp.dot(
                    x_scr[0:n], w_in_t[:, pl.ds(at, WIDE)], preferred_element_type=jnp.float32
                )
                return at

            at = front(0)
            for i in range(HB1 // WIDE):
                following = front(i + 1) if i + 1 < HB1 // WIDE else None
                for r in range(0, n, STRIP):
                    strip = jnp.tanh(before[i % 2, r : r + STRIP])
                    hidden[i % 2, r : r + STRIP] = strip.astype(jnp.bfloat16)
                acc[0:n] += jnp.dot(
                    hidden[i % 2, 0:n],
                    w_out_t[pl.ds(at, WIDE), :],
                    preferred_element_type=jnp.float32,
                )
                at = following
            return carry

        lax.fori_loop(0, H // HB1, block, 0)
        tendency = acc[0 : NX * rows].reshape(NX, rows, F)
        result = wet[:, :rows] * (state[:, :rows] + tendency)
        state[:, :rows] = result
        traj_ref[step] = result[:, :CHUNK].astype(jnp.bfloat16)
        tend_ref[step] = tendency[:, :CHUNK]


def rollout(meta, msg, left, right, w_in_t, w_out_t, diffusivity, stiffness):
    block = mode_block()
    vmem = pl.BlockSpec(memory_space=pltpu.VMEM)
    return pl.pallas_call(
        rollout_kernel,
        out_shape=[
            jax.ShapeDtypeStruct((STEPS, NX, CHUNK, F), jnp.bfloat16),
            jax.ShapeDtypeStruct((STEPS, NX, CHUNK, F), jnp.bfloat16),
            jax.ShapeDtypeStruct((STEPS, NX, CHUNK, F), jnp.float32),
            jax.ShapeDtypeStruct((NX, CHUNK, F), jnp.float32),
        ],
        in_specs=[pl.BlockSpec(memory_space=pltpu.SMEM)] + [vmem] * 9,
        out_specs=[vmem] * 4,
        scratch_shapes=[
            pltpu.VMEM((NX, SLAB, F), jnp.float32),
            pltpu.VMEM((NX, SLAB, F), jnp.float32),
            pltpu.VMEM((NX, SLAB, F), jnp.float32),
            pltpu.VMEM((NX * SLAB, F), jnp.float32),
            pltpu.VMEM((NX * SLAB, F), jnp.bfloat16),
            pltpu.VMEM((NX, F), jnp.float32),
            pltpu.VMEM((NX, F), jnp.float32),
            pltpu.VMEM((3, NX, 128), jnp.float32),
            pltpu.VMEM((3, 128, NX), jnp.float32),
            pltpu.VMEM((2, NX * SLAB, WIDE), jnp.float32),
            pltpu.VMEM((2, NX * SLAB, WIDE), jnp.bfloat16),
        ],
        compiler_params=params(),
        cost_estimate=pl.CostEstimate(
            flops=4 * 2816 * F * H, bytes_accessed=6 * 2**20, transcendentals=2816 * H
        ),
        name="rollout",
    )(
        meta,
        msg,
        left,
        right,
        w_in_t,
        w_out_t,
        jnp.asarray(split_table(block)),
        jnp.asarray(split_table(block.T)),
        diffusivity.reshape(1, F),
        stiffness.reshape(1, F),
    )


def prepare_kernel(plan_ref, target_ref, w_in_ref, w_out_ref, out_ref, w_in_t, w_out_t, wide):
    wide[...] = target_ref[0].astype(jnp.float32)
    for x in range(2):
        t = wide[pl.ds(x, F, stride=2), :].T
        out_ref[0, :, x] = t.reshape(8, CHUNK, F).astype(jnp.bfloat16)
    w_in_t[...] = w_in_ref[...].T
    w_out_t[...] = w_out_ref[...].T


def prepare(targets, w_in, w_out, plan):
    part = H // MB
    down = lambda i, plan: (i, 0)
    along = lambda i, plan: (0, i)
    return pl.pallas_call(
        prepare_kernel,
        grid_spec=pltpu.PrefetchScalarGridSpec(
            num_scalar_prefetch=1,
            grid=(MB,),
            in_specs=[
                pl.BlockSpec((1, 2 * F, 128), lambda i, plan: (plan[i], 0, 0)),
                pl.BlockSpec((part, F), down),
                pl.BlockSpec((F, part), along),
            ],
            out_specs=[
                pl.BlockSpec((1, 8, 2, CHUNK, F), lambda i, plan: (i, 0, 0, 0, 0)),
                pl.BlockSpec((F, part), along),
                pl.BlockSpec((part, F), down),
            ],
            scratch_shapes=[pltpu.VMEM((2 * F, 128), jnp.float32)],
        ),
        out_shape=[
            jax.ShapeDtypeStruct((MB, 8, 2, CHUNK, F), jnp.bfloat16),
            jax.ShapeDtypeStruct((F, H), jnp.bfloat16),
            jax.ShapeDtypeStruct((H, F), jnp.bfloat16),
        ],
        compiler_params=params(),
        cost_estimate=pl.CostEstimate(flops=0, bytes_accessed=6 * 2**20, transcendentals=0),
        name="prepare",
    )(plan, targets, w_in, w_out)


def spread_kernel(in_ref, out_ref):
    for x in range(2):
        block = in_ref[0, :, x].astype(jnp.float32).reshape(128, F)
        out_ref[0, pl.ds(x, F, stride=2), :] = block.T


def spread_trajectory(arrived):
    return pl.pallas_call(
        spread_kernel,
        grid=(MB,),
        in_specs=[pl.BlockSpec((1, 8, 2, CHUNK, F), lambda i: (i, 0, 0, 0, 0))],
        out_specs=pl.BlockSpec((1, 2 * F, 128), lambda i: (i, 0, 0)),
        out_shape=jax.ShapeDtypeStruct((MB, 2 * F, 128), jnp.float32),
        compiler_params=params(),
        name="spread_trajectory",
    )(arrived)


def grad_block(x_ref, x_t, misfit, misfit_t, w_in_ref, w_out_t_ref, out_ref, scratch):
    before, back, hidden, change = scratch
    rows = w_in_ref.shape[0]

    def front(part):
        at = slice(part * WIDE, (part + 1) * WIDE)
        before[part % 2] = jnp.dot(w_in_ref[...], x_t[:, at], preferred_element_type=jnp.float32)
        back[part % 2] = jnp.dot(
            w_out_t_ref[...], misfit_t[:, at], preferred_element_type=jnp.float32
        )
        return at

    grad_in = jnp.zeros((rows, F), jnp.float32)
    grad_out = jnp.zeros((rows, F), jnp.float32)
    at = front(0)
    for part in range(COLS // WIDE):
        following = front(part + 1) if part + 1 < COLS // WIDE else None
        n = part % 2
        for r in range(0, rows, STRIP):
            strip = jnp.tanh(before[n, r : r + STRIP])
            hidden[n, r : r + STRIP] = strip.astype(jnp.bfloat16)
            strip = back[n, r : r + STRIP] * (1.0 - strip * strip)
            change[n, r : r + STRIP] = strip.astype(jnp.bfloat16)
        grad_out += jnp.dot(hidden[n], misfit[at], preferred_element_type=jnp.float32)
        grad_in += jnp.dot(change[n], x_ref[at], preferred_element_type=jnp.float32)
        at = following
    out_ref[:, 0] = grad_in.reshape(rows // ROWS, ROWS, F)
    out_ref[:, 1] = grad_out.reshape(rows // ROWS, ROWS, F)


def first_kernel(
    half_ref, x_ref, tend_ref, target_ref, wet_ref, w_in_ref, w_out_ref,
    out_ref, x_t, misfit, misfit_t,
    *scratch,
):
    @pl.when(pl.program_id(0) == 0)
    def _():
        for step in range(STEPS):
            at = slice(step * OWN, (step + 1) * OWN)
            gap = wet_ref[...] * (tend_ref[at] - target_ref[at].astype(jnp.float32))
            gap = (gap * GRAD_SCALE).astype(jnp.bfloat16)
            misfit[at] = gap
            misfit_t[:, at] = gap.T
            x_t[:, at] = x_ref[at].T

    grad_block(x_ref, x_t, misfit, misfit_t, w_in_ref, w_out_ref, out_ref, scratch)


def second_kernel(
    half_ref, x_ref, x_t, misfit, misfit_t, w_in_ref, w_out_ref, out_ref, *scratch
):
    grad_block(x_ref, x_t, misfit, misfit_t, w_in_ref, w_out_ref, out_ref, scratch)


def half_grads(half, columns, w_in, w_out_t, first):
    blocks = HALF // HB2
    whole = lambda i, half: (0, 0)
    weight = lambda i, half: (half[0] * blocks + i, 0)
    out_specs = [pl.BlockSpec((HB2 // ROWS, 2, ROWS, F), lambda i, half: (i, 0, 0, 0))]
    out_shape = [jax.ShapeDtypeStruct((PARTS, 2, ROWS, F), jnp.float32)]
    if first:
        for shape in ((F, COLS), (COLS, F), (F, COLS)):
            out_specs.append(pl.BlockSpec(shape, whole))
            out_shape.append(jax.ShapeDtypeStruct(shape, jnp.bfloat16))
    return pl.pallas_call(
        first_kernel if first else second_kernel,
        grid_spec=pltpu.PrefetchScalarGridSpec(
            num_scalar_prefetch=1,
            grid=(blocks,),
            in_specs=[pl.BlockSpec(c.shape, whole) for c in columns]
            + [pl.BlockSpec((HB2, F), weight)] * 2,
            out_specs=out_specs,
            scratch_shapes=[pltpu.VMEM((2, HB2, WIDE), jnp.float32)] * 2
            + [pltpu.VMEM((2, HB2, WIDE), jnp.bfloat16)] * 2,
        ),
        out_shape=out_shape,
        compiler_params=params(("arbitrary",)),
        cost_estimate=pl.CostEstimate(flops=10**8, bytes_accessed=2**20, transcendentals=0),
        name="first_grads" if first else "second_grads",
    )(half, *columns, w_in, w_out_t)


def pair_kernel(mine_ref, other_ref, out_ref):
    out_ref[...] = (mine_ref[...] + other_ref[...]).astype(jnp.bfloat16)


def pair_sum(mine, other):
    block = pl.BlockSpec((PARTS // 4, 2, ROWS, F), lambda i: (i, 0, 0, 0))
    return pl.pallas_call(
        pair_kernel,
        grid=(4,),
        in_specs=[block] * 2,
        out_specs=block,
        out_shape=jax.ShapeDtypeStruct((PARTS, 2, ROWS, F), jnp.bfloat16),
        compiler_params=params(("arbitrary",)),
        name="pair_sum",
    )(mine, other)


def plane_kernel(in_ref, out_ref):
    total = in_ref[0].astype(jnp.float32)
    for n in range(1, PARTS):
        total += in_ref[n].astype(jnp.float32)
    out_ref[...] = total.astype(jnp.bfloat16)


def plane_sum(parts):
    vmem = pl.BlockSpec(memory_space=pltpu.VMEM)
    return pl.pallas_call(
        plane_kernel,
        out_shape=jax.ShapeDtypeStruct((2, ROWS, F), jnp.bfloat16),
        in_specs=[vmem],
        out_specs=vmem,
        compiler_params=params(mib=32),
        name="plane_sum",
    )(parts)


def column_kernel(own_ref, near_ref, far_ref, both_ref, out_ref):
    powers = []
    for g in range(2):
        own, near, far, both = (
            ref[g].astype(jnp.float32) for ref in (own_ref, near_ref, far_ref, both_ref)
        )
        total = (own + near) + (far + both)
        power = exponent(jnp.max(jnp.abs(total), axis=0, keepdims=True))
        powers.append(power)
        code = to_int16(encode(total, power))
        for n in range(PARTS):
            out_ref[n, g * ROWS : (g + 1) * ROWS] = code
    tail = to_int16(jnp.concatenate(powers + [jnp.zeros((14, F), jnp.float32)], axis=0))
    for n in range(PARTS):
        out_ref[n, 2 * ROWS : 2 * ROWS + 16] = tail


def column_copies(*planes):
    vmem = pl.BlockSpec(memory_space=pltpu.VMEM)
    return pl.pallas_call(
        column_kernel,
        out_shape=jax.ShapeDtypeStruct((PARTS, 2 * ROWS + 16, F), jnp.int16),
        in_specs=[vmem] * 4,
        out_specs=vmem,
        compiler_params=params(mib=32),
        name="column_copies",
    )(*planes)


def finish_kernel(half_ref, code_ref, *refs):
    grad_in_ref, grad_out_ref = refs[-2:]
    for n in range(0, code_ref.shape[0], 2):
        at = slice(n * ROWS, (n + 2) * ROWS)
        both = []
        for m in (n, n + 1):
            code = to_float(code_ref[m])
            grad_in_ref[m * ROWS : (m + 1) * ROWS] = decode(
                code[0:ROWS], code[2 * ROWS : 2 * ROWS + 1]
            )
            both.append(decode(code[ROWS : 2 * ROWS], code[2 * ROWS + 1 : 2 * ROWS + 2]))
        grad_out_ref[:, at] = jnp.concatenate(both, axis=0).T


def finish_half(half, code, before=()):
    return pl.pallas_call(
        finish_kernel,
        grid_spec=pltpu.PrefetchScalarGridSpec(
            num_scalar_prefetch=1,
            grid=(2,),
            in_specs=[pl.BlockSpec((PARTS // 2, 2 * ROWS + 16, F), lambda i, half: (i, 0, 0))]
            + [pl.BlockSpec(memory_space=pl.ANY)] * len(before),
            out_specs=[
                pl.BlockSpec((1024, F), lambda i, half: (half[0] * 2 + i, 0)),
                pl.BlockSpec((F, 1024), lambda i, half: (0, half[0] * 2 + i)),
            ],
        ),
        out_shape=[
            jax.ShapeDtypeStruct((H, F), jnp.float32),
            jax.ShapeDtypeStruct((F, H), jnp.float32),
        ],
        input_output_aliases={2: 0, 3: 1} if before else {},
        compiler_params=params(("arbitrary",), 32),
        name="finish_half",
    )(half, code, *before)


def swap(value, axes):
    return lax.all_to_all(value, axes, split_axis=0, concat_axis=0, tiled=True)


def local(initial_states, targets, w_in, w_out, diffusivity, stiffness, land_mask, wet_levels, plan):
    core = lax.axis_index("core").astype(jnp.int32).reshape(1)
    meta = jnp.stack([lax.axis_index("sec"), lax.axis_index(TILE) % 8]).astype(jnp.int32)

    states = initial_states.reshape(MB, 2 * F, 128)
    msg = swap(init_slabs(meta, plan, states, land_mask, wet_levels), TILE)
    place = lambda half, chunk, col: (half * 8 + chunk) * 4 + col
    forward = [
        (place(h, j, c), place(h, (j + 1) % 8, c + (j + 1) // 8))
        for h in range(2)
        for j in range(8)
        for c in range(4)
        if c + (j + 1) // 8 < 4
    ]
    left = lax.ppermute(msg[:, 32:48], TILE + COL, forward)
    right = lax.ppermute(msg[:, 0:16], TILE + COL, [(b, a) for a, b in forward])

    target, w_in_t, w_out_t = prepare(targets.reshape(MB, 2 * F, 128), w_in, w_out, plan)
    target = swap(target.reshape(64, 2, CHUNK, F), ("sec",) + TILE).reshape(COLS, F)

    traj, inputs, tend, wet = rollout(meta, msg, left, right, w_in_t, w_out_t, diffusivity, stiffness)
    arrived = swap(traj.reshape(64, 2, CHUNK, F), ("sec",) + TILE)

    inputs = inputs.reshape(COLS, F)
    columns = (inputs, tend.reshape(COLS, F), target, wet.reshape(OWN, F))
    other, *columns = half_grads(1 - core, columns, w_in, w_out_t, True)
    swapped = lax.ppermute(other, "core", [(0, 1), (1, 0)])
    (mine,) = half_grads(core, (inputs, *columns), w_in, w_out_t, False)
    mine, arrived = lax.optimization_barrier((mine, arrived))
    pair = pair_sum(mine, swapped)

    trajectory = spread_trajectory(arrived.reshape(MB, 8, 2, CHUNK, F))
    plane = plane_sum(swap(pair, SPREAD))
    plane, trajectory = lax.optimization_barrier((plane, trajectory))
    others = [
        lax.ppermute(plane, ("zh", "c1"), [(i, i ^ n) for i in range(4)]) for n in range(1, 4)
    ]
    code = swap(column_copies(plane, *others), SPREAD)
    across = lax.ppermute(code, "core", [(0, 1), (1, 0)])
    grad_in, grad_out = finish_half(1 - core, across, finish_half(core, code))
    return (trajectory.reshape(1, MB, F, 2, 128), grad_in, grad_out)


def solution(mesh):
    fine = Mesh(mesh.devices.reshape(4, 2, 4, 2, 2, 2), ("sec", "zh", "cx", "core", "c1", "c0"))
    in_specs = (
        P(None, None, TILE, COL),
        P("sec", None, None, TILE, COL),
        P(),
        P(),
        P(),
        P(),
        P(TILE, COL),
        P(TILE, COL),
        P(),
    )
    out_specs = (P("sec", None, None, TILE, COL), P(), P())
    return jax.shard_map(local, mesh=fine, in_specs=in_specs, out_specs=out_specs, check_vma=False)
```

```python
import math

import jax
import jax.numpy as jnp
import numpy as np
from jax import lax
from jax.experimental import pallas as pl
from jax.experimental.pallas import tpu as pltpu
from jax.sharding import Mesh, PartitionSpec as P

V = 8
L = 16
H = 4096
F = 128
STEPS = 4
MB = 8
NX = 32
NY = 512
CHUNK = 16
HALO = STEPS
SLAB = CHUNK + 2 * HALO
MSG = 48
CODE = 32000.0
UNIT = 32768.0 / CODE
OWN = NX * CHUNK
COLS = STEPS * OWN
HB1 = 2048
HB2 = 1024
WIDE = 512
STRIP = 32
HALF = H // 2
GRAD_SCALE = 1.0 / math.sqrt(MB * STEPS * NX * NY)
TILE = ("zh", "cx", "core")
COL = ("c1", "c0")
SPREAD = ("sec", "cx", "c0")
PARTS = 32
ROWS = H // 2 // PARTS


def mode_block():
    order = np.arange(L)
    angles = np.pi * (order[None, :] + 0.5) * order[:, None] / L
    weights = np.where(order[:, None] == 0, math.sqrt(1.0 / L), math.sqrt(2.0 / L))
    return np.kron(np.eye(V), np.cos(angles) * weights)


def split_table(matrix):
    high = matrix.astype(jnp.bfloat16)
    low = (matrix - high.astype(np.float64)).astype(jnp.bfloat16)
    return np.concatenate([high, high, low], axis=0)


def params(semantics=None, mib=60):
    return pltpu.CompilerParams(dimension_semantics=semantics, vmem_limit_bytes=mib * 2**20)


def exponent(largest):
    return jnp.ceil(jnp.log(jnp.maximum(largest, 1e-30)) * (1.0 / math.log(2.0)) + 0.01)


def encode(value, power):
    scaled = value * (jnp.exp2(15.0 - power) * (1.0 / UNIT))
    return jnp.round(jnp.clip(scaled, -32767.0, 32767.0))


def to_int16(value):
    return value.astype(jnp.int32).astype(jnp.int16)


def to_float(code):
    return code.astype(jnp.int32).astype(jnp.float32)


def decode(value, power):
    return value * (jnp.exp2(power - 15.0) * UNIT)


def init_kernel(meta_ref, plan_ref, state_ref, land_ref, levels_ref, msg_ref):
    power = exponent(jnp.max(jnp.abs(state_ref[0]), keepdims=True))
    code = [encode(state_ref[0, pl.ds(x, F, stride=2), :], power).T for x in range(2)]
    depth = jnp.where(land_ref[...] == 1, levels_ref[...], 0).astype(jnp.float32)
    extra = jnp.concatenate(
        [depth, jnp.broadcast_to(power, (1, 128)), jnp.zeros((5, 128), jnp.float32)], axis=0
    )
    for j in range(8):
        y = CHUNK * j
        first = [c[y : y + HALO] for c in code]
        middle = [c[y + HALO : y + CHUNK - HALO] for c in code]
        last = [c[y + CHUNK - HALO : y + CHUNK] for c in code]
        msg_ref[j] = to_int16(jnp.concatenate(first + [extra] + middle + last + [extra], axis=0))


def init_slabs(meta, plan, states, land_mask, wet_levels):
    whole = lambda i, meta, plan: (0, 0)
    return pl.pallas_call(
        init_kernel,
        grid_spec=pltpu.PrefetchScalarGridSpec(
            num_scalar_prefetch=2,
            grid=(2,),
            in_specs=[
                pl.BlockSpec((1, 2 * F, 128), lambda i, meta, plan: (plan[2 * meta[0] + i], 0, 0)),
                pl.BlockSpec((2, 128), whole),
                pl.BlockSpec((2, 128), whole),
            ],
            out_specs=pl.BlockSpec((8, MSG, F), lambda i, meta, plan: (i, 0, 0)),
        ),
        out_shape=jax.ShapeDtypeStruct((16, MSG, F), jnp.int16),
        compiler_params=params(("arbitrary",)),
        name="init_slabs",
    )(meta, plan, states, land_mask, wet_levels)


def levels():
    return (lax.broadcasted_iota(jnp.int32, (1, F), 1) % L).astype(jnp.float32)


def pack_halo(halo, step):
    if step == STEPS - 1:
        return jnp.zeros((0, F), jnp.float32)
    share = (1, 2, 4)[step]
    halo = halo.reshape(NX // share, share, 8, F)
    packed = halo[:, 0]
    row = lax.broadcasted_iota(jnp.int32, packed.shape, 1)
    for n in range(1, share):
        shift = n * 8 // share
        keep = STEPS - 1 - step
        place = (row + (8 - shift) + keep) % 8 < 2 * keep
        packed = jnp.where(place, pltpu.roll(halo[:, n], shift, 1), packed)
    return packed.reshape(NX // share * 8, F)


def unpack_halo(packed, step):
    share = (1, 2, 4)[step]
    packed = packed.reshape(NX // share, 8, F)
    parts = [packed] + [pltpu.roll(packed, 8 - n * 8 // share, 1) for n in range(1, share)]
    return jnp.stack(parts, axis=1).reshape(NX, 8, F)


def split_dot(value, table):
    high = value.astype(jnp.bfloat16)
    low = (value - high.astype(jnp.float32)).astype(jnp.bfloat16)
    both = jnp.concatenate([high, low], axis=1)
    return jnp.dot(both, table[0 : 2 * F], preferred_element_type=jnp.float32) + jnp.dot(
        high, table[2 * F :], preferred_element_type=jnp.float32
    )


def rollout_kernel(
    meta_ref, msg_ref, left_ref, right_ref, w_in_t, w_out_t, mode_ref, mode_t, diff_ref, stiff_ref,
    traj_ref, inputs_ref, tend_ref, own_wet_ref,
    state, wet, modal, acc, x_scr, gain, pull, depth, depth_t, before, hidden,
):
    for t in range(16):
        for n, (ref, base) in enumerate(
            ((msg_ref, 0), (msg_ref, 16), (msg_ref, 32), (right_ref, 0), (left_ref, 0))
        ):
            piece = to_float(ref[t, base : base + 16])
            if n != 1:
                scale = decode(1.0, piece[10:11])
            rows = 8 if n == 1 else HALO
            at = (0, HALO, CHUNK - HALO, CHUNK, CHUNK + HALO)[n]
            for x in range(2):
                state[2 * t + x, at : at + rows] = piece[x * rows : (x + 1) * rows] * scale
            if n in (0, 3, 4):
                depth[n // 2 if n else 0, 2 * t : 2 * t + 2] = piece[8:10]
    for n in range(3):
        depth_t[n] = depth[n].T
    mine = meta_ref[1]
    y_own = pl.multiple_of(mine * CHUNK, CHUNK)
    y_right = pl.multiple_of(lax.rem(mine + 1, 8) * CHUNK, CHUNK)
    y_left = pl.multiple_of(lax.rem(mine + 7, 8) * CHUNK + 8, 8)
    here = jnp.concatenate(
        [
            depth_t[0, pl.ds(y_own, CHUNK)],
            depth_t[1, pl.ds(y_right, 8)][:HALO],
            depth_t[2, pl.ds(y_left, 8)][8 - HALO :],
        ],
        axis=0,
    )
    level = levels()
    for x in range(NX):
        wet[x] = jnp.where(level < here[:, x : x + 1], 1.0, 0.0)
    own_wet_ref[...] = wet[:, :CHUNK]

    a = stiff_ref[...]
    u = 1.0 + a
    for i in range(NX):
        r = 1.0 / (a + u)
        gain[pl.ds(i, 1), :] = r
        pull[pl.ds(i, 1), :] = a * r
        u = 1.0 + a * (u * r)
    diff = diff_ref[...].reshape(1, 1, F)
    edge = jnp.zeros((1, SLAB, F), jnp.float32)
    for step in range(STEPS):
        now = state[...]
        around = (
            jnp.concatenate([edge, now[:-1]], axis=0)
            + jnp.concatenate([now[1:], edge], axis=0)
            + pltpu.roll(now, 1, 1)
            + pltpu.roll(now, SLAB - 1, 1)
            - 4.0 * now
        )
        smoothed = wet[...] * (now + diff * around)
        modal[...] = split_dot(smoothed.reshape(NX * SLAB, F), mode_t).reshape(NX, SLAB, F)
        part = modal[0] * gain[pl.ds(0, 1), :]
        modal[0] = part
        for i in range(1, NX):
            part = modal[i] * gain[pl.ds(i, 1), :] + pull[pl.ds(i, 1), :] * part
            modal[i] = part
        for i in range(NX - 2, -1, -1):
            part = modal[i] + pull[pl.ds(i, 1), :] * part
            modal[i] = part
        after = split_dot(modal[...].reshape(NX * SLAB, F), mode_ref).reshape(NX, SLAB, F)
        after = wet[...] * after
        inputs_ref[step] = after[:, :CHUNK].astype(jnp.bfloat16)
        extra = pack_halo(after[:, CHUNK:], step)
        count = OWN + extra.shape[0]
        state[...] = after
        x_scr[0:OWN] = after[:, :CHUNK].reshape(OWN, F).astype(jnp.bfloat16)
        if step < STEPS - 1:
            x_scr[OWN:count] = extra.astype(jnp.bfloat16)
        acc[0:count] = jnp.zeros((count, F), jnp.float32)

        def block(b, carry, n=count):
            def front(i):
                at = pl.multiple_of(b * HB1 + i * WIDE, WIDE)
                before[i % 2, 0:n] = jnp.dot(
                    x_scr[0:n], w_in_t[:, pl.ds(at, WIDE)], preferred_element_type=jnp.float32
                )
                return at

            at = front(0)
            for i in range(HB1 // WIDE):
                following = front(i + 1) if i + 1 < HB1 // WIDE else None
                for r in range(0, n, STRIP):
                    strip = jnp.tanh(before[i % 2, r : r + STRIP])
                    hidden[i % 2, r : r + STRIP] = strip.astype(jnp.bfloat16)
                acc[0:n] += jnp.dot(
                    hidden[i % 2, 0:n],
                    w_out_t[pl.ds(at, WIDE), :],
                    preferred_element_type=jnp.float32,
                )
                at = following
            return carry

        lax.fori_loop(0, H // HB1, block, 0)
        tendency = acc[0:OWN].reshape(NX, CHUNK, F)
        result = wet[:, :CHUNK] * (state[:, :CHUNK] + tendency)
        traj_ref[step] = result.astype(jnp.bfloat16)
        tend_ref[step] = tendency
        if step < STEPS - 1:
            beside = unpack_halo(acc[OWN:count], step)
            state[:, CHUNK:] = wet[:, CHUNK:] * (state[:, CHUNK:] + beside)
            state[:, :CHUNK] = result


def rollout(meta, msg, left, right, w_in_t, w_out_t, diffusivity, stiffness):
    block = mode_block()
    vmem = pl.BlockSpec(memory_space=pltpu.VMEM)
    return pl.pallas_call(
        rollout_kernel,
        out_shape=[
            jax.ShapeDtypeStruct((STEPS, NX, CHUNK, F), jnp.bfloat16),
            jax.ShapeDtypeStruct((STEPS, NX, CHUNK, F), jnp.bfloat16),
            jax.ShapeDtypeStruct((STEPS, NX, CHUNK, F), jnp.float32),
            jax.ShapeDtypeStruct((NX, CHUNK, F), jnp.float32),
        ],
        in_specs=[pl.BlockSpec(memory_space=pltpu.SMEM)] + [vmem] * 9,
        out_specs=[vmem] * 4,
        scratch_shapes=[
            pltpu.VMEM((NX, SLAB, F), jnp.float32),
            pltpu.VMEM((NX, SLAB, F), jnp.float32),
            pltpu.VMEM((NX, SLAB, F), jnp.float32),
            pltpu.VMEM((NX * SLAB, F), jnp.float32),
            pltpu.VMEM((NX * SLAB, F), jnp.bfloat16),
            pltpu.VMEM((NX, F), jnp.float32),
            pltpu.VMEM((NX, F), jnp.float32),
            pltpu.VMEM((3, NX, 128), jnp.float32),
            pltpu.VMEM((3, 128, NX), jnp.float32),
            pltpu.VMEM((2, NX * SLAB, WIDE), jnp.float32),
            pltpu.VMEM((2, NX * SLAB, WIDE), jnp.bfloat16),
        ],
        compiler_params=params(),
        cost_estimate=pl.CostEstimate(
            flops=4 * 2816 * F * H, bytes_accessed=6 * 2**20, transcendentals=2816 * H
        ),
        name="rollout",
    )(
        meta,
        msg,
        left,
        right,
        w_in_t,
        w_out_t,
        jnp.asarray(split_table(block)),
        jnp.asarray(split_table(block.T)),
        diffusivity.reshape(1, F),
        stiffness.reshape(1, F),
    )


def prepare_kernel(plan_ref, target_ref, w_in_ref, w_out_ref, out_ref, w_in_t, w_out_t, wide):
    wide[...] = target_ref[0].astype(jnp.float32)
    for x in range(2):
        t = wide[pl.ds(x, F, stride=2), :].T
        out_ref[0, :, x] = t.reshape(8, CHUNK, F).astype(jnp.bfloat16)
    w_in_t[...] = w_in_ref[...].T
    w_out_t[...] = w_out_ref[...].T


def prepare(targets, w_in, w_out, plan):
    part = H // MB
    down = lambda i, plan: (i, 0)
    along = lambda i, plan: (0, i)
    return pl.pallas_call(
        prepare_kernel,
        grid_spec=pltpu.PrefetchScalarGridSpec(
            num_scalar_prefetch=1,
            grid=(MB,),
            in_specs=[
                pl.BlockSpec((1, 2 * F, 128), lambda i, plan: (plan[i], 0, 0)),
                pl.BlockSpec((part, F), down),
                pl.BlockSpec((F, part), along),
            ],
            out_specs=[
                pl.BlockSpec((1, 8, 2, CHUNK, F), lambda i, plan: (i, 0, 0, 0, 0)),
                pl.BlockSpec((F, part), along),
                pl.BlockSpec((part, F), down),
            ],
            scratch_shapes=[pltpu.VMEM((2 * F, 128), jnp.float32)],
        ),
        out_shape=[
            jax.ShapeDtypeStruct((MB, 8, 2, CHUNK, F), jnp.bfloat16),
            jax.ShapeDtypeStruct((F, H), jnp.bfloat16),
            jax.ShapeDtypeStruct((H, F), jnp.bfloat16),
        ],
        compiler_params=params(),
        cost_estimate=pl.CostEstimate(flops=0, bytes_accessed=6 * 2**20, transcendentals=0),
        name="prepare",
    )(plan, targets, w_in, w_out)


def spread_kernel(in_ref, out_ref):
    for x in range(2):
        block = in_ref[0, :, x].astype(jnp.float32).reshape(128, F)
        out_ref[0, pl.ds(x, F, stride=2), :] = block.T


def spread_trajectory(arrived):
    return pl.pallas_call(
        spread_kernel,
        grid=(MB,),
        in_specs=[pl.BlockSpec((1, 8, 2, CHUNK, F), lambda i: (i, 0, 0, 0, 0))],
        out_specs=pl.BlockSpec((1, 2 * F, 128), lambda i: (i, 0, 0)),
        out_shape=jax.ShapeDtypeStruct((MB, 2 * F, 128), jnp.float32),
        compiler_params=params(),
        name="spread_trajectory",
    )(arrived)


def grad_block(x_ref, x_t, misfit, misfit_t, w_in_ref, w_out_t_ref, scratch):
    before, back, hidden, change = scratch
    rows = w_in_ref.shape[0]

    def front(part):
        at = slice(part * WIDE, (part + 1) * WIDE)
        before[part % 2] = jnp.dot(w_in_ref[...], x_t[:, at], preferred_element_type=jnp.float32)
        back[part % 2] = jnp.dot(
            w_out_t_ref[...], misfit_t[:, at], preferred_element_type=jnp.float32
        )
        return at

    grad_in = jnp.zeros((rows, F), jnp.float32)
    grad_out = jnp.zeros((rows, F), jnp.float32)
    at = front(0)
    for part in range(COLS // WIDE):
        following = front(part + 1) if part + 1 < COLS // WIDE else None
        n = part % 2
        for r in range(0, rows, STRIP):
            strip = jnp.tanh(before[n, r : r + STRIP])
            hidden[n, r : r + STRIP] = strip.astype(jnp.bfloat16)
            strip = back[n, r : r + STRIP] * (1.0 - strip * strip)
            change[n, r : r + STRIP] = strip.astype(jnp.bfloat16)
        grad_out += jnp.dot(hidden[n], misfit[at], preferred_element_type=jnp.float32)
        grad_in += jnp.dot(change[n], x_ref[at], preferred_element_type=jnp.float32)
        at = following
    shape = (rows // ROWS, ROWS, F)
    return grad_in.reshape(shape), grad_out.reshape(shape)


def columns_kernel(x_ref, tend_ref, target_ref, wet_ref, out_ref):
    gap = wet_ref[...] * (tend_ref[...] - target_ref[...].astype(jnp.float32)) * GRAD_SCALE
    out_ref[0] = x_ref[...]
    out_ref[1] = gap.astype(jnp.bfloat16)


def own_columns(inputs, tend, target, wet):
    rows = pl.BlockSpec((OWN, F), lambda i: (i, 0))
    return pl.pallas_call(
        columns_kernel,
        grid=(STEPS,),
        in_specs=[rows] * 3 + [pl.BlockSpec((OWN, F), lambda i: (0, 0))],
        out_specs=pl.BlockSpec((2, OWN, F), lambda i: (0, i, 0)),
        out_shape=jax.ShapeDtypeStruct((2, COLS, F), jnp.bfloat16),
        compiler_params=params(("arbitrary",)),
        name="own_columns",
    )(inputs, tend, target, wet)


def grad_kernel(half_ref, columns_ref, w_in_ref, w_out_ref, *refs):
    *add_ref, out_ref, x_t, misfit_t, before, back, hidden, change = refs

    @pl.when(pl.program_id(0) == 0)
    def _():
        for part in range(STEPS):
            at = slice(part * OWN, (part + 1) * OWN)
            x_t[:, at] = columns_ref[0, at].T
            misfit_t[:, at] = columns_ref[1, at].T

    grads = grad_block(
        columns_ref.at[0],
        x_t,
        columns_ref.at[1],
        misfit_t,
        w_in_ref,
        w_out_ref,
        (before, back, hidden, change),
    )
    for n, grad in enumerate(grads):
        if add_ref:
            grad = grad + add_ref[0][:, n]
        out_ref[:, n] = grad.astype(out_ref.dtype)


def half_grads(half, columns, w_in, w_out_t, add=None):
    blocks = HALF // HB2
    weight = pl.BlockSpec((HB2, F), lambda i, half: (half[0] * blocks + i, 0))
    rows = pl.BlockSpec((HB2 // ROWS, 2, ROWS, F), lambda i, half: (i, 0, 0, 0))
    first = add is None
    return pl.pallas_call(
        grad_kernel,
        grid_spec=pltpu.PrefetchScalarGridSpec(
            num_scalar_prefetch=1,
            grid=(blocks,),
            in_specs=[pl.BlockSpec((2, COLS, F), lambda i, half: (0, 0, 0)), weight, weight]
            + ([] if first else [rows]),
            out_specs=rows,
            scratch_shapes=[pltpu.VMEM((F, COLS), jnp.bfloat16)] * 2
            + [pltpu.VMEM((2, HB2, WIDE), jnp.float32)] * 2
            + [pltpu.VMEM((2, HB2, WIDE), jnp.bfloat16)] * 2,
        ),
        out_shape=jax.ShapeDtypeStruct(
            (PARTS, 2, ROWS, F), jnp.float32 if first else jnp.bfloat16
        ),
        compiler_params=params(("arbitrary",)),
        cost_estimate=pl.CostEstimate(flops=10**8, bytes_accessed=2**20, transcendentals=0),
        name="first_grads" if first else "second_grads",
    )(half, columns, w_in, w_out_t, *(() if first else (add,)))


def plane_kernel(in_ref, out_ref):
    total = in_ref[0].astype(jnp.float32)
    for n in range(1, PARTS):
        total += in_ref[n].astype(jnp.float32)
    out_ref[...] = total.astype(jnp.bfloat16)


def plane_sum(parts):
    vmem = pl.BlockSpec(memory_space=pltpu.VMEM)
    return pl.pallas_call(
        plane_kernel,
        out_shape=jax.ShapeDtypeStruct((2, ROWS, F), jnp.bfloat16),
        in_specs=[vmem],
        out_specs=vmem,
        compiler_params=params(mib=32),
        name="plane_sum",
    )(parts)


def column_kernel(own_ref, near_ref, far_ref, both_ref, out_ref):
    powers = []
    for g in range(2):
        own, near, far, both = (
            ref[g].astype(jnp.float32) for ref in (own_ref, near_ref, far_ref, both_ref)
        )
        total = (own + near) + (far + both)
        power = exponent(jnp.max(jnp.abs(total), axis=0, keepdims=True))
        powers.append(power)
        code = to_int16(encode(total, power))
        for n in range(PARTS):
            out_ref[n, g * ROWS : (g + 1) * ROWS] = code
    tail = to_int16(jnp.concatenate(powers + [jnp.zeros((14, F), jnp.float32)], axis=0))
    for n in range(PARTS):
        out_ref[n, 2 * ROWS : 2 * ROWS + 16] = tail


def column_copies(*planes):
    vmem = pl.BlockSpec(memory_space=pltpu.VMEM)
    return pl.pallas_call(
        column_kernel,
        out_shape=jax.ShapeDtypeStruct((PARTS, 2 * ROWS + 16, F), jnp.int16),
        in_specs=[vmem] * 4,
        out_specs=vmem,
        compiler_params=params(mib=32),
        name="column_copies",
    )(*planes)


def finish_kernel(half_ref, code_ref, *refs):
    grad_in_ref, grad_out_ref = refs[-2:]
    for n in range(0, code_ref.shape[0], 2):
        at = slice(n * ROWS, (n + 2) * ROWS)
        both = []
        for m in (n, n + 1):
            code = to_float(code_ref[m])
            grad_in_ref[m * ROWS : (m + 1) * ROWS] = decode(
                code[0:ROWS], code[2 * ROWS : 2 * ROWS + 1]
            )
            both.append(decode(code[ROWS : 2 * ROWS], code[2 * ROWS + 1 : 2 * ROWS + 2]))
        grad_out_ref[:, at] = jnp.concatenate(both, axis=0).T


def finish_half(half, code, before=()):
    return pl.pallas_call(
        finish_kernel,
        grid_spec=pltpu.PrefetchScalarGridSpec(
            num_scalar_prefetch=1,
            grid=(2,),
            in_specs=[pl.BlockSpec((PARTS // 2, 2 * ROWS + 16, F), lambda i, half: (i, 0, 0))]
            + [pl.BlockSpec(memory_space=pl.ANY)] * len(before),
            out_specs=[
                pl.BlockSpec((1024, F), lambda i, half: (half[0] * 2 + i, 0)),
                pl.BlockSpec((F, 1024), lambda i, half: (0, half[0] * 2 + i)),
            ],
        ),
        out_shape=[
            jax.ShapeDtypeStruct((H, F), jnp.float32),
            jax.ShapeDtypeStruct((F, H), jnp.float32),
        ],
        input_output_aliases={2: 0, 3: 1} if before else {},
        compiler_params=params(("arbitrary",), 32),
        name="finish_half",
    )(half, code, *before)


def swap(value, axes):
    return lax.all_to_all(value, axes, split_axis=0, concat_axis=0, tiled=True)


def local(initial_states, targets, w_in, w_out, diffusivity, stiffness, land_mask, wet_levels, plan):
    core = lax.axis_index("core").astype(jnp.int32).reshape(1)
    meta = jnp.stack([lax.axis_index("sec"), lax.axis_index(TILE) % 8]).astype(jnp.int32)

    states = initial_states.reshape(MB, 2 * F, 128)
    msg = swap(init_slabs(meta, plan, states, land_mask, wet_levels), TILE)
    place = lambda half, chunk, col: (half * 8 + chunk) * 4 + col
    forward = [
        (place(h, j, c), place(h, (j + 1) % 8, c + (j + 1) // 8))
        for h in range(2)
        for j in range(8)
        for c in range(4)
        if c + (j + 1) // 8 < 4
    ]
    left = lax.ppermute(msg[:, 32:48], TILE + COL, forward)
    right = lax.ppermute(msg[:, 0:16], TILE + COL, [(b, a) for a, b in forward])

    target, w_in_t, w_out_t = prepare(targets.reshape(MB, 2 * F, 128), w_in, w_out, plan)
    target = swap(target.reshape(64, 2, CHUNK, F), ("sec",) + TILE).reshape(COLS, F)

    traj, inputs, tend, wet = rollout(meta, msg, left, right, w_in_t, w_out_t, diffusivity, stiffness)
    arrived = swap(traj.reshape(64, 2, CHUNK, F), ("sec",) + TILE)

    own = own_columns(
        inputs.reshape(COLS, F), tend.reshape(COLS, F), target, wet.reshape(OWN, F)
    )
    theirs = lax.ppermute(own, "core", [(0, 1), (1, 0)])
    pair = half_grads(core, theirs, w_in, w_out_t, half_grads(core, own, w_in, w_out_t))
    pair, arrived = lax.optimization_barrier((pair, arrived))

    trajectory = spread_trajectory(arrived.reshape(MB, 8, 2, CHUNK, F))
    plane = plane_sum(swap(pair, SPREAD))
    plane, trajectory = lax.optimization_barrier((plane, trajectory))
    others = [
        lax.ppermute(plane, ("zh", "c1"), [(i, i ^ n) for i in range(4)]) for n in range(1, 4)
    ]
    code = swap(column_copies(plane, *others), SPREAD)
    across = lax.ppermute(code, "core", [(0, 1), (1, 0)])
    grad_in, grad_out = finish_half(1 - core, across, finish_half(core, code))
    return (trajectory.reshape(1, MB, F, 2, 128), grad_in, grad_out)


def solution(mesh):
    fine = Mesh(mesh.devices.reshape(4, 2, 4, 2, 2, 2), ("sec", "zh", "cx", "core", "c1", "c0"))
    in_specs = (
        P(None, None, TILE, COL),
        P("sec", None, None, TILE, COL),
        P(),
        P(),
        P(),
        P(),
        P(TILE, COL),
        P(TILE, COL),
        P(),
    )
    out_specs = (P("sec", None, None, TILE, COL), P(), P())
    return jax.shard_map(local, mesh=fine, in_specs=in_specs, out_specs=out_specs, check_vma=False)
```

```python
import math

import jax
import jax.numpy as jnp
import numpy as np
from jax import lax
from jax.experimental import pallas as pl
from jax.experimental.pallas import tpu as pltpu
from jax.sharding import Mesh, PartitionSpec as P

V = 8
L = 16
H = 4096
F = 128
STEPS = 4
MB = 8
NX = 32
NY = 512
CHUNK = 16
HALO = STEPS
SLAB = CHUNK + 2 * HALO
MSG = 48
CODE = 32000.0
UNIT = 32768.0 / CODE
OWN = NX * CHUNK
COLS = STEPS * OWN
HB1 = 2048
HB2 = 1024
WIDE = 512
STRIP = 32
HALF = H // 2
GRAD_SCALE = 1.0 / math.sqrt(MB * STEPS * NX * NY)
TILE = ("zh", "cx", "core")
COL = ("c1", "c0")
SPREAD = ("sec", "cx", "c0")
PARTS = 32
ROWS = H // 2 // PARTS


def mode_block():
    order = np.arange(L)
    angles = np.pi * (order[None, :] + 0.5) * order[:, None] / L
    weights = np.where(order[:, None] == 0, math.sqrt(1.0 / L), math.sqrt(2.0 / L))
    return np.kron(np.eye(V), np.cos(angles) * weights)


def split_table(matrix):
    high = matrix.astype(jnp.bfloat16)
    low = (matrix - high.astype(np.float64)).astype(jnp.bfloat16)
    return np.concatenate([high, high, low], axis=0)


def params(semantics=None, mib=60):
    return pltpu.CompilerParams(dimension_semantics=semantics, vmem_limit_bytes=mib * 2**20)


def exponent(largest):
    return jnp.ceil(jnp.log(jnp.maximum(largest, 1e-30)) * (1.0 / math.log(2.0)) + 0.01)


def encode(value, power):
    scaled = value * (jnp.exp2(15.0 - power) * (1.0 / UNIT))
    return jnp.round(jnp.clip(scaled, -32767.0, 32767.0))


def to_int16(value):
    return value.astype(jnp.int32).astype(jnp.int16)


def to_float(code):
    return code.astype(jnp.int32).astype(jnp.float32)


def decode(value, power):
    return value * (jnp.exp2(power - 15.0) * UNIT)


def init_kernel(meta_ref, plan_ref, state_ref, land_ref, levels_ref, msg_ref):
    power = exponent(jnp.max(jnp.abs(state_ref[0]), keepdims=True))
    code = [encode(state_ref[0, pl.ds(x, F, stride=2), :], power).T for x in range(2)]
    depth = jnp.where(land_ref[...] == 1, levels_ref[...], 0).astype(jnp.float32)
    extra = jnp.concatenate(
        [depth, jnp.broadcast_to(power, (1, 128)), jnp.zeros((5, 128), jnp.float32)], axis=0
    )
    for j in range(8):
        y = CHUNK * j
        first = [c[y : y + HALO] for c in code]
        middle = [c[y + HALO : y + CHUNK - HALO] for c in code]
        last = [c[y + CHUNK - HALO : y + CHUNK] for c in code]
        msg_ref[j] = to_int16(jnp.concatenate(first + [extra] + middle + last + [extra], axis=0))


def init_slabs(meta, plan, states, land_mask, wet_levels):
    whole = lambda i, meta, plan: (0, 0)
    return pl.pallas_call(
        init_kernel,
        grid_spec=pltpu.PrefetchScalarGridSpec(
            num_scalar_prefetch=2,
            grid=(2,),
            in_specs=[
                pl.BlockSpec((1, 2 * F, 128), lambda i, meta, plan: (plan[2 * meta[0] + i], 0, 0)),
                pl.BlockSpec((2, 128), whole),
                pl.BlockSpec((2, 128), whole),
            ],
            out_specs=pl.BlockSpec((8, MSG, F), lambda i, meta, plan: (i, 0, 0)),
        ),
        out_shape=jax.ShapeDtypeStruct((16, MSG, F), jnp.int16),
        compiler_params=params(("arbitrary",)),
        name="init_slabs",
    )(meta, plan, states, land_mask, wet_levels)


def levels():
    return (lax.broadcasted_iota(jnp.int32, (1, F), 1) % L).astype(jnp.float32)


def pack_halo(halo, step):
    if step == STEPS - 1:
        return jnp.zeros((0, F), jnp.float32)
    share = (1, 2, 4)[step]
    halo = halo.reshape(NX // share, share, 8, F)
    packed = halo[:, 0]
    row = lax.broadcasted_iota(jnp.int32, packed.shape, 1)
    for n in range(1, share):
        shift = n * 8 // share
        keep = STEPS - 1 - step
        place = (row + (8 - shift) + keep) % 8 < 2 * keep
        packed = jnp.where(place, pltpu.roll(halo[:, n], shift, 1), packed)
    return packed.reshape(NX // share * 8, F)


def unpack_halo(packed, step):
    share = (1, 2, 4)[step]
    packed = packed.reshape(NX // share, 8, F)
    parts = [packed] + [pltpu.roll(packed, 8 - n * 8 // share, 1) for n in range(1, share)]
    return jnp.stack(parts, axis=1).reshape(NX, 8, F)


def rollout_kernel(
    meta_ref, msg_ref, left_ref, right_ref, w_in_t, w_out_t, mode_ref, mode_t, diff_ref, stiff_ref,
    traj_ref, inputs_ref, tend_ref, own_wet_ref,
    state, wet, modal, acc, x_scr, gain, pull, depth, depth_t, before, hidden, split,
):
    for t in range(16):
        for n, (ref, base) in enumerate(
            ((msg_ref, 0), (msg_ref, 16), (msg_ref, 32), (right_ref, 0), (left_ref, 0))
        ):
            piece = to_float(ref[t, base : base + 16])
            if n != 1:
                scale = decode(1.0, piece[10:11])
            rows = 8 if n == 1 else HALO
            at = (0, HALO, CHUNK - HALO, CHUNK, CHUNK + HALO)[n]
            for x in range(2):
                state[2 * t + x, at : at + rows] = piece[x * rows : (x + 1) * rows] * scale
            if n in (0, 3, 4):
                depth[n // 2 if n else 0, 2 * t : 2 * t + 2] = piece[8:10]
    for n in range(3):
        depth_t[n] = depth[n].T
    mine = meta_ref[1]
    y_own = pl.multiple_of(mine * CHUNK, CHUNK)
    y_right = pl.multiple_of(lax.rem(mine + 1, 8) * CHUNK, CHUNK)
    y_left = pl.multiple_of(lax.rem(mine + 7, 8) * CHUNK + 8, 8)
    here = jnp.concatenate(
        [
            depth_t[0, pl.ds(y_own, CHUNK)],
            depth_t[1, pl.ds(y_right, 8)][:HALO],
            depth_t[2, pl.ds(y_left, 8)][8 - HALO :],
        ],
        axis=0,
    )
    level = levels()
    for x in range(NX):
        wet[x] = jnp.where(level < here[:, x : x + 1], 1.0, 0.0)
    own_wet_ref[...] = wet[:, :CHUNK]

    a = stiff_ref[...]
    u = 1.0 + a
    for i in range(NX):
        r = 1.0 / (a + u)
        gain[pl.ds(i, 1), :] = r
        pull[pl.ds(i, 1), :] = a * r
        u = 1.0 + a * (u * r)
    diff = diff_ref[...]

    def put_split(x, value):
        at = slice(x * SLAB, (x + 2) * SLAB)
        high = value.astype(jnp.bfloat16)
        split[at, 0:F] = high
        split[at, F : 2 * F] = (value - high.astype(jnp.float32)).astype(jnp.bfloat16)

    def transform(table):
        return jnp.dot(
            split[...], table[0 : 2 * F], preferred_element_type=jnp.float32
        ) + jnp.dot(split[:, 0:F], table[2 * F :], preferred_element_type=jnp.float32)

    for step in range(STEPS):
        for x in range(0, NX, 2):
            pieces = []
            for at in (x, x + 1):
                here = state[at]
                around = pltpu.roll(here, 1, 0) + pltpu.roll(here, SLAB - 1, 0) - 4.0 * here
                if at > 0:
                    around += state[at - 1]
                if at < NX - 1:
                    around += state[at + 1]
                pieces.append(wet[at] * (here + diff * around))
            put_split(x, jnp.concatenate(pieces, axis=0))
        modal[...] = transform(mode_t).reshape(NX, SLAB, F)
        part = modal[0] * gain[pl.ds(0, 1), :]
        modal[0] = part
        for i in range(1, NX):
            part = modal[i] * gain[pl.ds(i, 1), :] + pull[pl.ds(i, 1), :] * part
            modal[i] = part
        for i in range(NX - 2, -1, -1):
            behind = part
            part = modal[i] + pull[pl.ds(i, 1), :] * part
            if i % 2 == 0:
                put_split(i, jnp.concatenate([part, behind], axis=0))
        after = wet[...] * transform(mode_ref).reshape(NX, SLAB, F)
        inputs_ref[step] = after[:, :CHUNK].astype(jnp.bfloat16)
        extra = pack_halo(after[:, CHUNK:], step)
        count = OWN + extra.shape[0]
        state[...] = after
        x_scr[0:OWN] = after[:, :CHUNK].reshape(OWN, F).astype(jnp.bfloat16)
        if step < STEPS - 1:
            x_scr[OWN:count] = extra.astype(jnp.bfloat16)
        acc[0:count] = jnp.zeros((count, F), jnp.float32)

        def block(b, carry, n=count):
            def front(i):
                at = pl.multiple_of(b * HB1 + i * WIDE, WIDE)
                before[i % 2, 0:n] = jnp.dot(
                    x_scr[0:n], w_in_t[:, pl.ds(at, WIDE)], preferred_element_type=jnp.float32
                )
                return at

            at = front(0)
            for i in range(HB1 // WIDE):
                following = front(i + 1) if i + 1 < HB1 // WIDE else None
                for r in range(0, n, STRIP):
                    strip = jnp.tanh(before[i % 2, r : r + STRIP])
                    hidden[i % 2, r : r + STRIP] = strip.astype(jnp.bfloat16)
                acc[0:n] += jnp.dot(
                    hidden[i % 2, 0:n],
                    w_out_t[pl.ds(at, WIDE), :],
                    preferred_element_type=jnp.float32,
                )
                at = following
            return carry

        lax.fori_loop(0, H // HB1, block, 0)
        tendency = acc[0:OWN].reshape(NX, CHUNK, F)
        result = wet[:, :CHUNK] * (state[:, :CHUNK] + tendency)
        traj_ref[step] = result.astype(jnp.bfloat16)
        tend_ref[step] = tendency
        if step < STEPS - 1:
            beside = unpack_halo(acc[OWN:count], step)
            state[:, CHUNK:] = wet[:, CHUNK:] * (state[:, CHUNK:] + beside)
            state[:, :CHUNK] = result


def rollout(meta, msg, left, right, w_in_t, w_out_t, diffusivity, stiffness):
    block = mode_block()
    vmem = pl.BlockSpec(memory_space=pltpu.VMEM)
    return pl.pallas_call(
        rollout_kernel,
        out_shape=[
            jax.ShapeDtypeStruct((STEPS, NX, CHUNK, F), jnp.bfloat16),
            jax.ShapeDtypeStruct((STEPS, NX, CHUNK, F), jnp.bfloat16),
            jax.ShapeDtypeStruct((STEPS, NX, CHUNK, F), jnp.float32),
            jax.ShapeDtypeStruct((NX, CHUNK, F), jnp.float32),
        ],
        in_specs=[pl.BlockSpec(memory_space=pltpu.SMEM)] + [vmem] * 9,
        out_specs=[vmem] * 4,
        scratch_shapes=[
            pltpu.VMEM((NX, SLAB, F), jnp.float32),
            pltpu.VMEM((NX, SLAB, F), jnp.float32),
            pltpu.VMEM((NX, SLAB, F), jnp.float32),
            pltpu.VMEM((NX * SLAB, F), jnp.float32),
            pltpu.VMEM((NX * SLAB, F), jnp.bfloat16),
            pltpu.VMEM((NX, F), jnp.float32),
            pltpu.VMEM((NX, F), jnp.float32),
            pltpu.VMEM((3, NX, 128), jnp.float32),
            pltpu.VMEM((3, 128, NX), jnp.float32),
            pltpu.VMEM((2, NX * SLAB, WIDE), jnp.float32),
            pltpu.VMEM((2, NX * SLAB, WIDE), jnp.bfloat16),
            pltpu.VMEM((NX * SLAB, 2 * F), jnp.bfloat16),
        ],
        compiler_params=params(),
        cost_estimate=pl.CostEstimate(
            flops=4 * 2816 * F * H, bytes_accessed=6 * 2**20, transcendentals=2816 * H
        ),
        name="rollout",
    )(
        meta,
        msg,
        left,
        right,
        w_in_t,
        w_out_t,
        jnp.asarray(split_table(block)),
        jnp.asarray(split_table(block.T)),
        diffusivity.reshape(1, F),
        stiffness.reshape(1, F),
    )


def prepare_kernel(plan_ref, target_ref, w_in_ref, w_out_ref, out_ref, w_in_t, w_out_t, wide):
    wide[...] = target_ref[0].astype(jnp.float32)
    for x in range(2):
        t = wide[pl.ds(x, F, stride=2), :].T
        out_ref[0, :, x] = t.reshape(8, CHUNK, F).astype(jnp.bfloat16)
    w_in_t[...] = w_in_ref[...].T
    w_out_t[...] = w_out_ref[...].T


def prepare(targets, w_in, w_out, plan):
    part = H // MB
    down = lambda i, plan: (i, 0)
    along = lambda i, plan: (0, i)
    return pl.pallas_call(
        prepare_kernel,
        grid_spec=pltpu.PrefetchScalarGridSpec(
            num_scalar_prefetch=1,
            grid=(MB,),
            in_specs=[
                pl.BlockSpec((1, 2 * F, 128), lambda i, plan: (plan[i], 0, 0)),
                pl.BlockSpec((part, F), down),
                pl.BlockSpec((F, part), along),
            ],
            out_specs=[
                pl.BlockSpec((1, 8, 2, CHUNK, F), lambda i, plan: (i, 0, 0, 0, 0)),
                pl.BlockSpec((F, part), along),
                pl.BlockSpec((part, F), down),
            ],
            scratch_shapes=[pltpu.VMEM((2 * F, 128), jnp.float32)],
        ),
        out_shape=[
            jax.ShapeDtypeStruct((MB, 8, 2, CHUNK, F), jnp.bfloat16),
            jax.ShapeDtypeStruct((F, H), jnp.bfloat16),
            jax.ShapeDtypeStruct((H, F), jnp.bfloat16),
        ],
        compiler_params=params(),
        cost_estimate=pl.CostEstimate(flops=0, bytes_accessed=6 * 2**20, transcendentals=0),
        name="prepare",
    )(plan, targets, w_in, w_out)


def spread_kernel(in_ref, out_ref):
    for x in range(2):
        block = in_ref[0, :, x].astype(jnp.float32).reshape(128, F)
        out_ref[0, pl.ds(x, F, stride=2), :] = block.T


def spread_trajectory(arrived):
    return pl.pallas_call(
        spread_kernel,
        grid=(MB,),
        in_specs=[pl.BlockSpec((1, 8, 2, CHUNK, F), lambda i: (i, 0, 0, 0, 0))],
        out_specs=pl.BlockSpec((1, 2 * F, 128), lambda i: (i, 0, 0)),
        out_shape=jax.ShapeDtypeStruct((MB, 2 * F, 128), jnp.float32),
        compiler_params=params(),
        name="spread_trajectory",
    )(arrived)


def grad_block(x_ref, x_t, misfit, misfit_t, w_in_ref, w_out_t_ref, scratch):
    before, back, hidden, change = scratch
    rows = w_in_ref.shape[0]

    def front(part):
        at = slice(part * WIDE, (part + 1) * WIDE)
        before[part % 2] = jnp.dot(w_in_ref[...], x_t[:, at], preferred_element_type=jnp.float32)
        back[part % 2] = jnp.dot(
            w_out_t_ref[...], misfit_t[:, at], preferred_element_type=jnp.float32
        )
        return at

    grad_in = jnp.zeros((rows, F), jnp.float32)
    grad_out = jnp.zeros((rows, F), jnp.float32)
    at = front(0)
    for part in range(COLS // WIDE):
        following = front(part + 1) if part + 1 < COLS // WIDE else None
        n = part % 2
        for r in range(0, rows, STRIP):
            strip = jnp.tanh(before[n, r : r + STRIP])
            hidden[n, r : r + STRIP] = strip.astype(jnp.bfloat16)
            strip = back[n, r : r + STRIP] * (1.0 - strip * strip)
            change[n, r : r + STRIP] = strip.astype(jnp.bfloat16)
        grad_out += jnp.dot(hidden[n], misfit[at], preferred_element_type=jnp.float32)
        grad_in += jnp.dot(change[n], x_ref[at], preferred_element_type=jnp.float32)
        at = following
    shape = (rows // ROWS, ROWS, F)
    return grad_in.reshape(shape), grad_out.reshape(shape)


def columns_kernel(x_ref, tend_ref, target_ref, wet_ref, out_ref):
    for r in range(0, COLS, 64):
        at = slice(r, r + 64)
        gap = tend_ref[at] - target_ref[at].astype(jnp.float32)
        gap = wet_ref[r % OWN : r % OWN + 64] * gap * GRAD_SCALE
        out_ref[0, at] = x_ref[at]
        out_ref[1, at] = gap.astype(jnp.bfloat16)


def own_columns(inputs, tend, target, wet):
    return pl.pallas_call(
        columns_kernel,
        out_shape=jax.ShapeDtypeStruct((2, COLS, F), jnp.bfloat16),
        in_specs=[pl.BlockSpec(memory_space=pltpu.VMEM)] * 4,
        out_specs=pl.BlockSpec(memory_space=pltpu.VMEM),
        compiler_params=params(),
        name="own_columns",
    )(inputs, tend, target, wet)


def grad_kernel(half_ref, columns_ref, w_in_ref, w_out_ref, *refs):
    *add_ref, out_ref, x_t, misfit_t, before, back, hidden, change = refs

    @pl.when(pl.program_id(0) == 0)
    def _():
        for part in range(STEPS):
            at = slice(part * OWN, (part + 1) * OWN)
            x_t[:, at] = columns_ref[0, at].T
            misfit_t[:, at] = columns_ref[1, at].T

    grads = grad_block(
        columns_ref.at[0],
        x_t,
        columns_ref.at[1],
        misfit_t,
        w_in_ref,
        w_out_ref,
        (before, back, hidden, change),
    )
    for n, grad in enumerate(grads):
        if add_ref:
            grad = grad + add_ref[0][:, n]
        out_ref[:, n] = grad.astype(out_ref.dtype)


def half_grads(half, columns, w_in, w_out_t, add=None):
    blocks = HALF // HB2
    weight = pl.BlockSpec((HB2, F), lambda i, half: (half[0] * blocks + i, 0))
    rows = pl.BlockSpec((HB2 // ROWS, 2, ROWS, F), lambda i, half: (i, 0, 0, 0))
    first = add is None
    return pl.pallas_call(
        grad_kernel,
        grid_spec=pltpu.PrefetchScalarGridSpec(
            num_scalar_prefetch=1,
            grid=(blocks,),
            in_specs=[pl.BlockSpec((2, COLS, F), lambda i, half: (0, 0, 0)), weight, weight]
            + ([] if first else [rows]),
            out_specs=rows,
            scratch_shapes=[pltpu.VMEM((F, COLS), jnp.bfloat16)] * 2
            + [pltpu.VMEM((2, HB2, WIDE), jnp.float32)] * 2
            + [pltpu.VMEM((2, HB2, WIDE), jnp.bfloat16)] * 2,
        ),
        out_shape=jax.ShapeDtypeStruct(
            (PARTS, 2, ROWS, F), jnp.float32 if first else jnp.bfloat16
        ),
        compiler_params=params(("arbitrary",)),
        cost_estimate=pl.CostEstimate(flops=10**8, bytes_accessed=2**20, transcendentals=0),
        name="first_grads" if first else "second_grads",
    )(half, columns, w_in, w_out_t, *(() if first else (add,)))


def plane_kernel(in_ref, out_ref):
    total = in_ref[0].astype(jnp.float32)
    for n in range(1, PARTS):
        total += in_ref[n].astype(jnp.float32)
    out_ref[...] = total.astype(jnp.bfloat16)


def plane_sum(parts):
    vmem = pl.BlockSpec(memory_space=pltpu.VMEM)
    return pl.pallas_call(
        plane_kernel,
        out_shape=jax.ShapeDtypeStruct((2, ROWS, F), jnp.bfloat16),
        in_specs=[vmem],
        out_specs=vmem,
        compiler_params=params(mib=32),
        name="plane_sum",
    )(parts)


def column_kernel(own_ref, near_ref, far_ref, both_ref, out_ref):
    powers = []
    for g in range(2):
        own, near, far, both = (
            ref[g].astype(jnp.float32) for ref in (own_ref, near_ref, far_ref, both_ref)
        )
        total = (own + near) + (far + both)
        power = exponent(jnp.max(jnp.abs(total), axis=0, keepdims=True))
        powers.append(power)
        code = to_int16(encode(total, power))
        for n in range(PARTS):
            out_ref[n, g * ROWS : (g + 1) * ROWS] = code
    tail = to_int16(jnp.concatenate(powers + [jnp.zeros((14, F), jnp.float32)], axis=0))
    for n in range(PARTS):
        out_ref[n, 2 * ROWS : 2 * ROWS + 16] = tail


def column_copies(*planes):
    vmem = pl.BlockSpec(memory_space=pltpu.VMEM)
    return pl.pallas_call(
        column_kernel,
        out_shape=jax.ShapeDtypeStruct((PARTS, 2 * ROWS + 16, F), jnp.int16),
        in_specs=[vmem] * 4,
        out_specs=vmem,
        compiler_params=params(mib=32),
        name="column_copies",
    )(*planes)


def finish_kernel(half_ref, code_ref, *refs):
    grad_in_ref, grad_out_ref = refs[-2:]
    for n in range(0, code_ref.shape[0], 2):
        at = slice(n * ROWS, (n + 2) * ROWS)
        both = []
        for m in (n, n + 1):
            code = to_float(code_ref[m])
            grad_in_ref[m * ROWS : (m + 1) * ROWS] = decode(
                code[0:ROWS], code[2 * ROWS : 2 * ROWS + 1]
            )
            both.append(decode(code[ROWS : 2 * ROWS], code[2 * ROWS + 1 : 2 * ROWS + 2]))
        grad_out_ref[:, at] = jnp.concatenate(both, axis=0).T


def finish_half(half, code, before=()):
    return pl.pallas_call(
        finish_kernel,
        grid_spec=pltpu.PrefetchScalarGridSpec(
            num_scalar_prefetch=1,
            grid=(2,),
            in_specs=[pl.BlockSpec((PARTS // 2, 2 * ROWS + 16, F), lambda i, half: (i, 0, 0))]
            + [pl.BlockSpec(memory_space=pl.ANY)] * len(before),
            out_specs=[
                pl.BlockSpec((1024, F), lambda i, half: (half[0] * 2 + i, 0)),
                pl.BlockSpec((F, 1024), lambda i, half: (0, half[0] * 2 + i)),
            ],
        ),
        out_shape=[
            jax.ShapeDtypeStruct((H, F), jnp.float32),
            jax.ShapeDtypeStruct((F, H), jnp.float32),
        ],
        input_output_aliases={2: 0, 3: 1} if before else {},
        compiler_params=params(("arbitrary",), 32),
        name="finish_half",
    )(half, code, *before)


def swap(value, axes):
    return lax.all_to_all(value, axes, split_axis=0, concat_axis=0, tiled=True)


def local(initial_states, targets, w_in, w_out, diffusivity, stiffness, land_mask, wet_levels, plan):
    core = lax.axis_index("core").astype(jnp.int32).reshape(1)
    meta = jnp.stack([lax.axis_index("sec"), lax.axis_index(TILE) % 8]).astype(jnp.int32)

    states = initial_states.reshape(MB, 2 * F, 128)
    msg = swap(init_slabs(meta, plan, states, land_mask, wet_levels), TILE)
    place = lambda half, chunk, col: (half * 8 + chunk) * 4 + col
    forward = [
        (place(h, j, c), place(h, (j + 1) % 8, c + (j + 1) // 8))
        for h in range(2)
        for j in range(8)
        for c in range(4)
        if c + (j + 1) // 8 < 4
    ]
    target, w_in_t, w_out_t = prepare(targets.reshape(MB, 2 * F, 128), w_in, w_out, plan)
    last, first, target = lax.optimization_barrier((msg[:, 32:48], msg[:, 0:16], target))
    left = lax.ppermute(last, TILE + COL, forward)
    right = lax.ppermute(first, TILE + COL, [(b, a) for a, b in forward])
    left, right, target = lax.optimization_barrier((left, right, target))
    target = swap(target.reshape(64, 2, CHUNK, F), ("sec",) + TILE).reshape(COLS, F)

    traj, inputs, tend, wet = rollout(meta, msg, left, right, w_in_t, w_out_t, diffusivity, stiffness)
    arrived = swap(traj.reshape(64, 2, CHUNK, F), ("sec",) + TILE)

    own = own_columns(
        inputs.reshape(COLS, F), tend.reshape(COLS, F), target, wet.reshape(OWN, F)
    )
    theirs = lax.ppermute(own, "core", [(0, 1), (1, 0)])
    pair = half_grads(core, theirs, w_in, w_out_t, half_grads(core, own, w_in, w_out_t))
    pair, arrived = lax.optimization_barrier((pair, arrived))

    trajectory = spread_trajectory(arrived.reshape(MB, 8, 2, CHUNK, F))
    plane = plane_sum(swap(pair, SPREAD))
    plane, trajectory = lax.optimization_barrier((plane, trajectory))
    others = [
        lax.ppermute(plane, ("zh", "c1"), [(i, i ^ n) for i in range(4)]) for n in range(1, 4)
    ]
    code = swap(column_copies(plane, *others), SPREAD)
    across = lax.ppermute(code, "core", [(0, 1), (1, 0)])
    grad_in, grad_out = finish_half(1 - core, across, finish_half(core, code))
    return (trajectory.reshape(1, MB, F, 2, 128), grad_in, grad_out)


def solution(mesh):
    fine = Mesh(mesh.devices.reshape(4, 2, 4, 2, 2, 2), ("sec", "zh", "cx", "core", "c1", "c0"))
    in_specs = (
        P(None, None, TILE, COL),
        P("sec", None, None, TILE, COL),
        P(),
        P(),
        P(),
        P(),
        P(TILE, COL),
        P(TILE, COL),
        P(),
    )
    out_specs = (P("sec", None, None, TILE, COL), P(), P())
    return jax.shard_map(local, mesh=fine, in_specs=in_specs, out_specs=out_specs, check_vma=False)
```

```python
import math

import jax
import jax.numpy as jnp
import numpy as np
from jax import lax
from jax.experimental import pallas as pl
from jax.experimental.pallas import tpu as pltpu
from jax.sharding import Mesh, PartitionSpec as P

V = 8
L = 16
H = 4096
F = 128
STEPS = 4
MB = 8
NX = 32
NY = 512
CHUNK = 16
HALO = STEPS
SLAB = CHUNK + 2 * HALO
MSG = 48
CODE = 32000.0
UNIT = 32768.0 / CODE
OWN = NX * CHUNK
COLS = STEPS * OWN
HB1 = 2048
HB2 = 1024
WIDE = 512
STRIP = 32
HALF = H // 2
GRAD_SCALE = 1.0 / math.sqrt(MB * STEPS * NX * NY)
TILE = ("zh", "cx", "core")
COL = ("c1", "c0")
SPREAD = ("sec", "cx", "c0")
PARTS = 32
ROWS = H // 2 // PARTS


def mode_block():
    order = np.arange(L)
    angles = np.pi * (order[None, :] + 0.5) * order[:, None] / L
    weights = np.where(order[:, None] == 0, math.sqrt(1.0 / L), math.sqrt(2.0 / L))
    return np.kron(np.eye(V), np.cos(angles) * weights)


def split_table(matrix):
    high = matrix.astype(jnp.bfloat16)
    low = (matrix - high.astype(np.float64)).astype(jnp.bfloat16)
    return np.concatenate([high, high, low], axis=0)


def params(semantics=None, mib=60):
    return pltpu.CompilerParams(dimension_semantics=semantics, vmem_limit_bytes=mib * 2**20)


def exponent(largest):
    return jnp.ceil(jnp.log(jnp.maximum(largest, 1e-30)) * (1.0 / math.log(2.0)) + 0.01)


def encode(value, power):
    scaled = value * (jnp.exp2(15.0 - power) * (1.0 / UNIT))
    return jnp.round(jnp.clip(scaled, -32767.0, 32767.0))


def to_int16(value):
    return value.astype(jnp.int32).astype(jnp.int16)


def to_float(code):
    return code.astype(jnp.int32).astype(jnp.float32)


def decode(value, power):
    return value * (jnp.exp2(power - 15.0) * UNIT)


def init_kernel(section_ref, plan_ref, state_ref, land_ref, levels_ref, msg_ref):
    power = exponent(jnp.max(jnp.abs(state_ref[0]), keepdims=True))
    code = [encode(state_ref[0, pl.ds(x, F, stride=2), :], power).T for x in range(2)]
    depth = jnp.where(land_ref[...] == 1, levels_ref[...], 0).astype(jnp.float32)
    extra = jnp.concatenate(
        [depth, jnp.broadcast_to(power, (1, 128)), jnp.zeros((5, 128), jnp.float32)], axis=0
    )
    for j in range(8):
        y = CHUNK * j
        first = [c[y : y + HALO] for c in code]
        middle = [c[y + HALO : y + CHUNK - HALO] for c in code]
        last = [c[y + CHUNK - HALO : y + CHUNK] for c in code]
        msg_ref[j] = to_int16(jnp.concatenate(first + [extra] + middle + last + [extra], axis=0))


def init_slabs(section, plan, states, land_mask, wet_levels):
    whole = lambda i, sec, plan: (0, 0)
    return pl.pallas_call(
        init_kernel,
        grid_spec=pltpu.PrefetchScalarGridSpec(
            num_scalar_prefetch=2,
            grid=(2,),
            in_specs=[
                pl.BlockSpec((1, 2 * F, 128), lambda i, sec, plan: (plan[2 * sec[0] + i], 0, 0)),
                pl.BlockSpec((2, 128), whole),
                pl.BlockSpec((2, 128), whole),
            ],
            out_specs=pl.BlockSpec((8, MSG, F), lambda i, sec, plan: (i, 0, 0)),
        ),
        out_shape=jax.ShapeDtypeStruct((16, MSG, F), jnp.int16),
        compiler_params=params(("arbitrary",)),
        name="init_slabs",
    )(section, plan, states, land_mask, wet_levels)


def levels():
    return (lax.broadcasted_iota(jnp.int32, (1, F), 1) % L).astype(jnp.float32)


def pack_halo(halo, step):
    if step == STEPS - 1:
        return jnp.zeros((0, F), jnp.float32)
    share = (1, 2, 4)[step]
    halo = halo.reshape(NX // share, share, 8, F)
    packed = halo[:, 0]
    row = lax.broadcasted_iota(jnp.int32, packed.shape, 1)
    for n in range(1, share):
        shift = n * 8 // share
        keep = STEPS - 1 - step
        place = (row + (8 - shift) + keep) % 8 < 2 * keep
        packed = jnp.where(place, pltpu.roll(halo[:, n], shift, 1), packed)
    return packed.reshape(NX // share * 8, F)


def unpack_halo(packed, step):
    share = (1, 2, 4)[step]
    packed = packed.reshape(NX // share, 8, F)
    parts = [packed] + [pltpu.roll(packed, 8 - n * 8 // share, 1) for n in range(1, share)]
    return jnp.stack(parts, axis=1).reshape(NX, 8, F)


def rollout_kernel(
    chunk_ref, msg_ref, left_ref, right_ref, w_in_t, w_out_t, mode_ref, mode_t, diff_ref, stiff_ref,
    traj_ref, inputs_ref, tend_ref, own_wet_ref,
    state, wet, modal, acc, x_scr, gain, pull, depth, depth_t, before, hidden, split,
):
    for t in range(16):
        for n, (ref, base) in enumerate(
            ((msg_ref, 0), (msg_ref, 16), (msg_ref, 32), (right_ref, 0), (left_ref, 0))
        ):
            piece = to_float(ref[t, base : base + 16])
            if n != 1:
                scale = decode(1.0, piece[10:11])
            rows = 8 if n == 1 else HALO
            at = (0, HALO, CHUNK - HALO, CHUNK, CHUNK + HALO)[n]
            for x in range(2):
                state[2 * t + x, at : at + rows] = piece[x * rows : (x + 1) * rows] * scale
            if n in (0, 3, 4):
                depth[n // 2 if n else 0, 2 * t : 2 * t + 2] = piece[8:10]
    for n in range(3):
        depth_t[n] = depth[n].T
    mine = chunk_ref[0]
    y_own = pl.multiple_of(mine * CHUNK, CHUNK)
    y_right = pl.multiple_of(lax.rem(mine + 1, 8) * CHUNK, CHUNK)
    y_left = pl.multiple_of(lax.rem(mine + 7, 8) * CHUNK + 8, 8)
    here = jnp.concatenate(
        [
            depth_t[0, pl.ds(y_own, CHUNK)],
            depth_t[1, pl.ds(y_right, 8)][:HALO],
            depth_t[2, pl.ds(y_left, 8)][8 - HALO :],
        ],
        axis=0,
    )
    level = levels()
    for x in range(NX):
        wet[x] = jnp.where(level < here[:, x : x + 1], 1.0, 0.0)
    own_wet_ref[...] = wet[:, :CHUNK]

    a = stiff_ref[...]
    u = 1.0 + a
    for i in range(NX):
        r = 1.0 / (a + u)
        gain[pl.ds(i, 1), :] = r
        pull[pl.ds(i, 1), :] = a * r
        u = 1.0 + a * (u * r)
    diff = diff_ref[...]

    def put_split(x, value):
        at = slice(x * SLAB, (x + 2) * SLAB)
        high = value.astype(jnp.bfloat16)
        split[at, 0:F] = high
        split[at, F : 2 * F] = (value - high.astype(jnp.float32)).astype(jnp.bfloat16)

    def transform(table):
        return jnp.dot(
            split[...], table[0 : 2 * F], preferred_element_type=jnp.float32
        ) + jnp.dot(split[:, 0:F], table[2 * F :], preferred_element_type=jnp.float32)

    for step in range(STEPS):
        for x in range(0, NX, 2):
            pieces = []
            for at in (x, x + 1):
                here = state[at]
                around = pltpu.roll(here, 1, 0) + pltpu.roll(here, SLAB - 1, 0) - 4.0 * here
                if at > 0:
                    around += state[at - 1]
                if at < NX - 1:
                    around += state[at + 1]
                pieces.append(wet[at] * (here + diff * around))
            put_split(x, jnp.concatenate(pieces, axis=0))
        modal[...] = transform(mode_t).reshape(NX, SLAB, F)
        part = modal[0] * gain[pl.ds(0, 1), :]
        modal[0] = part
        for i in range(1, NX):
            part = modal[i] * gain[pl.ds(i, 1), :] + pull[pl.ds(i, 1), :] * part
            modal[i] = part
        for i in range(NX - 2, -1, -1):
            behind = part
            part = modal[i] + pull[pl.ds(i, 1), :] * part
            if i % 2 == 0:
                put_split(i, jnp.concatenate([part, behind], axis=0))
        after = wet[...] * transform(mode_ref).reshape(NX, SLAB, F)
        inputs_ref[step] = after[:, :CHUNK].astype(jnp.bfloat16)
        extra = pack_halo(after[:, CHUNK:], step)
        count = OWN + extra.shape[0]
        state[...] = after
        x_scr[0:OWN] = after[:, :CHUNK].reshape(OWN, F).astype(jnp.bfloat16)
        if step < STEPS - 1:
            x_scr[OWN:count] = extra.astype(jnp.bfloat16)
        acc[0:count] = jnp.zeros((count, F), jnp.float32)

        def block(b, carry, n=count):
            def front(i):
                at = pl.multiple_of(b * HB1 + i * WIDE, WIDE)
                before[i % 2, 0:n] = jnp.dot(
                    x_scr[0:n], w_in_t[:, pl.ds(at, WIDE)], preferred_element_type=jnp.float32
                )
                return at

            at = front(0)
            for i in range(HB1 // WIDE):
                following = front(i + 1) if i + 1 < HB1 // WIDE else None
                for r in range(0, n, STRIP):
                    strip = jnp.tanh(before[i % 2, r : r + STRIP])
                    hidden[i % 2, r : r + STRIP] = strip.astype(jnp.bfloat16)
                acc[0:n] += jnp.dot(
                    hidden[i % 2, 0:n],
                    w_out_t[pl.ds(at, WIDE), :],
                    preferred_element_type=jnp.float32,
                )
                at = following
            return carry

        lax.fori_loop(0, H // HB1, block, 0)
        tendency = acc[0:OWN].reshape(NX, CHUNK, F)
        result = wet[:, :CHUNK] * (state[:, :CHUNK] + tendency)
        traj_ref[step] = result.astype(jnp.bfloat16)
        tend_ref[step] = tendency
        if step < STEPS - 1:
            beside = unpack_halo(acc[OWN:count], step)
            state[:, CHUNK:] = wet[:, CHUNK:] * (state[:, CHUNK:] + beside)
            state[:, :CHUNK] = result


def rollout(chunk, msg, left, right, w_in_t, w_out_t, diffusivity, stiffness):
    block = mode_block()
    vmem = pl.BlockSpec(memory_space=pltpu.VMEM)
    return pl.pallas_call(
        rollout_kernel,
        out_shape=[
            jax.ShapeDtypeStruct((STEPS, NX, CHUNK, F), jnp.bfloat16),
            jax.ShapeDtypeStruct((STEPS, NX, CHUNK, F), jnp.bfloat16),
            jax.ShapeDtypeStruct((STEPS, NX, CHUNK, F), jnp.float32),
            jax.ShapeDtypeStruct((NX, CHUNK, F), jnp.float32),
        ],
        in_specs=[pl.BlockSpec(memory_space=pltpu.SMEM)] + [vmem] * 9,
        out_specs=[vmem] * 4,
        scratch_shapes=[
            pltpu.VMEM((NX, SLAB, F), jnp.float32),
            pltpu.VMEM((NX, SLAB, F), jnp.float32),
            pltpu.VMEM((NX, SLAB, F), jnp.float32),
            pltpu.VMEM((NX * SLAB, F), jnp.float32),
            pltpu.VMEM((NX * SLAB, F), jnp.bfloat16),
            pltpu.VMEM((NX, F), jnp.float32),
            pltpu.VMEM((NX, F), jnp.float32),
            pltpu.VMEM((3, NX, 128), jnp.float32),
            pltpu.VMEM((3, 128, NX), jnp.float32),
            pltpu.VMEM((2, NX * SLAB, WIDE), jnp.float32),
            pltpu.VMEM((2, NX * SLAB, WIDE), jnp.bfloat16),
            pltpu.VMEM((NX * SLAB, 2 * F), jnp.bfloat16),
        ],
        compiler_params=params(),
        cost_estimate=pl.CostEstimate(
            flops=4 * 2816 * F * H, bytes_accessed=6 * 2**20, transcendentals=2816 * H
        ),
        name="rollout",
    )(
        chunk,
        msg,
        left,
        right,
        w_in_t,
        w_out_t,
        jnp.asarray(split_table(block)),
        jnp.asarray(split_table(block.T)),
        diffusivity.reshape(1, F),
        stiffness.reshape(1, F),
    )


def prepare_kernel(plan_ref, target_ref, w_in_ref, w_out_ref, out_ref, w_in_t, w_out_t, wide):
    wide[...] = target_ref[0].astype(jnp.float32)
    for x in range(2):
        t = wide[pl.ds(x, F, stride=2), :].T
        out_ref[0, :, x] = t.reshape(8, CHUNK, F).astype(jnp.bfloat16)
    w_in_t[...] = w_in_ref[...].T
    w_out_t[...] = w_out_ref[...].T


def prepare(targets, w_in, w_out, plan):
    part = H // MB
    down = lambda i, plan: (i, 0)
    along = lambda i, plan: (0, i)
    return pl.pallas_call(
        prepare_kernel,
        grid_spec=pltpu.PrefetchScalarGridSpec(
            num_scalar_prefetch=1,
            grid=(MB,),
            in_specs=[
                pl.BlockSpec((1, 2 * F, 128), lambda i, plan: (plan[i], 0, 0)),
                pl.BlockSpec((part, F), down),
                pl.BlockSpec((F, part), along),
            ],
            out_specs=[
                pl.BlockSpec((1, 8, 2, CHUNK, F), lambda i, plan: (i, 0, 0, 0, 0)),
                pl.BlockSpec((F, part), along),
                pl.BlockSpec((part, F), down),
            ],
            scratch_shapes=[pltpu.VMEM((2 * F, 128), jnp.float32)],
        ),
        out_shape=[
            jax.ShapeDtypeStruct((MB, 8, 2, CHUNK, F), jnp.bfloat16),
            jax.ShapeDtypeStruct((F, H), jnp.bfloat16),
            jax.ShapeDtypeStruct((H, F), jnp.bfloat16),
        ],
        compiler_params=params(),
        cost_estimate=pl.CostEstimate(flops=0, bytes_accessed=6 * 2**20, transcendentals=0),
        name="prepare",
    )(plan, targets, w_in, w_out)


def spread_kernel(in_ref, out_ref):
    for x in range(2):
        block = in_ref[0, :, x].astype(jnp.float32).reshape(128, F)
        out_ref[0, pl.ds(x, F, stride=2), :] = block.T


def spread_trajectory(arrived):
    return pl.pallas_call(
        spread_kernel,
        grid=(MB,),
        in_specs=[pl.BlockSpec((1, 8, 2, CHUNK, F), lambda i: (i, 0, 0, 0, 0))],
        out_specs=pl.BlockSpec((1, 2 * F, 128), lambda i: (i, 0, 0)),
        out_shape=jax.ShapeDtypeStruct((MB, 2 * F, 128), jnp.float32),
        compiler_params=params(),
        name="spread_trajectory",
    )(arrived)


def grad_block(columns, w_in_ref, w_out_t_ref, scratch):
    before, back, hidden, change = scratch
    rows = w_in_ref.shape[0]
    parts = [
        (refs, slice(part * WIDE, (part + 1) * WIDE))
        for refs in columns
        for part in range(COLS // WIDE)
    ]

    def front(n):
        (_, x_t, _, misfit_t), at = parts[n]
        before[n % 2] = jnp.dot(w_in_ref[...], x_t[:, at], preferred_element_type=jnp.float32)
        back[n % 2] = jnp.dot(
            w_out_t_ref[...], misfit_t[:, at], preferred_element_type=jnp.float32
        )

    grad_in = jnp.zeros((rows, F), jnp.float32)
    grad_out = jnp.zeros((rows, F), jnp.float32)
    front(0)
    for n, ((x_ref, _, misfit, _), at) in enumerate(parts):
        if n + 1 < len(parts):
            front(n + 1)
        m = n % 2
        for r in range(0, rows, STRIP):
            strip = jnp.tanh(before[m, r : r + STRIP])
            hidden[m, r : r + STRIP] = strip.astype(jnp.bfloat16)
            strip = back[m, r : r + STRIP] * (1.0 - strip * strip)
            change[m, r : r + STRIP] = strip.astype(jnp.bfloat16)
        grad_out += jnp.dot(hidden[m], misfit[at], preferred_element_type=jnp.float32)
        grad_in += jnp.dot(change[m], x_ref[at], preferred_element_type=jnp.float32)
    shape = (rows // ROWS, ROWS, F)
    return grad_in.reshape(shape), grad_out.reshape(shape)


def columns_kernel(x_ref, tend_ref, target_ref, wet_ref, out_ref):
    for r in range(0, COLS, 64):
        at = slice(r, r + 64)
        gap = tend_ref[at] - target_ref[at].astype(jnp.float32)
        gap = wet_ref[r % OWN : r % OWN + 64] * gap * GRAD_SCALE
        out_ref[0, at] = x_ref[at]
        out_ref[1, at] = gap.astype(jnp.bfloat16)


def own_columns(inputs, tend, target, wet):
    return pl.pallas_call(
        columns_kernel,
        out_shape=jax.ShapeDtypeStruct((2, COLS, F), jnp.bfloat16),
        in_specs=[pl.BlockSpec(memory_space=pltpu.VMEM)] * 4,
        out_specs=pl.BlockSpec(memory_space=pltpu.VMEM),
        compiler_params=params(),
        name="own_columns",
    )(inputs, tend, target, wet)


def grad_kernel(half_ref, own_ref, their_ref, w_in_ref, w_out_ref, out_ref, turned, *scratch):
    both = (own_ref, their_ref)

    @pl.when(pl.program_id(0) == 0)
    def _():
        for n, ref in enumerate(both):
            for part in range(STEPS):
                at = slice(part * OWN, (part + 1) * OWN)
                turned[n, 0, :, at] = ref[0, at].T
                turned[n, 1, :, at] = ref[1, at].T

    columns = [
        (ref.at[0], turned.at[n, 0], ref.at[1], turned.at[n, 1]) for n, ref in enumerate(both)
    ]
    for n, grad in enumerate(grad_block(columns, w_in_ref, w_out_ref, scratch)):
        out_ref[:, n] = grad.astype(jnp.bfloat16)


def half_grads(half, own, theirs, w_in, w_out_t):
    blocks = HALF // HB2
    weight = pl.BlockSpec((HB2, F), lambda i, half: (half[0] * blocks + i, 0))
    whole = pl.BlockSpec((2, COLS, F), lambda i, half: (0, 0, 0))
    return pl.pallas_call(
        grad_kernel,
        grid_spec=pltpu.PrefetchScalarGridSpec(
            num_scalar_prefetch=1,
            grid=(blocks,),
            in_specs=[whole, whole, weight, weight],
            out_specs=pl.BlockSpec((HB2 // ROWS, 2, ROWS, F), lambda i, half: (i, 0, 0, 0)),
            scratch_shapes=[pltpu.VMEM((2, 2, F, COLS), jnp.bfloat16)]
            + [pltpu.VMEM((2, HB2, WIDE), jnp.float32)] * 2
            + [pltpu.VMEM((2, HB2, WIDE), jnp.bfloat16)] * 2,
        ),
        out_shape=jax.ShapeDtypeStruct((PARTS, 2, ROWS, F), jnp.bfloat16),
        compiler_params=params(("arbitrary",)),
        cost_estimate=pl.CostEstimate(
            flops=16 * COLS * F * HALF, bytes_accessed=5 * 2**20, transcendentals=2 * COLS * HALF
        ),
        name="half_grads",
    )(half, own, theirs, w_in, w_out_t)


def plane_kernel(in_ref, out_ref):
    total = in_ref[0].astype(jnp.float32)
    for n in range(1, PARTS):
        total += in_ref[n].astype(jnp.float32)
    out_ref[...] = total.astype(jnp.bfloat16)


def plane_sum(parts):
    vmem = pl.BlockSpec(memory_space=pltpu.VMEM)
    return pl.pallas_call(
        plane_kernel,
        out_shape=jax.ShapeDtypeStruct((2, ROWS, F), jnp.bfloat16),
        in_specs=[vmem],
        out_specs=vmem,
        compiler_params=params(mib=32),
        name="plane_sum",
    )(parts)


def column_kernel(own_ref, near_ref, far_ref, both_ref, out_ref):
    powers = []
    for g in range(2):
        own, near, far, both = (
            ref[g].astype(jnp.float32) for ref in (own_ref, near_ref, far_ref, both_ref)
        )
        total = (own + near) + (far + both)
        power = exponent(jnp.max(jnp.abs(total), axis=0, keepdims=True))
        powers.append(power)
        code = to_int16(encode(total, power))
        for n in range(PARTS):
            out_ref[n, g * ROWS : (g + 1) * ROWS] = code
    tail = to_int16(jnp.concatenate(powers + [jnp.zeros((14, F), jnp.float32)], axis=0))
    for n in range(PARTS):
        out_ref[n, 2 * ROWS : 2 * ROWS + 16] = tail


def column_copies(*planes):
    vmem = pl.BlockSpec(memory_space=pltpu.VMEM)
    return pl.pallas_call(
        column_kernel,
        out_shape=jax.ShapeDtypeStruct((PARTS, 2 * ROWS + 16, F), jnp.int16),
        in_specs=[vmem] * 4,
        out_specs=vmem,
        compiler_params=params(mib=32),
        name="column_copies",
    )(*planes)


def finish_kernel(half_ref, code_ref, *refs):
    grad_in_ref, grad_out_ref = refs[-2:]
    for n in range(0, code_ref.shape[0], 2):
        at = slice(n * ROWS, (n + 2) * ROWS)
        both = []
        for m in (n, n + 1):
            code = to_float(code_ref[m])
            grad_in_ref[m * ROWS : (m + 1) * ROWS] = decode(
                code[0:ROWS], code[2 * ROWS : 2 * ROWS + 1]
            )
            both.append(decode(code[ROWS : 2 * ROWS], code[2 * ROWS + 1 : 2 * ROWS + 2]))
        grad_out_ref[:, at] = jnp.concatenate(both, axis=0).T


def finish_half(half, code, before=()):
    return pl.pallas_call(
        finish_kernel,
        grid_spec=pltpu.PrefetchScalarGridSpec(
            num_scalar_prefetch=1,
            grid=(2,),
            in_specs=[pl.BlockSpec((PARTS // 2, 2 * ROWS + 16, F), lambda i, half: (i, 0, 0))]
            + [pl.BlockSpec(memory_space=pl.ANY)] * len(before),
            out_specs=[
                pl.BlockSpec((1024, F), lambda i, half: (half[0] * 2 + i, 0)),
                pl.BlockSpec((F, 1024), lambda i, half: (0, half[0] * 2 + i)),
            ],
        ),
        out_shape=[
            jax.ShapeDtypeStruct((H, F), jnp.float32),
            jax.ShapeDtypeStruct((F, H), jnp.float32),
        ],
        input_output_aliases={2: 0, 3: 1} if before else {},
        compiler_params=params(("arbitrary",), 32),
        name="finish_half",
    )(half, code, *before)


def swap(value, axes):
    return lax.all_to_all(value, axes, split_axis=0, concat_axis=0, tiled=True)


def local(initial_states, targets, w_in, w_out, diffusivity, stiffness, land_mask, wet_levels, plan):
    core = lax.axis_index("core").astype(jnp.int32).reshape(1)
    section = lax.axis_index("sec").astype(jnp.int32).reshape(1)
    chunk = (lax.axis_index(("cx", "core"))).astype(jnp.int32).reshape(1)

    states = initial_states.reshape(MB, 2 * F, 128)
    msg = swap(init_slabs(section, plan, states, land_mask, wet_levels), TILE)
    place = lambda half, chunk, col: (half * 8 + chunk) * 4 + col
    forward = [
        (place(h, j, c), place(h, (j + 1) % 8, c + (j + 1) // 8))
        for h in range(2)
        for j in range(8)
        for c in range(4)
        if c + (j + 1) // 8 < 4
    ]
    target, w_in_t, w_out_t = prepare(targets.reshape(MB, 2 * F, 128), w_in, w_out, plan)
    last, first, target = lax.optimization_barrier((msg[:, 32:48], msg[:, 0:16], target))
    left = lax.ppermute(last, TILE + COL, forward)
    right = lax.ppermute(first, TILE + COL, [(b, a) for a, b in forward])
    left, right, target = lax.optimization_barrier((left, right, target))
    target = swap(target.reshape(64, 2, CHUNK, F), ("sec",) + TILE).reshape(COLS, F)

    traj, inputs, tend, wet = rollout(chunk, msg, left, right, w_in_t, w_out_t, diffusivity, stiffness)
    arrived = swap(traj.reshape(64, 2, CHUNK, F), ("sec",) + TILE)

    own = own_columns(
        inputs.reshape(COLS, F), tend.reshape(COLS, F), target, wet.reshape(OWN, F)
    )
    theirs = lax.ppermute(own, "core", [(0, 1), (1, 0)])
    pair = half_grads(core, own, theirs, w_in, w_out_t)
    pair, arrived = lax.optimization_barrier((pair, arrived))

    trajectory = spread_trajectory(arrived.reshape(MB, 8, 2, CHUNK, F))
    plane = plane_sum(swap(pair, SPREAD))
    plane, trajectory = lax.optimization_barrier((plane, trajectory))
    others = [
        lax.ppermute(plane, ("zh", "c1"), [(i, i ^ n) for i in range(4)]) for n in range(1, 4)
    ]
    code = swap(column_copies(plane, *others), SPREAD)
    across = lax.ppermute(code, "core", [(0, 1), (1, 0)])
    grad_in, grad_out = finish_half(1 - core, across, finish_half(core, code))
    return (trajectory.reshape(1, MB, F, 2, 128), grad_in, grad_out)


def solution(mesh):
    fine = Mesh(mesh.devices.reshape(4, 2, 4, 2, 2, 2), ("sec", "zh", "cx", "core", "c1", "c0"))
    in_specs = (
        P(None, None, TILE, COL),
        P("sec", None, None, TILE, COL),
        P(),
        P(),
        P(),
        P(),
        P(TILE, COL),
        P(TILE, COL),
        P(),
    )
    out_specs = (P("sec", None, None, TILE, COL), P(), P())
    return jax.shard_map(local, mesh=fine, in_specs=in_specs, out_specs=out_specs, check_vma=False)
```

```python
import math

import jax
import jax.numpy as jnp
import numpy as np
from jax import lax
from jax.experimental import pallas as pl
from jax.experimental.pallas import tpu as pltpu
from jax.sharding import Mesh, PartitionSpec as P

V = 8
L = 16
H = 4096
F = 128
STEPS = 4
MB = 8
NX = 32
NY = 512
CHUNK = 16
HALO = STEPS
SLAB = CHUNK + 2 * HALO
MSG = 48
CODE = 32000.0
UNIT = 32768.0 / CODE
OWN = NX * CHUNK
COLS = STEPS * OWN
HB1 = 2048
HB2 = 1024
WIDE = 512
STRIP = 32
HALF = H // 2
GRAD_SCALE = 1.0 / math.sqrt(MB * STEPS * NX * NY)
TILE = ("zh", "cx", "core")
COL = ("c1", "c0")
SAME_CORE = ("sec", "zh", "cx")
ACROSS = [(0, 1), (1, 0)]
SPREAD = ("sec", "cx", "c0")
PARTS = 32
ROWS = H // 2 // PARTS


def mode_block():
    order = np.arange(L)
    angles = np.pi * (order[None, :] + 0.5) * order[:, None] / L
    weights = np.where(order[:, None] == 0, math.sqrt(1.0 / L), math.sqrt(2.0 / L))
    return np.kron(np.eye(V), np.cos(angles) * weights)


def split_table(matrix):
    high = matrix.astype(jnp.bfloat16)
    low = (matrix - high.astype(np.float64)).astype(jnp.bfloat16)
    return np.concatenate([high, high, low], axis=0)


def params(semantics=None, mib=60):
    return pltpu.CompilerParams(dimension_semantics=semantics, vmem_limit_bytes=mib * 2**20)


def exponent(largest):
    return jnp.ceil(jnp.log(jnp.maximum(largest, 1e-30)) * (1.0 / math.log(2.0)) + 0.01)


def encode(value, power):
    scaled = value * (jnp.exp2(15.0 - power) * (1.0 / UNIT))
    return jnp.round(jnp.clip(scaled, -32767.0, 32767.0))


def to_int16(value):
    return value.astype(jnp.int32).astype(jnp.int16)


def to_float(code):
    return code.astype(jnp.int32).astype(jnp.float32)


def decode(value, power):
    return value * (jnp.exp2(power - 15.0) * UNIT)


def init_kernel(section_ref, plan_ref, state_ref, land_ref, levels_ref, msg_ref):
    power = exponent(jnp.max(jnp.abs(state_ref[0]), keepdims=True))
    code = [encode(state_ref[0, pl.ds(x, F, stride=2), :], power).T for x in range(2)]
    depth = jnp.where(land_ref[...] == 1, levels_ref[...], 0).astype(jnp.float32)
    extra = jnp.concatenate(
        [depth, jnp.broadcast_to(power, (1, 128)), jnp.zeros((5, 128), jnp.float32)], axis=0
    )
    for j in range(8):
        y = CHUNK * j
        first = [c[y : y + HALO] for c in code]
        middle = [c[y + HALO : y + CHUNK - HALO] for c in code]
        last = [c[y + CHUNK - HALO : y + CHUNK] for c in code]
        msg_ref[j] = to_int16(jnp.concatenate(first + [extra] + middle + last + [extra], axis=0))


def init_slabs(section, plan, states, land_mask, wet_levels):
    whole = lambda i, sec, plan: (0, 0)
    return pl.pallas_call(
        init_kernel,
        grid_spec=pltpu.PrefetchScalarGridSpec(
            num_scalar_prefetch=2,
            grid=(2,),
            in_specs=[
                pl.BlockSpec((1, 2 * F, 128), lambda i, sec, plan: (plan[2 * sec[0] + i], 0, 0)),
                pl.BlockSpec((2, 128), whole),
                pl.BlockSpec((2, 128), whole),
            ],
            out_specs=pl.BlockSpec((8, MSG, F), lambda i, sec, plan: (i, 0, 0)),
        ),
        out_shape=jax.ShapeDtypeStruct((16, MSG, F), jnp.int16),
        compiler_params=params(("arbitrary",)),
        name="init_slabs",
    )(section, plan, states, land_mask, wet_levels)


def levels():
    return (lax.broadcasted_iota(jnp.int32, (1, F), 1) % L).astype(jnp.float32)


def pack_halo(halo, step):
    if step == STEPS - 1:
        return jnp.zeros((0, F), jnp.float32)
    share = (1, 2, 4)[step]
    halo = halo.reshape(NX // share, share, 8, F)
    packed = halo[:, 0]
    row = lax.broadcasted_iota(jnp.int32, packed.shape, 1)
    for n in range(1, share):
        shift = n * 8 // share
        keep = STEPS - 1 - step
        place = (row + (8 - shift) + keep) % 8 < 2 * keep
        packed = jnp.where(place, pltpu.roll(halo[:, n], shift, 1), packed)
    return packed.reshape(NX // share * 8, F)


def unpack_halo(packed, step):
    share = (1, 2, 4)[step]
    packed = packed.reshape(NX // share, 8, F)
    parts = [packed] + [pltpu.roll(packed, 8 - n * 8 // share, 1) for n in range(1, share)]
    return jnp.stack(parts, axis=1).reshape(NX, 8, F)


def rollout_kernel(
    chunk_ref, msg_ref, left_ref, right_ref, w_in_t, w_out_t, mode_ref, mode_t, diff_ref, stiff_ref,
    traj_ref, inputs_ref, tend_ref, own_wet_ref,
    state, wet, modal, acc, x_scr, gain, pull, depth, depth_t, before, hidden, split,
):
    for t in range(16):
        for n, (ref, base) in enumerate(
            ((msg_ref, 0), (msg_ref, 16), (msg_ref, 32), (right_ref, 0), (left_ref, 0))
        ):
            piece = to_float(ref[t, base : base + 16])
            if n != 1:
                scale = decode(1.0, piece[10:11])
            rows = 8 if n == 1 else HALO
            at = (0, HALO, CHUNK - HALO, CHUNK, CHUNK + HALO)[n]
            for x in range(2):
                state[2 * t + x, at : at + rows] = piece[x * rows : (x + 1) * rows] * scale
            if n in (0, 3, 4):
                depth[n // 2 if n else 0, 2 * t : 2 * t + 2] = piece[8:10]
    for n in range(3):
        depth_t[n] = depth[n].T
    mine = chunk_ref[0]
    y_own = pl.multiple_of(mine * CHUNK, CHUNK)
    y_right = pl.multiple_of(lax.rem(mine + 1, 8) * CHUNK, CHUNK)
    y_left = pl.multiple_of(lax.rem(mine + 7, 8) * CHUNK + 8, 8)
    here = jnp.concatenate(
        [
            depth_t[0, pl.ds(y_own, CHUNK)],
            depth_t[1, pl.ds(y_right, 8)][:HALO],
            depth_t[2, pl.ds(y_left, 8)][8 - HALO :],
        ],
        axis=0,
    )
    level = levels()
    for x in range(NX):
        wet[x] = jnp.where(level < here[:, x : x + 1], 1.0, 0.0)
    own_wet_ref[...] = wet[:, :CHUNK]

    a = stiff_ref[...]
    u = 1.0 + a
    for i in range(NX):
        r = 1.0 / (a + u)
        gain[pl.ds(i, 1), :] = r
        pull[pl.ds(i, 1), :] = a * r
        u = 1.0 + a * (u * r)
    diff = diff_ref[...]

    def put_split(x, value):
        at = slice(x * SLAB, (x + 2) * SLAB)
        high = value.astype(jnp.bfloat16)
        split[at, 0:F] = high
        split[at, F : 2 * F] = (value - high.astype(jnp.float32)).astype(jnp.bfloat16)

    def transform(table):
        return jnp.dot(
            split[...], table[0 : 2 * F], preferred_element_type=jnp.float32
        ) + jnp.dot(split[:, 0:F], table[2 * F :], preferred_element_type=jnp.float32)

    for step in range(STEPS):
        for x in range(0, NX, 2):
            pieces = []
            for at in (x, x + 1):
                here = state[at]
                around = pltpu.roll(here, 1, 0) + pltpu.roll(here, SLAB - 1, 0) - 4.0 * here
                if at > 0:
                    around += state[at - 1]
                if at < NX - 1:
                    around += state[at + 1]
                pieces.append(wet[at] * (here + diff * around))
            put_split(x, jnp.concatenate(pieces, axis=0))
        modal[...] = transform(mode_t).reshape(NX, SLAB, F)
        part = modal[0] * gain[pl.ds(0, 1), :]
        modal[0] = part
        for i in range(1, NX):
            part = modal[i] * gain[pl.ds(i, 1), :] + pull[pl.ds(i, 1), :] * part
            modal[i] = part
        for i in range(NX - 2, -1, -1):
            behind = part
            part = modal[i] + pull[pl.ds(i, 1), :] * part
            if i % 2 == 0:
                put_split(i, jnp.concatenate([part, behind], axis=0))
        after = wet[...] * transform(mode_ref).reshape(NX, SLAB, F)
        inputs_ref[step] = after[:, :CHUNK].astype(jnp.bfloat16)
        extra = pack_halo(after[:, CHUNK:], step)
        count = OWN + extra.shape[0]
        state[...] = after
        x_scr[0:OWN] = after[:, :CHUNK].reshape(OWN, F).astype(jnp.bfloat16)
        if step < STEPS - 1:
            x_scr[OWN:count] = extra.astype(jnp.bfloat16)
        acc[0:count] = jnp.zeros((count, F), jnp.float32)

        def block(b, carry, n=count):
            def front(i):
                at = pl.multiple_of(b * HB1 + i * WIDE, WIDE)
                before[i % 2, 0:n] = jnp.dot(
                    x_scr[0:n], w_in_t[:, pl.ds(at, WIDE)], preferred_element_type=jnp.float32
                )
                return at

            at = front(0)
            for i in range(HB1 // WIDE):
                following = front(i + 1) if i + 1 < HB1 // WIDE else None
                for r in range(0, n, STRIP):
                    strip = jnp.tanh(before[i % 2, r : r + STRIP])
                    hidden[i % 2, r : r + STRIP] = strip.astype(jnp.bfloat16)
                acc[0:n] += jnp.dot(
                    hidden[i % 2, 0:n],
                    w_out_t[pl.ds(at, WIDE), :],
                    preferred_element_type=jnp.float32,
                )
                at = following
            return carry

        lax.fori_loop(0, H // HB1, block, 0)
        tendency = acc[0:OWN].reshape(NX, CHUNK, F)
        result = wet[:, :CHUNK] * (state[:, :CHUNK] + tendency)
        traj_ref[step] = result.astype(jnp.bfloat16)
        tend_ref[step] = tendency
        if step < STEPS - 1:
            beside = unpack_halo(acc[OWN:count], step)
            state[:, CHUNK:] = wet[:, CHUNK:] * (state[:, CHUNK:] + beside)
            state[:, :CHUNK] = result


def rollout(chunk, msg, left, right, w_in_t, w_out_t, diffusivity, stiffness):
    block = mode_block()
    vmem = pl.BlockSpec(memory_space=pltpu.VMEM)
    return pl.pallas_call(
        rollout_kernel,
        out_shape=[
            jax.ShapeDtypeStruct((STEPS, NX, CHUNK, F), jnp.bfloat16),
            jax.ShapeDtypeStruct((STEPS, NX, CHUNK, F), jnp.bfloat16),
            jax.ShapeDtypeStruct((STEPS, NX, CHUNK, F), jnp.float32),
            jax.ShapeDtypeStruct((NX, CHUNK, F), jnp.float32),
        ],
        in_specs=[pl.BlockSpec(memory_space=pltpu.SMEM)] + [vmem] * 9,
        out_specs=[vmem] * 4,
        scratch_shapes=[
            pltpu.VMEM((NX, SLAB, F), jnp.float32),
            pltpu.VMEM((NX, SLAB, F), jnp.float32),
            pltpu.VMEM((NX, SLAB, F), jnp.float32),
            pltpu.VMEM((NX * SLAB, F), jnp.float32),
            pltpu.VMEM((NX * SLAB, F), jnp.bfloat16),
            pltpu.VMEM((NX, F), jnp.float32),
            pltpu.VMEM((NX, F), jnp.float32),
            pltpu.VMEM((3, NX, 128), jnp.float32),
            pltpu.VMEM((3, 128, NX), jnp.float32),
            pltpu.VMEM((2, NX * SLAB, WIDE), jnp.float32),
            pltpu.VMEM((2, NX * SLAB, WIDE), jnp.bfloat16),
            pltpu.VMEM((NX * SLAB, 2 * F), jnp.bfloat16),
        ],
        compiler_params=params(),
        cost_estimate=pl.CostEstimate(
            flops=4 * 2816 * F * H, bytes_accessed=6 * 2**20, transcendentals=2816 * H
        ),
        name="rollout",
    )(
        chunk,
        msg,
        left,
        right,
        w_in_t,
        w_out_t,
        jnp.asarray(split_table(block)),
        jnp.asarray(split_table(block.T)),
        diffusivity.reshape(1, F),
        stiffness.reshape(1, F),
    )


def prepare_kernel(
    plan_ref, core_ref, own_ref, their_ref, w_in_ref, w_out_ref, out_ref, w_in_t, w_out_t, wide, turned
):
    core = core_ref[0]
    for source, ref in ((core, own_ref), (1 - core, their_ref)):
        wide[...] = ref[0].astype(jnp.float32)
        for x in range(2):
            turned[x] = wide[pl.ds(x, F, stride=2), :].T
            for cx in range(4):
                at = pl.multiple_of((2 * cx + core) * CHUNK, CHUNK)
                out_ref[0, cx, source, x] = turned[x, pl.ds(at, CHUNK)].astype(jnp.bfloat16)
    w_in_t[...] = w_in_ref[...].T
    w_out_t[...] = w_out_ref[...].T


def prepare(targets, theirs, w_in, w_out, plan, core):
    part = H // MB
    down = lambda i, plan, core: (i, 0)
    along = lambda i, plan, core: (0, i)
    sample = pl.BlockSpec((1, 2 * F, 128), lambda i, plan, core: (plan[i], 0, 0))
    return pl.pallas_call(
        prepare_kernel,
        grid_spec=pltpu.PrefetchScalarGridSpec(
            num_scalar_prefetch=2,
            grid=(MB,),
            in_specs=[
                sample,
                sample,
                pl.BlockSpec((part, F), down),
                pl.BlockSpec((F, part), along),
            ],
            out_specs=[
                pl.BlockSpec((1, 4, 2, 2, CHUNK, F), lambda i, plan, core: (i, 0, 0, 0, 0, 0)),
                pl.BlockSpec((F, part), along),
                pl.BlockSpec((part, F), down),
            ],
            scratch_shapes=[
                pltpu.VMEM((2 * F, 128), jnp.float32),
                pltpu.VMEM((2, 128, F), jnp.float32),
            ],
        ),
        out_shape=[
            jax.ShapeDtypeStruct((MB, 4, 2, 2, CHUNK, F), jnp.bfloat16),
            jax.ShapeDtypeStruct((F, H), jnp.bfloat16),
            jax.ShapeDtypeStruct((H, F), jnp.bfloat16),
        ],
        compiler_params=params(),
        cost_estimate=pl.CostEstimate(flops=0, bytes_accessed=6 * 2**20, transcendentals=0),
        name="prepare",
    )(plan, core, targets, theirs, w_in, w_out)


def spread_kernel(core_ref, own_ref, their_ref, out_ref):
    even = core_ref[0] == 0
    for x in range(2):
        chunks = []
        for cx in range(4):
            own = own_ref[0, cx, 0, x].astype(jnp.float32)
            their = their_ref[0, cx, 0, x].astype(jnp.float32)
            chunks += [jnp.where(even, own, their), jnp.where(even, their, own)]
        out_ref[0, pl.ds(x, F, stride=2), :] = jnp.concatenate(chunks, axis=0).T


def spread_trajectory(core, own, theirs):
    block = pl.BlockSpec((1, 4, 1, 2, CHUNK, F), lambda i, core: (i, 0, core[0], 0, 0, 0))
    return pl.pallas_call(
        spread_kernel,
        grid_spec=pltpu.PrefetchScalarGridSpec(
            num_scalar_prefetch=1,
            grid=(MB,),
            in_specs=[block, block],
            out_specs=pl.BlockSpec((1, 2 * F, 128), lambda i, core: (i, 0, 0)),
        ),
        out_shape=jax.ShapeDtypeStruct((MB, 2 * F, 128), jnp.float32),
        compiler_params=params(),
        name="spread_trajectory",
    )(core, own, theirs)


def grad_block(columns, w_in_ref, w_out_t_ref, scratch):
    before, back, hidden, change = scratch
    rows = w_in_ref.shape[0]
    parts = [
        (refs, slice(part * WIDE, (part + 1) * WIDE))
        for refs in columns
        for part in range(COLS // WIDE)
    ]

    def front(n):
        (_, x_t, _, misfit_t), at = parts[n]
        before[n % 2] = jnp.dot(w_in_ref[...], x_t[:, at], preferred_element_type=jnp.float32)
        back[n % 2] = jnp.dot(
            w_out_t_ref[...], misfit_t[:, at], preferred_element_type=jnp.float32
        )

    grad_in = jnp.zeros((rows, F), jnp.float32)
    grad_out = jnp.zeros((rows, F), jnp.float32)
    front(0)
    for n, ((x_ref, _, misfit, _), at) in enumerate(parts):
        if n + 1 < len(parts):
            front(n + 1)
        m = n % 2
        for r in range(0, rows, STRIP):
            strip = jnp.tanh(before[m, r : r + STRIP])
            hidden[m, r : r + STRIP] = strip.astype(jnp.bfloat16)
            strip = back[m, r : r + STRIP] * (1.0 - strip * strip)
            change[m, r : r + STRIP] = strip.astype(jnp.bfloat16)
        grad_out += jnp.dot(hidden[m], misfit[at], preferred_element_type=jnp.float32)
        grad_in += jnp.dot(change[m], x_ref[at], preferred_element_type=jnp.float32)
    shape = (rows // ROWS, ROWS, F)
    return grad_in.reshape(shape), grad_out.reshape(shape)


def columns_kernel(x_ref, tend_ref, target_ref, wet_ref, out_ref):
    for r in range(0, COLS, 64):
        at = slice(r, r + 64)
        gap = tend_ref[at] - target_ref[at].astype(jnp.float32)
        gap = wet_ref[r % OWN : r % OWN + 64] * gap * GRAD_SCALE
        out_ref[0, at] = x_ref[at]
        out_ref[1, at] = gap.astype(jnp.bfloat16)


def own_columns(inputs, tend, target, wet):
    return pl.pallas_call(
        columns_kernel,
        out_shape=jax.ShapeDtypeStruct((2, COLS, F), jnp.bfloat16),
        in_specs=[pl.BlockSpec(memory_space=pltpu.VMEM)] * 4,
        out_specs=pl.BlockSpec(memory_space=pltpu.VMEM),
        compiler_params=params(),
        name="own_columns",
    )(inputs, tend, target, wet)


def grad_kernel(half_ref, own_ref, their_ref, w_in_ref, w_out_ref, out_ref, turned, *scratch):
    both = (own_ref, their_ref)

    @pl.when(pl.program_id(0) == 0)
    def _():
        for n, ref in enumerate(both):
            for part in range(STEPS):
                at = slice(part * OWN, (part + 1) * OWN)
                turned[n, 0, :, at] = ref[0, at].T
                turned[n, 1, :, at] = ref[1, at].T

    columns = [
        (ref.at[0], turned.at[n, 0], ref.at[1], turned.at[n, 1]) for n, ref in enumerate(both)
    ]
    for n, grad in enumerate(grad_block(columns, w_in_ref, w_out_ref, scratch)):
        out_ref[:, n] = grad.astype(jnp.bfloat16)


def half_grads(half, own, theirs, w_in, w_out_t):
    blocks = HALF // HB2
    weight = pl.BlockSpec((HB2, F), lambda i, half: (half[0] * blocks + i, 0))
    whole = pl.BlockSpec((2, COLS, F), lambda i, half: (0, 0, 0))
    return pl.pallas_call(
        grad_kernel,
        grid_spec=pltpu.PrefetchScalarGridSpec(
            num_scalar_prefetch=1,
            grid=(blocks,),
            in_specs=[whole, whole, weight, weight],
            out_specs=pl.BlockSpec((HB2 // ROWS, 2, ROWS, F), lambda i, half: (i, 0, 0, 0)),
            scratch_shapes=[pltpu.VMEM((2, 2, F, COLS), jnp.bfloat16)]
            + [pltpu.VMEM((2, HB2, WIDE), jnp.float32)] * 2
            + [pltpu.VMEM((2, HB2, WIDE), jnp.bfloat16)] * 2,
        ),
        out_shape=jax.ShapeDtypeStruct((PARTS, 2, ROWS, F), jnp.bfloat16),
        compiler_params=params(("arbitrary",)),
        cost_estimate=pl.CostEstimate(
            flops=16 * COLS * F * HALF, bytes_accessed=5 * 2**20, transcendentals=2 * COLS * HALF
        ),
        name="half_grads",
    )(half, own, theirs, w_in, w_out_t)


def plane_kernel(in_ref, out_ref):
    total = in_ref[0].astype(jnp.float32)
    for n in range(1, PARTS):
        total += in_ref[n].astype(jnp.float32)
    out_ref[...] = total.astype(jnp.bfloat16)


def plane_sum(parts):
    vmem = pl.BlockSpec(memory_space=pltpu.VMEM)
    return pl.pallas_call(
        plane_kernel,
        out_shape=jax.ShapeDtypeStruct((2, ROWS, F), jnp.bfloat16),
        in_specs=[vmem],
        out_specs=vmem,
        compiler_params=params(mib=32),
        name="plane_sum",
    )(parts)


def column_kernel(own_ref, near_ref, far_ref, both_ref, out_ref):
    powers = []
    for g in range(2):
        own, near, far, both = (
            ref[g].astype(jnp.float32) for ref in (own_ref, near_ref, far_ref, both_ref)
        )
        total = (own + near) + (far + both)
        power = exponent(jnp.max(jnp.abs(total), axis=0, keepdims=True))
        powers.append(power)
        code = to_int16(encode(total, power))
        for n in range(PARTS):
            out_ref[n, g * ROWS : (g + 1) * ROWS] = code
    tail = to_int16(jnp.concatenate(powers + [jnp.zeros((14, F), jnp.float32)], axis=0))
    for n in range(PARTS):
        out_ref[n, 2 * ROWS : 2 * ROWS + 16] = tail


def column_copies(*planes):
    vmem = pl.BlockSpec(memory_space=pltpu.VMEM)
    return pl.pallas_call(
        column_kernel,
        out_shape=jax.ShapeDtypeStruct((PARTS, 2 * ROWS + 16, F), jnp.int16),
        in_specs=[vmem] * 4,
        out_specs=vmem,
        compiler_params=params(mib=32),
        name="column_copies",
    )(*planes)


def finish_kernel(half_ref, code_ref, *refs):
    grad_in_ref, grad_out_ref = refs[-2:]
    for n in range(0, code_ref.shape[0], 2):
        at = slice(n * ROWS, (n + 2) * ROWS)
        both = []
        for m in (n, n + 1):
            code = to_float(code_ref[m])
            grad_in_ref[m * ROWS : (m + 1) * ROWS] = decode(
                code[0:ROWS], code[2 * ROWS : 2 * ROWS + 1]
            )
            both.append(decode(code[ROWS : 2 * ROWS], code[2 * ROWS + 1 : 2 * ROWS + 2]))
        grad_out_ref[:, at] = jnp.concatenate(both, axis=0).T


def finish_half(half, code, before=()):
    return pl.pallas_call(
        finish_kernel,
        grid_spec=pltpu.PrefetchScalarGridSpec(
            num_scalar_prefetch=1,
            grid=(2,),
            in_specs=[pl.BlockSpec((PARTS // 2, 2 * ROWS + 16, F), lambda i, half: (i, 0, 0))]
            + [pl.BlockSpec(memory_space=pl.ANY)] * len(before),
            out_specs=[
                pl.BlockSpec((1024, F), lambda i, half: (half[0] * 2 + i, 0)),
                pl.BlockSpec((F, 1024), lambda i, half: (0, half[0] * 2 + i)),
            ],
        ),
        out_shape=[
            jax.ShapeDtypeStruct((H, F), jnp.float32),
            jax.ShapeDtypeStruct((F, H), jnp.float32),
        ],
        input_output_aliases={2: 0, 3: 1} if before else {},
        compiler_params=params(("arbitrary",), 32),
        name="finish_half",
    )(half, code, *before)


def swap(value, axes):
    return lax.all_to_all(value, axes, split_axis=0, concat_axis=0, tiled=True)


def local(initial_states, targets, w_in, w_out, diffusivity, stiffness, land_mask, wet_levels, plan):
    core = lax.axis_index("core").astype(jnp.int32).reshape(1)
    section = lax.axis_index("sec").astype(jnp.int32).reshape(1)
    chunk = (lax.axis_index(("cx", "core"))).astype(jnp.int32).reshape(1)

    states = initial_states.reshape(MB, 2 * F, 128)
    msg = swap(init_slabs(section, plan, states, land_mask, wet_levels), TILE)
    place = lambda half, chunk, col: (half * 8 + chunk) * 4 + col
    forward = [
        (place(h, j, c), place(h, (j + 1) % 8, c + (j + 1) // 8))
        for h in range(2)
        for j in range(8)
        for c in range(4)
        if c + (j + 1) // 8 < 4
    ]
    targets = targets.reshape(MB, 2 * F, 128)
    their_targets = lax.ppermute(targets, "core", ACROSS)
    target, w_in_t, w_out_t = prepare(targets, their_targets, w_in, w_out, plan, core)
    last, first, target = lax.optimization_barrier((msg[:, 32:48], msg[:, 0:16], target))
    left = lax.ppermute(last, TILE + COL, forward)
    right = lax.ppermute(first, TILE + COL, [(b, a) for a, b in forward])
    left, right, target = lax.optimization_barrier((left, right, target))
    target = swap(target.reshape(32, 2, 2, CHUNK, F), SAME_CORE).reshape(COLS, F)

    traj, inputs, tend, wet = rollout(chunk, msg, left, right, w_in_t, w_out_t, diffusivity, stiffness)
    arrived = swap(traj.reshape(32, 2, 2, CHUNK, F), SAME_CORE)

    own = own_columns(
        inputs.reshape(COLS, F), tend.reshape(COLS, F), target, wet.reshape(OWN, F)
    )
    theirs = lax.ppermute(own, "core", ACROSS)
    pair = half_grads(core, own, theirs, w_in, w_out_t)
    pair, arrived = lax.optimization_barrier((pair, arrived))

    arrived = arrived.reshape(MB, 4, 2, 2, CHUNK, F)
    trajectory = spread_trajectory(core, arrived, lax.ppermute(arrived, "core", ACROSS))
    plane = plane_sum(swap(pair, SPREAD))
    plane, trajectory = lax.optimization_barrier((plane, trajectory))
    others = [
        lax.ppermute(plane, ("zh", "c1"), [(i, i ^ n) for i in range(4)]) for n in range(1, 4)
    ]
    code = swap(column_copies(plane, *others), SPREAD)
    across = lax.ppermute(code, "core", ACROSS)
    grad_in, grad_out = finish_half(1 - core, across, finish_half(core, code))
    return (trajectory.reshape(1, MB, F, 2, 128), grad_in, grad_out)


def solution(mesh):
    fine = Mesh(mesh.devices.reshape(4, 2, 4, 2, 2, 2), ("sec", "zh", "cx", "core", "c1", "c0"))
    in_specs = (
        P(None, None, TILE, COL),
        P("sec", None, None, TILE, COL),
        P(),
        P(),
        P(),
        P(),
        P(TILE, COL),
        P(TILE, COL),
        P(),
    )
    out_specs = (P("sec", None, None, TILE, COL), P(), P())
    return jax.shard_map(local, mesh=fine, in_specs=in_specs, out_specs=out_specs, check_vma=False)
```

```python
import math

import jax
import jax.numpy as jnp
import numpy as np
from jax import lax
from jax.experimental import pallas as pl
from jax.experimental.pallas import tpu as pltpu
from jax.sharding import Mesh, PartitionSpec as P

V = 8
L = 16
H = 4096
F = 128
STEPS = 4
MB = 8
NX = 32
NY = 512
CHUNK = 16
HALO = STEPS
SLAB = CHUNK + 2 * HALO
MSG = 48
CODE = 32000.0
UNIT = 32768.0 / CODE
OWN = NX * CHUNK
COLS = STEPS * OWN
HB1 = 2048
HB2 = 1024
WIDE = 512
STRIP = 32
HALF = H // 2
GRAD_SCALE = 1.0 / math.sqrt(MB * STEPS * NX * NY)
TILE = ("zh", "cx", "core")
COL = ("c1", "c0")
SPREAD = ("sec", "cx", "c0")
PARTS = 32
ROWS = H // 2 // PARTS


def mode_block():
    order = np.arange(L)
    angles = np.pi * (order[None, :] + 0.5) * order[:, None] / L
    weights = np.where(order[:, None] == 0, math.sqrt(1.0 / L), math.sqrt(2.0 / L))
    return np.kron(np.eye(V), np.cos(angles) * weights)


def split_table(matrix):
    high = matrix.astype(jnp.bfloat16)
    low = (matrix - high.astype(np.float64)).astype(jnp.bfloat16)
    return np.concatenate([high, high, low], axis=0)


def params(semantics=None, mib=60):
    return pltpu.CompilerParams(dimension_semantics=semantics, vmem_limit_bytes=mib * 2**20)


def exponent(largest):
    return jnp.ceil(jnp.log(jnp.maximum(largest, 1e-30)) * (1.0 / math.log(2.0)) + 0.01)


def encode(value, power):
    scaled = value * (jnp.exp2(15.0 - power) * (1.0 / UNIT))
    return jnp.round(jnp.clip(scaled, -32767.0, 32767.0))


def to_int16(value):
    return value.astype(jnp.int32).astype(jnp.int16)


def to_float(code):
    return code.astype(jnp.int32).astype(jnp.float32)


def decode(value, power):
    return value * (jnp.exp2(power - 15.0) * UNIT)


def init_kernel(section_ref, plan_ref, state_ref, land_ref, levels_ref, msg_ref):
    power = exponent(jnp.max(jnp.abs(state_ref[0]), keepdims=True))
    code = [encode(state_ref[0, pl.ds(x, F, stride=2), :], power).T for x in range(2)]
    depth = jnp.where(land_ref[...] == 1, levels_ref[...], 0).astype(jnp.float32)
    extra = jnp.concatenate(
        [depth, jnp.broadcast_to(power, (1, 128)), jnp.zeros((5, 128), jnp.float32)], axis=0
    )
    for j in range(8):
        y = CHUNK * j
        first = [c[y : y + HALO] for c in code]
        middle = [c[y + HALO : y + CHUNK - HALO] for c in code]
        last = [c[y + CHUNK - HALO : y + CHUNK] for c in code]
        msg_ref[j] = to_int16(jnp.concatenate(first + [extra] + middle + last + [extra], axis=0))


def init_slabs(section, plan, states, land_mask, wet_levels):
    whole = lambda i, sec, plan: (0, 0)
    return pl.pallas_call(
        init_kernel,
        grid_spec=pltpu.PrefetchScalarGridSpec(
            num_scalar_prefetch=2,
            grid=(2,),
            in_specs=[
                pl.BlockSpec((1, 2 * F, 128), lambda i, sec, plan: (plan[2 * sec[0] + i], 0, 0)),
                pl.BlockSpec((2, 128), whole),
                pl.BlockSpec((2, 128), whole),
            ],
            out_specs=pl.BlockSpec((8, MSG, F), lambda i, sec, plan: (i, 0, 0)),
        ),
        out_shape=jax.ShapeDtypeStruct((16, MSG, F), jnp.int16),
        compiler_params=params(("arbitrary",)),
        name="init_slabs",
    )(section, plan, states, land_mask, wet_levels)


def levels():
    return (lax.broadcasted_iota(jnp.int32, (1, F), 1) % L).astype(jnp.float32)


def pack_halo(halo, step):
    if step == STEPS - 1:
        return jnp.zeros((0, F), jnp.float32)
    share = (1, 2, 4)[step]
    halo = halo.reshape(NX // share, share, 8, F)
    packed = halo[:, 0]
    row = lax.broadcasted_iota(jnp.int32, packed.shape, 1)
    for n in range(1, share):
        shift = n * 8 // share
        keep = STEPS - 1 - step
        place = (row + (8 - shift) + keep) % 8 < 2 * keep
        packed = jnp.where(place, pltpu.roll(halo[:, n], shift, 1), packed)
    return packed.reshape(NX // share * 8, F)


def unpack_halo(packed, step):
    share = (1, 2, 4)[step]
    packed = packed.reshape(NX // share, 8, F)
    parts = [packed] + [pltpu.roll(packed, 8 - n * 8 // share, 1) for n in range(1, share)]
    return jnp.stack(parts, axis=1).reshape(NX, 8, F)


def rollout_kernel(
    chunk_ref, msg_ref, left_ref, right_ref, w_in_t, w_out_t, mode_ref, mode_t, diff_ref, stiff_ref,
    traj_ref, inputs_ref, tend_ref, own_wet_ref,
    state, wet, modal, acc, x_scr, gain, pull, depth, depth_t, before, hidden, split,
):
    for t in range(16):
        for n, (ref, base) in enumerate(
            ((msg_ref, 0), (msg_ref, 16), (msg_ref, 32), (right_ref, 0), (left_ref, 0))
        ):
            piece = to_float(ref[t, base : base + 16])
            if n != 1:
                scale = decode(1.0, piece[10:11])
            rows = 8 if n == 1 else HALO
            at = (0, HALO, CHUNK - HALO, CHUNK, CHUNK + HALO)[n]
            for x in range(2):
                state[2 * t + x, at : at + rows] = piece[x * rows : (x + 1) * rows] * scale
            if n in (0, 3, 4):
                depth[n // 2 if n else 0, 2 * t : 2 * t + 2] = piece[8:10]
    for n in range(3):
        depth_t[n] = depth[n].T
    mine = chunk_ref[0]
    y_own = pl.multiple_of(mine * CHUNK, CHUNK)
    y_right = pl.multiple_of(lax.rem(mine + 1, 8) * CHUNK, CHUNK)
    y_left = pl.multiple_of(lax.rem(mine + 7, 8) * CHUNK + 8, 8)
    here = jnp.concatenate(
        [
            depth_t[0, pl.ds(y_own, CHUNK)],
            depth_t[1, pl.ds(y_right, 8)][:HALO],
            depth_t[2, pl.ds(y_left, 8)][8 - HALO :],
        ],
        axis=0,
    )
    level = levels()
    for x in range(NX):
        wet[x] = jnp.where(level < here[:, x : x + 1], 1.0, 0.0)
    own_wet_ref[...] = wet[:, :CHUNK]

    a = stiff_ref[...]
    u = 1.0 + a
    for i in range(NX):
        r = 1.0 / (a + u)
        gain[pl.ds(i, 1), :] = r
        pull[pl.ds(i, 1), :] = a * r
        u = 1.0 + a * (u * r)
    diff = diff_ref[...]

    def put_split(x, value):
        at = slice(x * SLAB, (x + 2) * SLAB)
        high = value.astype(jnp.bfloat16)
        split[at, 0:F] = high
        split[at, F : 2 * F] = (value - high.astype(jnp.float32)).astype(jnp.bfloat16)

    def transform(table):
        return jnp.dot(
            split[...], table[0 : 2 * F], preferred_element_type=jnp.float32
        ) + jnp.dot(split[:, 0:F], table[2 * F :], preferred_element_type=jnp.float32)

    for step in range(STEPS):
        for x in range(0, NX, 2):
            pieces = []
            for at in (x, x + 1):
                here = state[at]
                around = pltpu.roll(here, 1, 0) + pltpu.roll(here, SLAB - 1, 0) - 4.0 * here
                if at > 0:
                    around += state[at - 1]
                if at < NX - 1:
                    around += state[at + 1]
                pieces.append(wet[at] * (here + diff * around))
            put_split(x, jnp.concatenate(pieces, axis=0))
        modal[...] = transform(mode_t).reshape(NX, SLAB, F)
        part = modal[0] * gain[pl.ds(0, 1), :]
        modal[0] = part
        for i in range(1, NX):
            part = modal[i] * gain[pl.ds(i, 1), :] + pull[pl.ds(i, 1), :] * part
            modal[i] = part
        for i in range(NX - 2, -1, -1):
            behind = part
            part = modal[i] + pull[pl.ds(i, 1), :] * part
            if i % 2 == 0:
                put_split(i, jnp.concatenate([part, behind], axis=0))
        after = wet[...] * transform(mode_ref).reshape(NX, SLAB, F)
        inputs_ref[step] = after[:, :CHUNK].astype(jnp.bfloat16)
        extra = pack_halo(after[:, CHUNK:], step)
        count = OWN + extra.shape[0]
        state[...] = after
        x_scr[0:OWN] = after[:, :CHUNK].reshape(OWN, F).astype(jnp.bfloat16)
        if step < STEPS - 1:
            x_scr[OWN:count] = extra.astype(jnp.bfloat16)
        acc[0:count] = jnp.zeros((count, F), jnp.float32)

        def block(b, carry, n=count):
            def front(i):
                at = pl.multiple_of(b * HB1 + i * WIDE, WIDE)
                before[i % 2, 0:n] = jnp.dot(
                    x_scr[0:n], w_in_t[:, pl.ds(at, WIDE)], preferred_element_type=jnp.float32
                )
                return at

            at = front(0)
            for i in range(HB1 // WIDE):
                following = front(i + 1) if i + 1 < HB1 // WIDE else None
                for r in range(0, n, STRIP):
                    strip = jnp.tanh(before[i % 2, r : r + STRIP])
                    hidden[i % 2, r : r + STRIP] = strip.astype(jnp.bfloat16)
                acc[0:n] += jnp.dot(
                    hidden[i % 2, 0:n],
                    w_out_t[pl.ds(at, WIDE), :],
                    preferred_element_type=jnp.float32,
                )
                at = following
            return carry

        lax.fori_loop(0, H // HB1, block, 0)
        tendency = acc[0:OWN].reshape(NX, CHUNK, F)
        result = wet[:, :CHUNK] * (state[:, :CHUNK] + tendency)
        traj_ref[step] = result.astype(jnp.bfloat16)
        tend_ref[step] = tendency
        if step < STEPS - 1:
            beside = unpack_halo(acc[OWN:count], step)
            state[:, CHUNK:] = wet[:, CHUNK:] * (state[:, CHUNK:] + beside)
            state[:, :CHUNK] = result


def rollout(chunk, msg, left, right, w_in_t, w_out_t, diffusivity, stiffness):
    block = mode_block()
    vmem = pl.BlockSpec(memory_space=pltpu.VMEM)
    return pl.pallas_call(
        rollout_kernel,
        out_shape=[
            jax.ShapeDtypeStruct((STEPS, NX, CHUNK, F), jnp.bfloat16),
            jax.ShapeDtypeStruct((STEPS, NX, CHUNK, F), jnp.bfloat16),
            jax.ShapeDtypeStruct((STEPS, NX, CHUNK, F), jnp.float32),
            jax.ShapeDtypeStruct((NX, CHUNK, F), jnp.float32),
        ],
        in_specs=[pl.BlockSpec(memory_space=pltpu.SMEM)] + [vmem] * 9,
        out_specs=[vmem] * 4,
        scratch_shapes=[
            pltpu.VMEM((NX, SLAB, F), jnp.float32),
            pltpu.VMEM((NX, SLAB, F), jnp.float32),
            pltpu.VMEM((NX, SLAB, F), jnp.float32),
            pltpu.VMEM((NX * SLAB, F), jnp.float32),
            pltpu.VMEM((NX * SLAB, F), jnp.bfloat16),
            pltpu.VMEM((NX, F), jnp.float32),
            pltpu.VMEM((NX, F), jnp.float32),
            pltpu.VMEM((3, NX, 128), jnp.float32),
            pltpu.VMEM((3, 128, NX), jnp.float32),
            pltpu.VMEM((2, NX * SLAB, WIDE), jnp.float32),
            pltpu.VMEM((2, NX * SLAB, WIDE), jnp.bfloat16),
            pltpu.VMEM((NX * SLAB, 2 * F), jnp.bfloat16),
        ],
        compiler_params=params(),
        cost_estimate=pl.CostEstimate(
            flops=4 * 2816 * F * H, bytes_accessed=6 * 2**20, transcendentals=2816 * H
        ),
        name="rollout",
    )(
        chunk,
        msg,
        left,
        right,
        w_in_t,
        w_out_t,
        jnp.asarray(split_table(block)),
        jnp.asarray(split_table(block.T)),
        diffusivity.reshape(1, F),
        stiffness.reshape(1, F),
    )


def prepare_kernel(plan_ref, target_ref, w_in_ref, w_out_ref, out_ref, w_in_t, w_out_t, wide):
    wide[...] = target_ref[0].astype(jnp.float32)
    for x in range(2):
        t = wide[pl.ds(x, F, stride=2), :].T
        out_ref[0, :, x] = t.reshape(8, CHUNK, F).astype(jnp.bfloat16)
    w_in_t[...] = w_in_ref[...].T
    w_out_t[...] = w_out_ref[...].T


def prepare(targets, w_in, w_out, plan):
    part = H // MB
    down = lambda i, plan: (i, 0)
    along = lambda i, plan: (0, i)
    return pl.pallas_call(
        prepare_kernel,
        grid_spec=pltpu.PrefetchScalarGridSpec(
            num_scalar_prefetch=1,
            grid=(MB,),
            in_specs=[
                pl.BlockSpec((1, 2 * F, 128), lambda i, plan: (plan[i], 0, 0)),
                pl.BlockSpec((part, F), down),
                pl.BlockSpec((F, part), along),
            ],
            out_specs=[
                pl.BlockSpec((1, 8, 2, CHUNK, F), lambda i, plan: (i, 0, 0, 0, 0)),
                pl.BlockSpec((F, part), along),
                pl.BlockSpec((part, F), down),
            ],
            scratch_shapes=[pltpu.VMEM((2 * F, 128), jnp.float32)],
        ),
        out_shape=[
            jax.ShapeDtypeStruct((MB, 8, 2, CHUNK, F), jnp.bfloat16),
            jax.ShapeDtypeStruct((F, H), jnp.bfloat16),
            jax.ShapeDtypeStruct((H, F), jnp.bfloat16),
        ],
        compiler_params=params(),
        cost_estimate=pl.CostEstimate(flops=0, bytes_accessed=6 * 2**20, transcendentals=0),
        name="prepare",
    )(plan, targets, w_in, w_out)


def spread_kernel(in_ref, out_ref):
    for x in range(2):
        block = in_ref[0, :, x].astype(jnp.float32).reshape(128, F)
        out_ref[0, pl.ds(x, F, stride=2), :] = block.T


def spread_trajectory(arrived):
    return pl.pallas_call(
        spread_kernel,
        grid=(MB,),
        in_specs=[pl.BlockSpec((1, 8, 2, CHUNK, F), lambda i: (i, 0, 0, 0, 0))],
        out_specs=pl.BlockSpec((1, 2 * F, 128), lambda i: (i, 0, 0)),
        out_shape=jax.ShapeDtypeStruct((MB, 2 * F, 128), jnp.float32),
        compiler_params=params(),
        name="spread_trajectory",
    )(arrived)


def grad_block(columns, w_in_ref, w_out_t_ref, scratch):
    before, back, hidden, change = scratch
    rows = w_in_ref.shape[0]
    parts = [
        (refs, slice(part * WIDE, (part + 1) * WIDE))
        for refs in columns
        for part in range(COLS // WIDE)
    ]

    def front(n):
        (_, x_t, _, misfit_t), at = parts[n]
        before[n % 2] = jnp.dot(w_in_ref[...], x_t[:, at], preferred_element_type=jnp.float32)
        back[n % 2] = jnp.dot(
            w_out_t_ref[...], misfit_t[:, at], preferred_element_type=jnp.float32
        )

    grad_in = jnp.zeros((rows, F), jnp.float32)
    grad_out = jnp.zeros((rows, F), jnp.float32)
    front(0)
    for n, ((x_ref, _, misfit, _), at) in enumerate(parts):
        if n + 1 < len(parts):
            front(n + 1)
        m = n % 2
        for r in range(0, rows, STRIP):
            strip = jnp.tanh(before[m, r : r + STRIP])
            hidden[m, r : r + STRIP] = strip.astype(jnp.bfloat16)
            strip = back[m, r : r + STRIP] * (1.0 - strip * strip)
            change[m, r : r + STRIP] = strip.astype(jnp.bfloat16)
        grad_out += jnp.dot(hidden[m], misfit[at], preferred_element_type=jnp.float32)
        grad_in += jnp.dot(change[m], x_ref[at], preferred_element_type=jnp.float32)
    shape = (rows // ROWS, ROWS, F)
    return grad_in.reshape(shape), grad_out.reshape(shape)


def columns_kernel(x_ref, tend_ref, target_ref, wet_ref, out_ref):
    for r in range(0, COLS, 64):
        at = slice(r, r + 64)
        gap = tend_ref[at] - target_ref[at].astype(jnp.float32)
        gap = wet_ref[r % OWN : r % OWN + 64] * gap * GRAD_SCALE
        out_ref[0, at] = x_ref[at]
        out_ref[1, at] = gap.astype(jnp.bfloat16)


def own_columns(inputs, tend, target, wet):
    return pl.pallas_call(
        columns_kernel,
        out_shape=jax.ShapeDtypeStruct((2, COLS, F), jnp.bfloat16),
        in_specs=[pl.BlockSpec(memory_space=pltpu.VMEM)] * 4,
        out_specs=pl.BlockSpec(memory_space=pltpu.VMEM),
        compiler_params=params(mib=24),
        name="own_columns",
    )(inputs, tend, target, wet)


def grad_kernel(half_ref, own_ref, their_ref, w_in_ref, w_out_ref, out_ref, turned, *scratch):
    both = (own_ref, their_ref)

    @pl.when(pl.program_id(0) == 0)
    def _():
        for n, ref in enumerate(both):
            for part in range(STEPS):
                at = slice(part * OWN, (part + 1) * OWN)
                turned[n, 0, :, at] = ref[0, at].T
                turned[n, 1, :, at] = ref[1, at].T

    columns = [
        (ref.at[0], turned.at[n, 0], ref.at[1], turned.at[n, 1]) for n, ref in enumerate(both)
    ]
    for n, grad in enumerate(grad_block(columns, w_in_ref, w_out_ref, scratch)):
        out_ref[:, n] = grad.astype(jnp.bfloat16)


def half_grads(half, own, theirs, w_in, w_out_t):
    blocks = HALF // HB2
    weight = pl.BlockSpec((HB2, F), lambda i, half: (half[0] * blocks + i, 0))
    whole = pl.BlockSpec((2, COLS, F), lambda i, half: (0, 0, 0))
    return pl.pallas_call(
        grad_kernel,
        grid_spec=pltpu.PrefetchScalarGridSpec(
            num_scalar_prefetch=1,
            grid=(blocks,),
            in_specs=[whole, whole, weight, weight],
            out_specs=pl.BlockSpec((HB2 // ROWS, 2, ROWS, F), lambda i, half: (i, 0, 0, 0)),
            scratch_shapes=[pltpu.VMEM((2, 2, F, COLS), jnp.bfloat16)]
            + [pltpu.VMEM((2, HB2, WIDE), jnp.float32)] * 2
            + [pltpu.VMEM((2, HB2, WIDE), jnp.bfloat16)] * 2,
        ),
        out_shape=jax.ShapeDtypeStruct((PARTS, 2, ROWS, F), jnp.bfloat16),
        compiler_params=params(("arbitrary",), 40),
        cost_estimate=pl.CostEstimate(
            flops=16 * COLS * F * HALF, bytes_accessed=5 * 2**20, transcendentals=2 * COLS * HALF
        ),
        name="half_grads",
    )(half, own, theirs, w_in, w_out_t)


def plane_kernel(in_ref, out_ref):
    total = in_ref[0].astype(jnp.float32)
    for n in range(1, PARTS):
        total += in_ref[n].astype(jnp.float32)
    out_ref[...] = total.astype(jnp.bfloat16)


def plane_sum(parts):
    vmem = pl.BlockSpec(memory_space=pltpu.VMEM)
    return pl.pallas_call(
        plane_kernel,
        out_shape=jax.ShapeDtypeStruct((2, ROWS, F), jnp.bfloat16),
        in_specs=[vmem],
        out_specs=vmem,
        compiler_params=params(mib=32),
        name="plane_sum",
    )(parts)


def column_kernel(own_ref, near_ref, far_ref, both_ref, out_ref):
    powers = []
    for g in range(2):
        own, near, far, both = (
            ref[g].astype(jnp.float32) for ref in (own_ref, near_ref, far_ref, both_ref)
        )
        total = (own + near) + (far + both)
        power = exponent(jnp.max(jnp.abs(total), axis=0, keepdims=True))
        powers.append(power)
        code = to_int16(encode(total, power))
        for n in range(PARTS):
            out_ref[n, g * ROWS : (g + 1) * ROWS] = code
    tail = to_int16(jnp.concatenate(powers + [jnp.zeros((14, F), jnp.float32)], axis=0))
    for n in range(PARTS):
        out_ref[n, 2 * ROWS : 2 * ROWS + 16] = tail


def column_copies(*planes):
    vmem = pl.BlockSpec(memory_space=pltpu.VMEM)
    return pl.pallas_call(
        column_kernel,
        out_shape=jax.ShapeDtypeStruct((PARTS, 2 * ROWS + 16, F), jnp.int16),
        in_specs=[vmem] * 4,
        out_specs=vmem,
        compiler_params=params(mib=32),
        name="column_copies",
    )(*planes)


def finish_kernel(half_ref, code_ref, *refs):
    grad_in_ref, grad_out_ref = refs[-2:]
    for n in range(0, code_ref.shape[0], 2):
        at = slice(n * ROWS, (n + 2) * ROWS)
        both = []
        for m in (n, n + 1):
            code = to_float(code_ref[m])
            grad_in_ref[m * ROWS : (m + 1) * ROWS] = decode(
                code[0:ROWS], code[2 * ROWS : 2 * ROWS + 1]
            )
            both.append(decode(code[ROWS : 2 * ROWS], code[2 * ROWS + 1 : 2 * ROWS + 2]))
        grad_out_ref[:, at] = jnp.concatenate(both, axis=0).T


def finish_half(half, code, before=()):
    return pl.pallas_call(
        finish_kernel,
        grid_spec=pltpu.PrefetchScalarGridSpec(
            num_scalar_prefetch=1,
            grid=(2,),
            in_specs=[pl.BlockSpec((PARTS // 2, 2 * ROWS + 16, F), lambda i, half: (i, 0, 0))]
            + [pl.BlockSpec(memory_space=pl.ANY)] * len(before),
            out_specs=[
                pl.BlockSpec((1024, F), lambda i, half: (half[0] * 2 + i, 0)),
                pl.BlockSpec((F, 1024), lambda i, half: (0, half[0] * 2 + i)),
            ],
        ),
        out_shape=[
            jax.ShapeDtypeStruct((H, F), jnp.float32),
            jax.ShapeDtypeStruct((F, H), jnp.float32),
        ],
        input_output_aliases={2: 0, 3: 1} if before else {},
        compiler_params=params(("arbitrary",), 32),
        name="finish_half",
    )(half, code, *before)


def swap(value, axes):
    return lax.all_to_all(value, axes, split_axis=0, concat_axis=0, tiled=True)


def local(initial_states, targets, w_in, w_out, diffusivity, stiffness, land_mask, wet_levels, plan):
    core = lax.axis_index("core").astype(jnp.int32).reshape(1)
    section = lax.axis_index("sec").astype(jnp.int32).reshape(1)
    chunk = (lax.axis_index(("cx", "core"))).astype(jnp.int32).reshape(1)

    states = initial_states.reshape(MB, 2 * F, 128)
    msg = swap(init_slabs(section, plan, states, land_mask, wet_levels), TILE)
    place = lambda half, chunk, col: (half * 8 + chunk) * 4 + col
    forward = [
        (place(h, j, c), place(h, (j + 1) % 8, c + (j + 1) // 8))
        for h in range(2)
        for j in range(8)
        for c in range(4)
        if c + (j + 1) // 8 < 4
    ]
    target, w_in_t, w_out_t = prepare(targets.reshape(MB, 2 * F, 128), w_in, w_out, plan)
    last, first, target = lax.optimization_barrier((msg[:, 32:48], msg[:, 0:16], target))
    left = lax.ppermute(last, TILE + COL, forward)
    right = lax.ppermute(first, TILE + COL, [(b, a) for a, b in forward])
    left, right, target = lax.optimization_barrier((left, right, target))
    target = swap(target.reshape(64, 2, CHUNK, F), ("sec",) + TILE).reshape(COLS, F)

    traj, inputs, tend, wet = rollout(chunk, msg, left, right, w_in_t, w_out_t, diffusivity, stiffness)
    arrived = swap(traj.reshape(64, 2, CHUNK, F), ("sec",) + TILE)

    own = own_columns(
        inputs.reshape(COLS, F), tend.reshape(COLS, F), target, wet.reshape(OWN, F)
    )
    theirs = lax.ppermute(own, "core", [(0, 1), (1, 0)])
    pair = half_grads(core, own, theirs, w_in, w_out_t)
    pair, arrived = lax.optimization_barrier((pair, arrived))

    trajectory = spread_trajectory(arrived.reshape(MB, 8, 2, CHUNK, F))
    plane = plane_sum(swap(pair, SPREAD))
    plane, trajectory = lax.optimization_barrier((plane, trajectory))
    others = [
        lax.ppermute(plane, ("zh", "c1"), [(i, i ^ n) for i in range(4)]) for n in range(1, 4)
    ]
    code = swap(column_copies(plane, *others), SPREAD)
    across = lax.ppermute(code, "core", [(0, 1), (1, 0)])
    grad_in, grad_out = finish_half(1 - core, across, finish_half(core, code))
    return (trajectory.reshape(1, MB, F, 2, 128), grad_in, grad_out)


def solution(mesh):
    fine = Mesh(mesh.devices.reshape(4, 2, 4, 2, 2, 2), ("sec", "zh", "cx", "core", "c1", "c0"))
    in_specs = (
        P(None, None, TILE, COL),
        P("sec", None, None, TILE, COL),
        P(),
        P(),
        P(),
        P(),
        P(TILE, COL),
        P(TILE, COL),
        P(),
    )
    out_specs = (P("sec", None, None, TILE, COL), P(), P())
    return jax.shard_map(local, mesh=fine, in_specs=in_specs, out_specs=out_specs, check_vma=False)
```

```python
import math

import jax
import jax.numpy as jnp
import numpy as np
from jax import lax
from jax.experimental import pallas as pl
from jax.experimental.pallas import tpu as pltpu
from jax.sharding import Mesh, PartitionSpec as P

V = 8
L = 16
H = 4096
F = 128
STEPS = 4
MB = 8
NX = 32
NY = 512
CHUNK = 16
HALO = STEPS
SLAB = CHUNK + 2 * HALO
MSG = 48
CODE = 32000.0
UNIT = 32768.0 / CODE
OWN = NX * CHUNK
COLS = STEPS * OWN
HB1 = 2048
HB2 = 2048
WIDE = 512
STRIP = 32
HALF = H // 2
GRAD_SCALE = 1.0 / math.sqrt(MB * STEPS * NX * NY)
TILE = ("zh", "cx", "core")
COL = ("c1", "c0")
SPREAD = ("sec", "cx", "c0")
PARTS = 32
ROWS = H // 2 // PARTS


def mode_block():
    order = np.arange(L)
    angles = np.pi * (order[None, :] + 0.5) * order[:, None] / L
    weights = np.where(order[:, None] == 0, math.sqrt(1.0 / L), math.sqrt(2.0 / L))
    return np.kron(np.eye(V), np.cos(angles) * weights)


def split_table(matrix):
    high = matrix.astype(jnp.bfloat16)
    low = (matrix - high.astype(np.float64)).astype(jnp.bfloat16)
    return np.concatenate([high, high, low], axis=0)


def params(semantics=None, mib=60):
    return pltpu.CompilerParams(dimension_semantics=semantics, vmem_limit_bytes=mib * 2**20)


def exponent(largest):
    return jnp.ceil(jnp.log(jnp.maximum(largest, 1e-30)) * (1.0 / math.log(2.0)) + 0.01)


def encode(value, power):
    scaled = value * (jnp.exp2(15.0 - power) * (1.0 / UNIT))
    return jnp.round(jnp.clip(scaled, -32767.0, 32767.0))


def to_int16(value):
    return value.astype(jnp.int32).astype(jnp.int16)


def to_float(code):
    return code.astype(jnp.int32).astype(jnp.float32)


def decode(value, power):
    return value * (jnp.exp2(power - 15.0) * UNIT)


def init_kernel(section_ref, plan_ref, state_ref, land_ref, levels_ref, msg_ref):
    power = exponent(jnp.max(jnp.abs(state_ref[0]), keepdims=True))
    code = [encode(state_ref[0, pl.ds(x, F, stride=2), :], power).T for x in range(2)]
    depth = jnp.where(land_ref[...] == 1, levels_ref[...], 0).astype(jnp.float32)
    extra = jnp.concatenate(
        [depth, jnp.broadcast_to(power, (1, 128)), jnp.zeros((5, 128), jnp.float32)], axis=0
    )
    for j in range(8):
        y = CHUNK * j
        first = [c[y : y + HALO] for c in code]
        middle = [c[y + HALO : y + CHUNK - HALO] for c in code]
        last = [c[y + CHUNK - HALO : y + CHUNK] for c in code]
        msg_ref[j] = to_int16(jnp.concatenate(first + [extra] + middle + last + [extra], axis=0))


def init_slabs(section, plan, states, land_mask, wet_levels):
    whole = lambda i, sec, plan: (0, 0)
    return pl.pallas_call(
        init_kernel,
        grid_spec=pltpu.PrefetchScalarGridSpec(
            num_scalar_prefetch=2,
            grid=(2,),
            in_specs=[
                pl.BlockSpec((1, 2 * F, 128), lambda i, sec, plan: (plan[2 * sec[0] + i], 0, 0)),
                pl.BlockSpec((2, 128), whole),
                pl.BlockSpec((2, 128), whole),
            ],
            out_specs=pl.BlockSpec((8, MSG, F), lambda i, sec, plan: (i, 0, 0)),
        ),
        out_shape=jax.ShapeDtypeStruct((16, MSG, F), jnp.int16),
        compiler_params=params(("arbitrary",)),
        name="init_slabs",
    )(section, plan, states, land_mask, wet_levels)


def levels():
    return (lax.broadcasted_iota(jnp.int32, (1, F), 1) % L).astype(jnp.float32)


def pack_halo(halo, step):
    if step == STEPS - 1:
        return jnp.zeros((0, F), jnp.float32)
    share = (1, 2, 4)[step]
    halo = halo.reshape(NX // share, share, 8, F)
    packed = halo[:, 0]
    row = lax.broadcasted_iota(jnp.int32, packed.shape, 1)
    for n in range(1, share):
        shift = n * 8 // share
        keep = STEPS - 1 - step
        place = (row + (8 - shift) + keep) % 8 < 2 * keep
        packed = jnp.where(place, pltpu.roll(halo[:, n], shift, 1), packed)
    return packed.reshape(NX // share * 8, F)


def unpack_halo(packed, step):
    share = (1, 2, 4)[step]
    packed = packed.reshape(NX // share, 8, F)
    parts = [packed] + [pltpu.roll(packed, 8 - n * 8 // share, 1) for n in range(1, share)]
    return jnp.stack(parts, axis=1).reshape(NX, 8, F)


def rollout_kernel(
    chunk_ref, msg_ref, left_ref, right_ref, w_in_t, w_out_t, mode_ref, mode_t, diff_ref, stiff_ref,
    traj_ref, inputs_ref, tend_ref, own_wet_ref,
    state, wet, modal, acc, x_scr, gain, pull, depth, depth_t, before, hidden, split,
):
    for t in range(16):
        for n, (ref, base) in enumerate(
            ((msg_ref, 0), (msg_ref, 16), (msg_ref, 32), (right_ref, 0), (left_ref, 0))
        ):
            piece = to_float(ref[t, base : base + 16])
            if n != 1:
                scale = decode(1.0, piece[10:11])
            rows = 8 if n == 1 else HALO
            at = (0, HALO, CHUNK - HALO, CHUNK, CHUNK + HALO)[n]
            for x in range(2):
                state[2 * t + x, at : at + rows] = piece[x * rows : (x + 1) * rows] * scale
            if n in (0, 3, 4):
                depth[n // 2 if n else 0, 2 * t : 2 * t + 2] = piece[8:10]
    for n in range(3):
        depth_t[n] = depth[n].T
    mine = chunk_ref[0]
    y_own = pl.multiple_of(mine * CHUNK, CHUNK)
    y_right = pl.multiple_of(lax.rem(mine + 1, 8) * CHUNK, CHUNK)
    y_left = pl.multiple_of(lax.rem(mine + 7, 8) * CHUNK + 8, 8)
    here = jnp.concatenate(
        [
            depth_t[0, pl.ds(y_own, CHUNK)],
            depth_t[1, pl.ds(y_right, 8)][:HALO],
            depth_t[2, pl.ds(y_left, 8)][8 - HALO :],
        ],
        axis=0,
    )
    level = levels()
    for x in range(NX):
        wet[x] = jnp.where(level < here[:, x : x + 1], 1.0, 0.0)
    own_wet_ref[...] = wet[:, :CHUNK]

    a = stiff_ref[...]
    u = 1.0 + a
    for i in range(NX):
        r = 1.0 / (a + u)
        gain[pl.ds(i, 1), :] = r
        pull[pl.ds(i, 1), :] = a * r
        u = 1.0 + a * (u * r)
    diff = diff_ref[...]

    def put_split(x, value):
        at = slice(x * SLAB, (x + 2) * SLAB)
        high = value.astype(jnp.bfloat16)
        split[at, 0:F] = high
        split[at, F : 2 * F] = (value - high.astype(jnp.float32)).astype(jnp.bfloat16)

    def transform(table):
        return jnp.dot(
            split[...], table[0 : 2 * F], preferred_element_type=jnp.float32
        ) + jnp.dot(split[:, 0:F], table[2 * F :], preferred_element_type=jnp.float32)

    for step in range(STEPS):
        for x in range(0, NX, 2):
            pieces = []
            for at in (x, x + 1):
                here = state[at]
                around = pltpu.roll(here, 1, 0) + pltpu.roll(here, SLAB - 1, 0) - 4.0 * here
                if at > 0:
                    around += state[at - 1]
                if at < NX - 1:
                    around += state[at + 1]
                pieces.append(wet[at] * (here + diff * around))
            put_split(x, jnp.concatenate(pieces, axis=0))
        modal[...] = transform(mode_t).reshape(NX, SLAB, F)
        part = modal[0] * gain[pl.ds(0, 1), :]
        modal[0] = part
        for i in range(1, NX):
            part = modal[i] * gain[pl.ds(i, 1), :] + pull[pl.ds(i, 1), :] * part
            modal[i] = part
        for i in range(NX - 2, -1, -1):
            behind = part
            part = modal[i] + pull[pl.ds(i, 1), :] * part
            if i % 2 == 0:
                put_split(i, jnp.concatenate([part, behind], axis=0))
        after = wet[...] * transform(mode_ref).reshape(NX, SLAB, F)
        inputs_ref[step] = after[:, :CHUNK].astype(jnp.bfloat16)
        extra = pack_halo(after[:, CHUNK:], step)
        count = OWN + extra.shape[0]
        state[...] = after
        x_scr[0:OWN] = after[:, :CHUNK].reshape(OWN, F).astype(jnp.bfloat16)
        if step < STEPS - 1:
            x_scr[OWN:count] = extra.astype(jnp.bfloat16)
        acc[0:count] = jnp.zeros((count, F), jnp.float32)

        def block(b, carry, n=count):
            def front(i):
                at = pl.multiple_of(b * HB1 + i * WIDE, WIDE)
                before[i % 2, 0:n] = jnp.dot(
                    x_scr[0:n], w_in_t[:, pl.ds(at, WIDE)], preferred_element_type=jnp.float32
                )
                return at

            at = front(0)
            for i in range(HB1 // WIDE):
                following = front(i + 1) if i + 1 < HB1 // WIDE else None
                for r in range(0, n, STRIP):
                    strip = jnp.tanh(before[i % 2, r : r + STRIP])
                    hidden[i % 2, r : r + STRIP] = strip.astype(jnp.bfloat16)
                acc[0:n] += jnp.dot(
                    hidden[i % 2, 0:n],
                    w_out_t[pl.ds(at, WIDE), :],
                    preferred_element_type=jnp.float32,
                )
                at = following
            return carry

        lax.fori_loop(0, H // HB1, block, 0)
        tendency = acc[0:OWN].reshape(NX, CHUNK, F)
        result = wet[:, :CHUNK] * (state[:, :CHUNK] + tendency)
        traj_ref[step] = result.astype(jnp.bfloat16)
        tend_ref[step] = tendency
        if step < STEPS - 1:
            beside = unpack_halo(acc[OWN:count], step)
            state[:, CHUNK:] = wet[:, CHUNK:] * (state[:, CHUNK:] + beside)
            state[:, :CHUNK] = result


def rollout(chunk, msg, left, right, w_in_t, w_out_t, diffusivity, stiffness):
    block = mode_block()
    vmem = pl.BlockSpec(memory_space=pltpu.VMEM)
    return pl.pallas_call(
        rollout_kernel,
        out_shape=[
            jax.ShapeDtypeStruct((STEPS, NX, CHUNK, F), jnp.bfloat16),
            jax.ShapeDtypeStruct((STEPS, NX, CHUNK, F), jnp.bfloat16),
            jax.ShapeDtypeStruct((STEPS, NX, CHUNK, F), jnp.float32),
            jax.ShapeDtypeStruct((NX, CHUNK, F), jnp.float32),
        ],
        in_specs=[pl.BlockSpec(memory_space=pltpu.SMEM)] + [vmem] * 9,
        out_specs=[vmem] * 4,
        scratch_shapes=[
            pltpu.VMEM((NX, SLAB, F), jnp.float32),
            pltpu.VMEM((NX, SLAB, F), jnp.float32),
            pltpu.VMEM((NX, SLAB, F), jnp.float32),
            pltpu.VMEM((NX * SLAB, F), jnp.float32),
            pltpu.VMEM((NX * SLAB, F), jnp.bfloat16),
            pltpu.VMEM((NX, F), jnp.float32),
            pltpu.VMEM((NX, F), jnp.float32),
            pltpu.VMEM((3, NX, 128), jnp.float32),
            pltpu.VMEM((3, 128, NX), jnp.float32),
            pltpu.VMEM((2, NX * SLAB, WIDE), jnp.float32),
            pltpu.VMEM((2, NX * SLAB, WIDE), jnp.bfloat16),
            pltpu.VMEM((NX * SLAB, 2 * F), jnp.bfloat16),
        ],
        compiler_params=params(),
        cost_estimate=pl.CostEstimate(
            flops=4 * 2816 * F * H, bytes_accessed=6 * 2**20, transcendentals=2816 * H
        ),
        name="rollout",
    )(
        chunk,
        msg,
        left,
        right,
        w_in_t,
        w_out_t,
        jnp.asarray(split_table(block)),
        jnp.asarray(split_table(block.T)),
        diffusivity.reshape(1, F),
        stiffness.reshape(1, F),
    )


def prepare_kernel(plan_ref, target_ref, w_in_ref, w_out_ref, out_ref, w_in_t, w_out_t, wide):
    wide[...] = target_ref[0].astype(jnp.float32)
    for x in range(2):
        t = wide[pl.ds(x, F, stride=2), :].T
        out_ref[0, :, x] = t.reshape(8, CHUNK, F).astype(jnp.bfloat16)
    w_in_t[...] = w_in_ref[...].T
    w_out_t[...] = w_out_ref[...].T


def prepare(targets, w_in, w_out, plan):
    part = H // MB
    down = lambda i, plan: (i, 0)
    along = lambda i, plan: (0, i)
    return pl.pallas_call(
        prepare_kernel,
        grid_spec=pltpu.PrefetchScalarGridSpec(
            num_scalar_prefetch=1,
            grid=(MB,),
            in_specs=[
                pl.BlockSpec((1, 2 * F, 128), lambda i, plan: (plan[i], 0, 0)),
                pl.BlockSpec((part, F), down),
                pl.BlockSpec((F, part), along),
            ],
            out_specs=[
                pl.BlockSpec((1, 8, 2, CHUNK, F), lambda i, plan: (i, 0, 0, 0, 0)),
                pl.BlockSpec((F, part), along),
                pl.BlockSpec((part, F), down),
            ],
            scratch_shapes=[pltpu.VMEM((2 * F, 128), jnp.float32)],
        ),
        out_shape=[
            jax.ShapeDtypeStruct((MB, 8, 2, CHUNK, F), jnp.bfloat16),
            jax.ShapeDtypeStruct((F, H), jnp.bfloat16),
            jax.ShapeDtypeStruct((H, F), jnp.bfloat16),
        ],
        compiler_params=params(),
        cost_estimate=pl.CostEstimate(flops=0, bytes_accessed=6 * 2**20, transcendentals=0),
        name="prepare",
    )(plan, targets, w_in, w_out)


def spread_kernel(in_ref, out_ref):
    for x in range(2):
        block = in_ref[0, :, x].astype(jnp.float32).reshape(128, F)
        out_ref[0, pl.ds(x, F, stride=2), :] = block.T


def spread_trajectory(arrived):
    return pl.pallas_call(
        spread_kernel,
        grid=(MB,),
        in_specs=[pl.BlockSpec((1, 8, 2, CHUNK, F), lambda i: (i, 0, 0, 0, 0))],
        out_specs=pl.BlockSpec((1, 2 * F, 128), lambda i: (i, 0, 0)),
        out_shape=jax.ShapeDtypeStruct((MB, 2 * F, 128), jnp.float32),
        compiler_params=params(),
        name="spread_trajectory",
    )(arrived)


def grad_block(columns, w_in_ref, w_out_t_ref, scratch):
    before, back, hidden, change = scratch
    rows = w_in_ref.shape[0]
    parts = [
        (refs, slice(part * WIDE, (part + 1) * WIDE))
        for refs in columns
        for part in range(COLS // WIDE)
    ]

    def front(n):
        (_, x_t, _, misfit_t), at = parts[n]
        before[n % 2] = jnp.dot(w_in_ref[...], x_t[:, at], preferred_element_type=jnp.float32)
        back[n % 2] = jnp.dot(
            w_out_t_ref[...], misfit_t[:, at], preferred_element_type=jnp.float32
        )

    grad_in = jnp.zeros((rows, F), jnp.float32)
    grad_out = jnp.zeros((rows, F), jnp.float32)
    front(0)
    for n, ((x_ref, _, misfit, _), at) in enumerate(parts):
        if n + 1 < len(parts):
            front(n + 1)
        m = n % 2
        for r in range(0, rows, STRIP):
            strip = jnp.tanh(before[m, r : r + STRIP])
            hidden[m, r : r + STRIP] = strip.astype(jnp.bfloat16)
            strip = back[m, r : r + STRIP] * (1.0 - strip * strip)
            change[m, r : r + STRIP] = strip.astype(jnp.bfloat16)
        grad_out += jnp.dot(hidden[m], misfit[at], preferred_element_type=jnp.float32)
        grad_in += jnp.dot(change[m], x_ref[at], preferred_element_type=jnp.float32)
    shape = (rows // ROWS, ROWS, F)
    return grad_in.reshape(shape), grad_out.reshape(shape)


def columns_kernel(x_ref, tend_ref, target_ref, wet_ref, out_ref):
    for r in range(0, COLS, 64):
        at = slice(r, r + 64)
        gap = tend_ref[at] - target_ref[at].astype(jnp.float32)
        gap = wet_ref[r % OWN : r % OWN + 64] * gap * GRAD_SCALE
        out_ref[0, at] = x_ref[at]
        out_ref[1, at] = gap.astype(jnp.bfloat16)


def own_columns(inputs, tend, target, wet):
    return pl.pallas_call(
        columns_kernel,
        out_shape=jax.ShapeDtypeStruct((2, COLS, F), jnp.bfloat16),
        in_specs=[pl.BlockSpec(memory_space=pltpu.VMEM)] * 4,
        out_specs=pl.BlockSpec(memory_space=pltpu.VMEM),
        compiler_params=params(),
        name="own_columns",
    )(inputs, tend, target, wet)


def grad_kernel(half_ref, own_ref, their_ref, w_in_ref, w_out_ref, out_ref, turned, *scratch):
    both = (own_ref, their_ref)

    @pl.when(pl.program_id(0) == 0)
    def _():
        for n, ref in enumerate(both):
            for part in range(STEPS):
                at = slice(part * OWN, (part + 1) * OWN)
                turned[n, 0, :, at] = ref[0, at].T
                turned[n, 1, :, at] = ref[1, at].T

    columns = [
        (ref.at[0], turned.at[n, 0], ref.at[1], turned.at[n, 1]) for n, ref in enumerate(both)
    ]
    for n, grad in enumerate(grad_block(columns, w_in_ref, w_out_ref, scratch)):
        out_ref[:, n] = grad.astype(jnp.bfloat16)


def half_grads(half, own, theirs, w_in, w_out_t):
    blocks = HALF // HB2
    weight = pl.BlockSpec((HB2, F), lambda i, half: (half[0] * blocks + i, 0))
    whole = pl.BlockSpec((2, COLS, F), lambda i, half: (0, 0, 0))
    return pl.pallas_call(
        grad_kernel,
        grid_spec=pltpu.PrefetchScalarGridSpec(
            num_scalar_prefetch=1,
            grid=(blocks,),
            in_specs=[whole, whole, weight, weight],
            out_specs=pl.BlockSpec((HB2 // ROWS, 2, ROWS, F), lambda i, half: (i, 0, 0, 0)),
            scratch_shapes=[pltpu.VMEM((2, 2, F, COLS), jnp.bfloat16)]
            + [pltpu.VMEM((2, HB2, WIDE), jnp.float32)] * 2
            + [pltpu.VMEM((2, HB2, WIDE), jnp.bfloat16)] * 2,
        ),
        out_shape=jax.ShapeDtypeStruct((PARTS, 2, ROWS, F), jnp.bfloat16),
        compiler_params=params(("arbitrary",)),
        cost_estimate=pl.CostEstimate(
            flops=16 * COLS * F * HALF, bytes_accessed=5 * 2**20, transcendentals=2 * COLS * HALF
        ),
        name="half_grads",
    )(half, own, theirs, w_in, w_out_t)


def plane_kernel(in_ref, out_ref):
    total = in_ref[0].astype(jnp.float32)
    for n in range(1, PARTS):
        total += in_ref[n].astype(jnp.float32)
    out_ref[...] = total.astype(jnp.bfloat16)


def plane_sum(parts):
    vmem = pl.BlockSpec(memory_space=pltpu.VMEM)
    return pl.pallas_call(
        plane_kernel,
        out_shape=jax.ShapeDtypeStruct((2, ROWS, F), jnp.bfloat16),
        in_specs=[vmem],
        out_specs=vmem,
        compiler_params=params(mib=32),
        name="plane_sum",
    )(parts)


def column_kernel(own_ref, near_ref, far_ref, both_ref, out_ref):
    powers = []
    for g in range(2):
        own, near, far, both = (
            ref[g].astype(jnp.float32) for ref in (own_ref, near_ref, far_ref, both_ref)
        )
        total = (own + near) + (far + both)
        power = exponent(jnp.max(jnp.abs(total), axis=0, keepdims=True))
        powers.append(power)
        code = to_int16(encode(total, power))
        for n in range(PARTS):
            out_ref[n, g * ROWS : (g + 1) * ROWS] = code
    tail = to_int16(jnp.concatenate(powers + [jnp.zeros((14, F), jnp.float32)], axis=0))
    for n in range(PARTS):
        out_ref[n, 2 * ROWS : 2 * ROWS + 16] = tail


def column_copies(*planes):
    vmem = pl.BlockSpec(memory_space=pltpu.VMEM)
    return pl.pallas_call(
        column_kernel,
        out_shape=jax.ShapeDtypeStruct((PARTS, 2 * ROWS + 16, F), jnp.int16),
        in_specs=[vmem] * 4,
        out_specs=vmem,
        compiler_params=params(mib=32),
        name="column_copies",
    )(*planes)


def finish_kernel(half_ref, code_ref, *refs):
    grad_in_ref, grad_out_ref = refs[-2:]
    for n in range(0, code_ref.shape[0], 2):
        at = slice(n * ROWS, (n + 2) * ROWS)
        both = []
        for m in (n, n + 1):
            code = to_float(code_ref[m])
            grad_in_ref[m * ROWS : (m + 1) * ROWS] = decode(
                code[0:ROWS], code[2 * ROWS : 2 * ROWS + 1]
            )
            both.append(decode(code[ROWS : 2 * ROWS], code[2 * ROWS + 1 : 2 * ROWS + 2]))
        grad_out_ref[:, at] = jnp.concatenate(both, axis=0).T


def finish_half(half, code, before=()):
    return pl.pallas_call(
        finish_kernel,
        grid_spec=pltpu.PrefetchScalarGridSpec(
            num_scalar_prefetch=1,
            grid=(2,),
            in_specs=[pl.BlockSpec((PARTS // 2, 2 * ROWS + 16, F), lambda i, half: (i, 0, 0))]
            + [pl.BlockSpec(memory_space=pl.ANY)] * len(before),
            out_specs=[
                pl.BlockSpec((1024, F), lambda i, half: (half[0] * 2 + i, 0)),
                pl.BlockSpec((F, 1024), lambda i, half: (0, half[0] * 2 + i)),
            ],
        ),
        out_shape=[
            jax.ShapeDtypeStruct((H, F), jnp.float32),
            jax.ShapeDtypeStruct((F, H), jnp.float32),
        ],
        input_output_aliases={2: 0, 3: 1} if before else {},
        compiler_params=params(("arbitrary",), 32),
        name="finish_half",
    )(half, code, *before)


def swap(value, axes):
    return lax.all_to_all(value, axes, split_axis=0, concat_axis=0, tiled=True)


def local(initial_states, targets, w_in, w_out, diffusivity, stiffness, land_mask, wet_levels, plan):
    core = lax.axis_index("core").astype(jnp.int32).reshape(1)
    section = lax.axis_index("sec").astype(jnp.int32).reshape(1)
    chunk = (lax.axis_index(("cx", "core"))).astype(jnp.int32).reshape(1)

    states = initial_states.reshape(MB, 2 * F, 128)
    msg = swap(init_slabs(section, plan, states, land_mask, wet_levels), TILE)
    place = lambda half, chunk, col: (half * 8 + chunk) * 4 + col
    forward = [
        (place(h, j, c), place(h, (j + 1) % 8, c + (j + 1) // 8))
        for h in range(2)
        for j in range(8)
        for c in range(4)
        if c + (j + 1) // 8 < 4
    ]
    target, w_in_t, w_out_t = prepare(targets.reshape(MB, 2 * F, 128), w_in, w_out, plan)
    last, first, target = lax.optimization_barrier((msg[:, 32:48], msg[:, 0:16], target))
    left = lax.ppermute(last, TILE + COL, forward)
    right = lax.ppermute(first, TILE + COL, [(b, a) for a, b in forward])
    left, right, target = lax.optimization_barrier((left, right, target))
    target = swap(target.reshape(64, 2, CHUNK, F), ("sec",) + TILE).reshape(COLS, F)

    traj, inputs, tend, wet = rollout(chunk, msg, left, right, w_in_t, w_out_t, diffusivity, stiffness)
    arrived = swap(traj.reshape(64, 2, CHUNK, F), ("sec",) + TILE)

    own = own_columns(
        inputs.reshape(COLS, F), tend.reshape(COLS, F), target, wet.reshape(OWN, F)
    )
    theirs = lax.ppermute(own, "core", [(0, 1), (1, 0)])
    pair = half_grads(core, own, theirs, w_in, w_out_t)
    pair, arrived = lax.optimization_barrier((pair, arrived))

    trajectory = spread_trajectory(arrived.reshape(MB, 8, 2, CHUNK, F))
    plane = plane_sum(swap(pair, SPREAD))
    plane, trajectory = lax.optimization_barrier((plane, trajectory))
    others = [
        lax.ppermute(plane, ("zh", "c1"), [(i, i ^ n) for i in range(4)]) for n in range(1, 4)
    ]
    code = swap(column_copies(plane, *others), SPREAD)
    across = lax.ppermute(code, "core", [(0, 1), (1, 0)])
    grad_in, grad_out = finish_half(1 - core, across, finish_half(core, code))
    return (trajectory.reshape(1, MB, F, 2, 128), grad_in, grad_out)


def solution(mesh):
    fine = Mesh(mesh.devices.reshape(4, 2, 4, 2, 2, 2), ("sec", "zh", "cx", "core", "c1", "c0"))
    in_specs = (
        P(None, None, TILE, COL),
        P("sec", None, None, TILE, COL),
        P(),
        P(),
        P(),
        P(),
        P(TILE, COL),
        P(TILE, COL),
        P(),
    )
    out_specs = (P("sec", None, None, TILE, COL), P(), P())
    return jax.shard_map(local, mesh=fine, in_specs=in_specs, out_specs=out_specs, check_vma=False)
```
